128 devices in a mesh: seq: 8 (over z, core), head: 16 (over y, x).
Axes of the slice: x: 4, y: 4, z: 4, core: 2. Of those that a mesh axis runs over, the one named last changes fastest.
Arguments:
- inputs: bfloat16 [2048, 2304], P('seq', 'head'), may hold values from -6 to 6
- output_grad: bfloat16 [2048, 2304], P('seq', 'head'), may hold values from -6 to 6
- w_query: bfloat16 [2304, 4096], P(None, 'head'), may hold values from -0.1875 to 0.1875
- w_key: bfloat16 [2304, 4096], P(None, 'head'), may hold values from -0.125 to 0.125
- w_value: bfloat16 [2304, 4096], P(None, 'head'), may hold values from -0.125 to 0.125
- w_output: bfloat16 [4096, 2304], P('head'), may hold values from -0.09375 to 0.09375
- gate_log: float32 [2048, 4096], P('seq', 'head'), may hold values from -3 to 0
- beta_gate: float32 [32, 2048], P('head', 'seq'), may hold values from 0.02 to 0.7
- initial_state: float32 [32, 128, 128], P('head'), may hold values from -4 to 4
- doc_starts: int32 [4], replicated, may hold values from 1920 to 2047, as said below
Outputs:
- input_grad: bfloat16 [2048, 2304], P('seq', 'head')
- gate_grad: float32 [2048, 4096], P('seq', 'head')
- beta_grad: float32 [32, 2048], P('head', 'seq')
- state_grad: float32 [32, 128, 128], P('head')
The draws below stay inside these ranges and needn't reach their ends.
Inputs may be any that keep to these rules, and one draw needn't show every extreme that they name: `doc_starts`: increasing and distinct; each is a position at which a new document begins; the smallest is 1920 and the largest is 2047; the tokens before the smallest continue a document that began before the window, whose state is initial_state.
All inputs are finite; a program needn't handle non-finite values.
Results may differ from the reference program's by a relative error of at most 0.02.
Values may be sent and summed in bfloat16 or wider, within the bound.
A program may use at most 64 MiB of HBM per device.

```python
import math
import jax
import jax.numpy as jnp
from jax import lax

D = 2304
H = 32
DK = 128
DV = 128
BLOCK = 64
DOCS = 4
TOK_DEV = 256
WINDOW_TOKENS = 2048


def draw_gate_log(key, part):
    key = jax.random.fold_in(key, 11)
    document_splits = jax.random.split(key, 7)
    channels = H * DK
    fast_share = 0.5
    rough_low = 0.7
    rough_high = 1.4
    fast = jax.random.uniform(document_splits[0], (channels,)) < fast_share
    fast_rate = jnp.exp(jax.random.uniform(document_splits[1], (channels,), minval=math.log(0.045), maxval=math.log(0.08)))
    slow_rate = jnp.exp(jax.random.uniform(document_splits[2], (channels,), minval=math.log(0.02), maxval=math.log(0.5))) / WINDOW_TOKENS
    baseline_rate = jnp.where(fast, fast_rate, slow_rate)
    shard_factor = jnp.exp(jax.random.uniform(document_splits[3], (WINDOW_TOKENS // TOK_DEV, channels), minval=-0.7, maxval=0.7))
    multiplier_rows = jnp.repeat(shard_factor, TOK_DEV, axis=0)
    jaggedness = jnp.exp(jax.random.uniform(document_splits[4], (WINDOW_TOKENS, channels), minval=math.log(rough_low), maxval=math.log(rough_high)))
    token_positions = jnp.arange(WINDOW_TOKENS, dtype=jnp.int32)
    spike_position = jax.random.randint(document_splits[5], (3,), 0, WINDOW_TOKENS)
    spike_penalty = jax.random.uniform(document_splits[6], (3,), minval=0.2, maxval=0.5)
    spike_events = jnp.sum(jnp.where(token_positions[:, None] == spike_position[None, :], jnp.log(1.0 - spike_penalty)[None, :], 0.0), axis=1)
    value_rows = -(baseline_rate[None, :] * multiplier_rows * jaggedness) + spike_events[:, None]
    return value_rows.astype(jnp.float32)


def draw_doc_starts(key, part):
    key = jax.random.fold_in(key, 23)
    first_start = WINDOW_TOKENS - TOK_DEV // 2
    inner = jax.random.permutation(key, WINDOW_TOKENS - first_start - 2)[:DOCS - 2] + first_start + 1
    ends = jnp.array([first_start, WINDOW_TOKENS - 1], dtype=jnp.int32)
    picked = jnp.concatenate([ends, inner.astype(jnp.int32)])
    return jnp.sort(picked).astype(jnp.int32)


def raised(values, stream_key, source, target, parts, factor):
    def block_of(dim):
        return (jnp.arange(values.shape[dim]) // (values.shape[dim] // parts)).reshape((-1,) + (1,) * (values.ndim - 1 - dim))

    one_side = jax.random.permutation(stream_key, parts)[block_of(target)]
    other_side = (block_of(target) + parts // 2) % parts
    return jnp.where((block_of(source) == one_side) | (block_of(source) == other_side), factor * values, values)


def shard_levels(own_key, shape, cuts, least, largest):
    gain, own = 1.0, jax.random.fold_in(own_key, 6)
    for position, parts in cuts:
        draws = jnp.exp(jax.random.uniform(jax.random.fold_in(own, position), (parts,), jnp.float32, least / len(cuts), largest / len(cuts)))
        gain = gain * jnp.repeat(draws, shape[position] // parts).reshape([-1 if axis == position else 1 for axis in range(len(shape))])
    return gain


def noise(rng, extent, scale, limit, cuts=(), held_as=jnp.bfloat16):
    entries = jax.random.normal(rng, extent, jnp.float32) * scale
    if len(cuts) > 0:
        entries = shard_levels(rng, extent, cuts, -0.22, 0.18) * entries
    return jnp.clip(entries, min=-limit, max=limit).astype(held_as)


def heavy_noise(rng, shape, width, most, shards, heavy, kind=jnp.bfloat16):
    values = width * jax.random.normal(rng, shape, jnp.float32)
    if shards:
        values = values * shard_levels(rng, shape, shards, -0.22, 0.18)
    return jnp.clip(raised(values, jax.random.fold_in(rng, 3), *heavy), -most, most).astype(kind)


def setup_inputs(seed: int = 0) -> dict:
    key_list = jax.random.split(jax.random.key(seed), 11)
    inputs = noise(key_list[0], (WINDOW_TOKENS, D), 1.0, 6.0, ((0, 8), (1, 16)))
    output_grad = noise(key_list[1], (WINDOW_TOKENS, D), 1.0, 6.0, ((0, 8), (1, 16)))
    w_query = heavy_noise(key_list[2], (D, H * DK), D ** -0.5, 0.1875, ((1, 16),), (1, 0, 16, 2.0))
    w_key = noise(key_list[3], (D, H * DK), D ** -0.5, 0.125, ((1, 16),))
    w_value = noise(key_list[4], (D, H * DV), D ** -0.5, 0.125, ((1, 16),))
    w_output = noise(key_list[5], (H * DV, D), (H * DV) ** -0.5, 0.09375, ((0, 16),))
    gate_log = draw_gate_log(jax.random.fold_in(key_list[10], 71), 0)
    beta_gate = jnp.clip(jnp.exp(math.log(0.7) - 3.5553481 * jax.random.uniform(key_list[7], (H, WINDOW_TOKENS), jnp.float32) ** shard_levels(key_list[7], (H, WINDOW_TOKENS), ((0, 16), (1, 8)), -0.2, 0.2)), 0.02, 0.7)
    initial_state = noise(key_list[8], (H, DK, DV), 0.5, 4.0, ((0, 16),), jnp.float32)
    doc_starts = draw_doc_starts(jax.random.fold_in(key_list[10], 71), 0)
    return {"inputs": inputs, "output_grad": output_grad, "w_query": w_query, "w_key": w_key, "w_value": w_value, "w_output": w_output, "gate_log": gate_log, "beta_gate": beta_gate, "initial_state": initial_state, "doc_starts": doc_starts}


EPSILON = 1e-06
MAXIMUM_PRECISE = lax.Precision.HIGHEST

def unit_rows(raw_rows):
    return raw_rows * lax.rsqrt(lax.optimization_barrier(jnp.sum(raw_rows * raw_rows, axis=-1, keepdims=True)) + EPSILON)

def head_major(matrix, head_count, length):
    tokens_here, columns = matrix.shape
    return matrix.reshape(tokens_here // length, length, head_count, columns // head_count).transpose(0, 2, 1, 3)

def token_major(tensor):
    blocks, head_count, length, columns = tensor.shape
    return tensor.transpose(0, 2, 1, 3).reshape(blocks * length, head_count * columns)

def block_terms(query_raw, keys_raw, value_rows, gate_logs, beta_rows, segment):
    length = query_raw.shape[2]
    queries = unit_rows(query_raw)
    keys_unit = unit_rows(keys_raw)
    cumulative = jnp.cumsum(gate_logs, axis=2)
    middle = cumulative[:, :, length // 2 - 1:length // 2, :]
    growth = jnp.exp(cumulative - middle)
    shrunk = keys_unit * jnp.exp(middle - cumulative)
    row_ids = lax.broadcasted_iota(jnp.int32, (length, length), 0)
    col_ids = lax.broadcasted_iota(jnp.int32, (length, length), 1)
    same_doc = segment[:, :, None] == segment[:, None, :]
    strict = jnp.logical_and(same_doc, row_ids > col_ids).astype(jnp.float32)[:, None]
    causal = jnp.logical_and(same_doc, row_ids >= col_ids).astype(jnp.float32)[:, None]
    key_key = jnp.einsum('nhic,nhjc->nhij', keys_unit * growth, shrunk, precision=MAXIMUM_PRECISE) * strict
    query_key_scores = jnp.einsum('nhic,nhjc->nhij', queries * growth, shrunk, precision=MAXIMUM_PRECISE) * causal
    system = jnp.eye(length, dtype=jnp.float32) + beta_rows[..., None] * key_key
    opening = (segment == 0).astype(jnp.float32)[:, None, :, None]
    entry_scale = jnp.exp(cumulative) * opening
    right_side = beta_rows[..., None] * jnp.concatenate([value_rows, keys_unit * entry_scale], axis=-1)
    solved = lax.linalg.triangular_solve(system, right_side, left_side=True, lower=True, unit_diagonal=True)
    value_width = value_rows.shape[-1]
    closing = (segment == segment[:, -1:]).astype(jnp.float32)[:, None, :, None]
    outgoing_state = keys_unit * jnp.exp(cumulative[:, :, -1:, :] - cumulative) * closing
    passed_through = jnp.exp(cumulative[:, :, -1, :]) * (segment[:, -1] == 0).astype(jnp.float32)[:, None, None]
    return (queries * entry_scale, query_key_scores, solved[..., :value_width], solved[..., value_width:], outgoing_state, passed_through)

def state_pass(block_parts, start_state, with_output):

    def advance(carried_state, block_item):
        incoming_state, query_key_scores, baseline_rows, coupled_terms, outgoing_state, passed_through = block_item
        blended_rows = baseline_rows - jnp.einsum('zpe,zei->zpi', coupled_terms, carried_state, precision=MAXIMUM_PRECISE)
        updated_state = passed_through[..., None] * carried_state + jnp.einsum('fgm,fgo->fmo', outgoing_state, blended_rows, precision=MAXIMUM_PRECISE)
        if with_output:
            state_readout = jnp.einsum('zpe,zei->zpi', incoming_state, carried_state, precision=MAXIMUM_PRECISE) + jnp.einsum('abe,aex->abx', query_key_scores, blended_rows, precision=MAXIMUM_PRECISE)
            return (updated_state, state_readout)
        return (updated_state, None)
    return lax.scan(advance, start_state, block_parts)

def reference(inputs, output_grad, w_query, w_key, w_value, w_output, gate_log, beta_gate, initial_state, doc_starts):
    query_raw = jnp.dot(inputs.astype(jnp.float32), w_query.astype(jnp.float32), preferred_element_type=jnp.float32)
    keys_raw = jnp.dot(inputs.astype(jnp.float32), w_key.astype(jnp.float32), preferred_element_type=jnp.float32)
    value_raw = jnp.dot(inputs.astype(jnp.float32), w_value.astype(jnp.float32), preferred_element_type=jnp.float32)
    attn_grad = jnp.dot(output_grad.astype(jnp.float32), w_output.T.astype(jnp.float32), preferred_element_type=jnp.float32)
    token_positions = jnp.arange(WINDOW_TOKENS, dtype=jnp.int32)
    starting = jnp.any(token_positions[:, None] == doc_starts[None, :], axis=1).astype(jnp.int32)
    segment = jnp.cumsum(starting.reshape(WINDOW_TOKENS // BLOCK, BLOCK), axis=1, dtype=jnp.int32)

    def forward(query_in, keys_in, value_in, gate_in, beta_in, state_in):
        head_count = state_in.shape[0]
        block_parts = block_terms(head_major(query_in, head_count, BLOCK), head_major(keys_in, head_count, BLOCK), head_major(value_in, head_count, BLOCK), head_major(gate_in, head_count, BLOCK), beta_in.reshape(head_count, WINDOW_TOKENS // BLOCK, BLOCK).transpose(1, 0, 2), segment)
        last_state, state_readout = state_pass(block_parts, state_in, True)
        return token_major(state_readout)
    attention_out, pullback = jax.vjp(forward, query_raw, keys_raw, value_raw, gate_log, beta_gate, initial_state)
    gradients = pullback(attn_grad)
    input_grad = jnp.dot(gradients[0].astype(jnp.bfloat16).astype(jnp.float32), w_query.T.astype(jnp.float32), preferred_element_type=jnp.float32)
    input_grad = input_grad + jnp.dot(gradients[1].astype(jnp.bfloat16).astype(jnp.float32), w_key.T.astype(jnp.float32), preferred_element_type=jnp.float32)
    input_grad = input_grad + jnp.dot(gradients[2].astype(jnp.bfloat16).astype(jnp.float32), w_value.T.astype(jnp.float32), preferred_element_type=jnp.float32)
    return (input_grad.astype(jnp.bfloat16), gradients[3], gradients[4], gradients[5])
```

```python
import jax
import jax.numpy as jnp
from jax import lax
from jax.experimental import pallas as pl
from jax.experimental.pallas import tpu as pltpu
from jax.sharding import PartitionSpec as P

F32, BF = jnp.float32, jnp.bfloat16
MESH = pl.DeviceIdType.MESH
CHUNK = 64
CHUNKS = 4
EPSILON = 1e-06


def mm(a, b, ca=1, cb=0):
    return lax.dot_general(
        a.astype(BF), b.astype(BF), (((ca,), (cb,)), ((), ())), preferred_element_type=F32
    )


def cat(parts, axis=0):
    return jnp.concatenate(parts, axis=axis)


def split(x):
    hi = x.astype(BF)
    return hi, (x - hi.astype(F32)).astype(BF)


def rowsum(x):
    return jnp.sum(x, axis=1, keepdims=True)


def per_head(rows):
    return cat([jnp.broadcast_to(r, (CHUNK, 128)) for r in rows])


def iotas():
    i = lax.broadcasted_iota(jnp.int32, (128, 128), 0)
    j = lax.broadcasted_iota(jnp.int32, (128, 128), 1)
    return i, j


HEADS = (slice(0, CHUNK), slice(CHUNK, 2 * CHUNK))


def invert(n, i, j):
    eye = (i == j).astype(F32)
    d = jnp.where((i >> 4) == (j >> 4), n, 0.0)
    d2 = mm(d, d)
    p = mm(eye - d, eye + d2)
    d4 = mm(d2, d2)
    p = mm(p, eye + d4)
    d8 = mm(d4, d4)
    t = mm(p, eye + d8)
    for s in (4, 5):
        off = jnp.where(((i >> (s + 1)) == (j >> (s + 1))) & ((i >> s) != (j >> s)), n, 0.0)
        t = t - mm(t, mm(off, t))
    return t


(QN, KN, RQ, RK, EO, EG, ES, EX, U_, Y0, BETA) = range(11)
(QG, KG, KS, W_, TK, KO, DO, CAUSAL, STRICT) = range(9)


def segments(ds_ref, t0):
    row = t0 + (lax.broadcasted_iota(jnp.int32, (128, 1), 0) & (CHUNK - 1))
    col = t0 + (lax.broadcasted_iota(jnp.int32, (1, 128), 1) & (CHUNK - 1))
    segr, segc = jnp.zeros_like(row), jnp.zeros_like(col)
    for k in range(4):
        start = ds_ref[k]
        here = (start >= t0).astype(jnp.int32)
        segr = segr + (row >= start).astype(jnp.int32) * here
        segc = segc + (col >= start).astype(jnp.int32) * here
    return segr, segc


def first_pass(c, t0, q, k, v, g, beta, dO, ds_ref, sf, sb, chain, passed):
    i, j = iotas()
    segr, segc = segments(ds_ref, t0)
    same = ((i >> 6) == (j >> 6)) & (segr == segc)
    strict, causal = same & (i > j), same & (i >= j)
    tri = (((i >> 6) == (j >> 6)) & (i >= j)).astype(BF)
    rq = lax.rsqrt(rowsum(q * q) + EPSILON)
    rk = lax.rsqrt(rowsum(k * k) + EPSILON)
    qn, kn = q * rq, k * rk
    hi, lo = split(g)
    G = mm(cat([tri, tri], 1), cat([hi, lo]))
    mid = per_head([G[31:32], G[95:96]])
    last = per_head([G[63:64], G[127:128]])
    opening = (segr == 0).astype(F32)
    final = [segr[63:64], segr[127:128]]
    closing = (segr == cat([jnp.broadcast_to(f, (CHUNK, 1)) for f in final])).astype(F32)
    eg, es = jnp.exp(G - mid), jnp.exp(mid - G)
    eo = jnp.exp(G) * opening
    ex = jnp.exp(last - G) * closing
    kg, qg, ks = (kn * eg).astype(BF), (qn * eg).astype(BF), (kn * es).astype(BF)
    kout = kn * ex
    ap = mm(cat([kg, qg]), ks, 1, 1)
    a = jnp.where(strict, ap[:128], 0.0)
    p = jnp.where(causal, ap[128:], 0.0)
    t = invert(beta * a, i, j)
    uw = mm(t, cat([beta * v, beta * (kn * eo)], 1))
    u, w = uw[:, :128], uw[:, 128:]
    qt = qn * eo - mm(p, w)
    pdo = mm(p, dO, 0, 0)
    yt = mm(t, cat([pdo, kout], 1), 0, 0)
    for h, s in enumerate(HEADS):
        end = CHUNK * h + CHUNK - 1
        keep = jnp.exp(G[end : end + 1]) * (final[h] == 0).astype(F32)
        passed[c, h : h + 1, :] = keep
        kw = mm(kout[s], uw[s], 0, 0)
        chain[c, h, 0] = jnp.where(i == j, keep, 0.0) - kw[:, 128:]
        chain[c, h, 1] = kw[:, :128]
        chain[c, h, 2] = mm(qt[s], dO[s], 0, 0)
    wide = lambda z: jnp.broadcast_to(z, (128, 128))
    for slot, value in (
        (QN, qn), (KN, kn), (RQ, wide(rq)), (RK, wide(rk)), (EO, eo), (EG, eg), (ES, es),
        (EX, ex), (U_, u), (Y0, yt[:, :128]), (BETA, wide(beta)),
    ):
        sf[c, slot] = value
    for slot, value in (
        (QG, qg), (KG, kg), (KS, ks), (W_, w), (TK, yt[:, 128:]), (KO, kout), (DO, dO),
        (CAUSAL, causal.astype(F32)), (STRICT, strict.astype(F32)),
    ):
        sb[c, slot] = value.astype(BF)


def second_pass(c, S, D, sf, sb, passed):
    f = lambda slot: sf[c, slot]
    b = lambda slot: sb[c, slot]
    i, j = iotas()
    S, D = [s.astype(BF) for s in S], [d.astype(BF) for d in D]
    w, tk, dO, beta = b(W_), b(TK), b(DO), f(BETA)
    x = f(U_) - cat([mm(w[s], S[h]) for h, s in enumerate(HEADS)])
    y = f(Y0) + cat([mm(tk[s], D[h]) for h, s in enumerate(HEADS)])
    dbeta = rowsum(y * x) / beta[:, :1]
    dv = beta * y
    xb, yb = x.astype(BF), y.astype(BF)
    pa = mm(cat([dO, yb]), xb, 1, 1)
    dp = jnp.where(b(CAUSAL).astype(F32) > 0, pa[:128], 0.0)
    da = jnp.where(b(STRICT).astype(F32) > 0, -beta * pa[128:], 0.0)
    ys = [mm(cat([dO[s], yb[s]]), S[h], 1, 1) for h, s in enumerate(HEADS)]
    eo = f(EO)
    qs = cat([ys[0][:CHUNK], ys[1][:CHUNK]]) * eo
    ke = cat([ys[0][CHUNK:], ys[1][CHUNK:]]) * (-beta * eo)
    dko = cat([mm(xb[s], D[h], 1, 1) for h, s in enumerate(HEADS)])
    pab = cat([dp, da]).astype(BF)
    qg, kg, ks = b(QG), b(KG), b(KS)
    dqk = mm(pab, ks)
    dqg, dkg = dqk[:128], dqk[128:]
    dks = mm(pab, cat([qg, kg]), 0, 0)
    qn, kn, eg = f(QN), f(KN), f(EG)
    dq = qs + dqg * eg
    dk = ke + dkg * eg + dks * f(ES) + dko * f(EX)
    kd = b(KO).astype(F32) * dko
    dG = (
        qn * qs + qg.astype(F32) * dqg + kg.astype(F32) * dkg
        - ks.astype(F32) * dks + kn * ke - kd
    )
    ends = []
    for h, s in enumerate(HEADS):
        hi, lo = split(S[h].astype(F32) * D[h].astype(F32))
        through = mm(jnp.ones((8, 256), BF), cat([hi, lo], 1), 1, 1)[0:1]
        ends.append(jnp.sum(kd[s], axis=0, keepdims=True) + passed[c, h : h + 1, :] * through)
    hi, lo = split(dG)
    upper = (((i >> 6) == (j >> 6)) & (i <= j)).astype(BF)
    dg = mm(cat([upper, upper], 1), cat([hi, lo])) + per_head(ends)
    dqr = f(RQ) * (dq - qn * rowsum(qn * dq))
    dkr = f(RK) * (dk - kn * rowsum(kn * dk))
    return dqr, dkr, dv, dg, dbeta


def flipped(x):
    x = x.astype(F32)
    tail = cat([x[:, 128:], jnp.zeros((256, 112), F32)], 1)
    return cat([x[:, :128].T, tail.T[:16]]).astype(BF)


def kernel(
    x_ref, og_ref, wq_ref, wk_ref, wv_ref, wo_ref, gate_ref, beta_ref, init_ref, ds_ref,
    ig_ref, gg_ref, bg_ref, sg_ref,
    wcat, wo, wot, xg, raw, gcat, sf, sb, chain, passed, prefix, suffix,
    own, heard, comm, bounds, part, r1, t2, t2f, r2,
    wsem, gsend, grecv, esend, erecv, rsend, rrecv,
):
    seq, head = lax.axis_index("seq"), lax.axis_index("head")
    y, x = head // 4, head % 4
    z, core = seq // 2, seq % 2
    xs = [{"head": y * 4 + (x + o) % 4} for o in (1, 2, 3)]
    ys = [{"head": ((y + o) % 4) * 4 + x} for o in (1, 2, 3)]
    zs = [{"seq": ((z + o) % 4) * 2 + core} for o in (1, 2, 3)]
    sibling = {"seq": z * 2 + (1 - core)}

    loads = [
        pltpu.make_async_copy(ref, wcat.at[:, 256 * n : 256 * n + 256], wsem.at[n])
        for n, ref in enumerate((wq_ref, wk_ref, wv_ref))
    ]
    loads.append(pltpu.make_async_copy(wo_ref, wo, wsem.at[3]))
    for load in loads:
        load.start()

    barrier = pltpu.get_barrier_semaphore()
    partners = xs + ys + zs + [sibling]
    for device in partners:
        pl.semaphore_signal(barrier, inc=1, device_id=device, device_id_type=MESH)

    for item, ref in enumerate((x_ref, og_ref)):
        turned = flipped(ref[...])
        xg[item, 0, y, x] = turned[:, :128]
        xg[item, 1, y, x] = turned[:, 128:]
    pl.semaphore_wait(barrier, len(partners))

    def remote(src, dst, ssem, rsem, device):
        return pltpu.make_async_remote_copy(
            src_ref=src, dst_ref=dst, send_sem=ssem, recv_sem=rsem,
            device_id=device, device_id_type=MESH,
        )

    def gather(item, half, phase):
        axis = xs if (half + phase) % 2 == 0 else ys
        if phase == 0:
            block = xg.at[item, half, y, x]
        else:
            block = xg.at[item, 0, y] if half == 0 else xg.at[item, 1, :, x]
        return [
            remote(block, block, gsend.at[item, half, phase, o], grecv.at[item, half, phase, o],
                   axis[o])
            for o in (1, 0, 2)
        ]

    near = [[gather(item, half, 0) for half in (0, 1)] for item in (0, 1)]
    far = [[gather(item, half, 1) for half in (0, 1)] for item in (0, 1)]
    for item in (0, 1):
        for o in range(3):
            for half in (0, 1):
                near[item][half][o].start()
    for item in (0, 1):
        for half in (0, 1):
            for copy in near[item][half]:
                copy.wait_recv()
            for copy in far[item][half]:
                copy.start()

    loads[3].wait()
    for n in range(18):
        wot[128 * n : 128 * n + 128, :] = wo[:, 128 * n : 128 * n + 128].T
    for load in loads[:3]:
        load.wait()

    def project(item, weight, columns):
        for half in (0, 1):
            for copy in far[item][half]:
                copy.wait_recv()
            rows = xg[item, half].reshape(2304, 128)
            raw[128 * half : 128 * half + 128, columns] = mm(rows, weight[...], 0, 0)

    project(0, wcat, slice(0, 768))
    project(1, wot, slice(768, 1024))

    def stacked(ref, c, first):
        t = slice(CHUNK * c, CHUNK * c + CHUNK)
        return cat([ref[t, first : first + 128], ref[t, first + 128 : first + 256]])

    diagonal = (
        lax.broadcasted_iota(jnp.int32, (CHUNK, CHUNK), 0)
        == lax.broadcasted_iota(jnp.int32, (CHUNK, CHUNK), 1)
    )
    for c in range(CHUNKS):
        t = slice(CHUNK * c, CHUNK * c + CHUNK)
        beta = cat([rowsum(jnp.where(diagonal, beta_ref[h : h + 1, t], 0.0)) for h in (0, 1)])
        first_pass(
            c, seq * 256 + CHUNK * c,
            stacked(raw, c, 0), stacked(raw, c, 256), stacked(raw, c, 512),
            stacked(gate_ref, c, 0), beta, stacked(raw, c, 768),
            ds_ref, sf, sb, chain, passed,
        )

    for h in (0, 1):
        m, v = chain[0, h, 0], chain[0, h, 1]
        prefix[h, 0, :, :128], prefix[h, 0, :, 128:] = m, v
        for n in (1, 2, 3):
            step = mm(chain[n, h, 0], cat([m, v], 1))
            m, v = step[:, :128], step[:, 128:] + chain[n, h, 1]
            if n < 3:
                prefix[h, n, :, :128], prefix[h, n, :, 128:] = m, v
        l = chain[3, h, 2]
        suffix[h, 2, :, 128:] = l
        for n in (2, 1, 0):
            l = mm(chain[n, h, 0], l, 0, 0) + chain[n, h, 2]
            if n > 0:
                suffix[h, n - 1, :, 128:] = l
        own[h, 0], own[h, 1], own[h, 2] = m.astype(BF), v.astype(BF), l.astype(BF)

    swap = remote(own.at[1 - core], heard, esend.at[0], erecv.at[0], sibling)
    swap.start()
    for h in (0, 1):
        m = chain[3, h, 0].T
        suffix[h, 2, :, :128] = m
        for n in (2, 1):
            m = mm(chain[n, h, 0], m, 0, 0)
            suffix[h, n - 1, :, :128] = m
    swap.wait_recv()

    first = core == 0
    mine = [own[core, n] for n in range(3)]
    other = [heard[n] for n in range(3)]
    m0, b0, l0 = [jnp.where(first, a, b) for a, b in zip(mine, other)]
    m1, b1, l1 = [jnp.where(first, b, a) for a, b in zip(mine, other)]
    both = mm(m1, cat([m0, b0], 1))
    comm[z, 0] = both[:, :128].astype(BF)
    comm[z, 1] = (both[:, 128:] + b1.astype(F32)).astype(BF)
    comm[z, 2] = (l0.astype(F32) + mm(m0, l1, 0, 0)).astype(BF)
    spread = [
        remote(comm.at[z], comm.at[z], esend.at[1 + o], erecv.at[1 + o], zs[o]) for o in (1, 0, 2)
    ]
    for copy in spread:
        copy.start()
    for copy in spread:
        copy.wait_recv()
    state, entering = init_ref[core], init_ref[core]
    for n in range(3):
        state = mm(comm[n, 0], state) + comm[n, 1].astype(F32)
        entering = jnp.where(z == n + 1, state, entering)
    grad = comm[3, 2].astype(F32)
    leaving = jnp.where(z == 2, grad, 0.0)
    for n in (2, 1, 0):
        grad = mm(comm[n, 0], grad, 0, 0) + comm[n, 2].astype(F32)
        leaving = jnp.where(z == n - 1, grad, leaving)
    after = mm(m0, entering) + b0.astype(F32)
    before = mm(m1, leaving, 0, 0) + l1.astype(F32)
    my_state, sib_state = jnp.where(first, entering, after), jnp.where(first, after, entering)
    my_grad, sib_grad = jnp.where(first, before, leaving), jnp.where(first, leaving, before)
    for n, value in enumerate((sib_state, sib_grad, grad)):
        heard2 = bounds
        heard2[2 + core, n] = value.astype(BF)
    give = remote(bounds.at[2 + core], bounds.at[core], esend.at[4], erecv.at[4], sibling)
    give.start()
    bounds[core, 0], bounds[core, 1] = my_state.astype(BF), my_grad.astype(BF)
    bounds[core, 2] = grad.astype(BF)
    give.wait_recv()

    for h in (0, 1):
        sg_ref[h] = bounds[h, 2].astype(F32)
    S, D = [], []
    for h in (0, 1):
        s, d = bounds[h, 0], bounds[h, 1]
        S.append([s] + [mm(prefix[h, n, :, :128], s) + prefix[h, n, :, 128:] for n in range(3)])
        D.append([mm(suffix[h, n, :, :128], d) + suffix[h, n, :, 128:] for n in range(3)] + [d])
    for c in range(CHUNKS):
        t = slice(CHUNK * c, CHUNK * c + CHUNK)
        dq, dk, dv, dg, dbeta = second_pass(
            c, [S[0][c], S[1][c]], [D[0][c], D[1][c]], sf, sb, passed
        )
        for h, s in enumerate(HEADS):
            for n, value in enumerate((dq, dk, dv)):
                gcat[t, 256 * n + 128 * h : 256 * n + 128 * h + 128] = value[s].astype(BF)
            gg_ref[t, 128 * h : 128 * h + 128] = dg[s]
            bg_ref[h : h + 1, t] = jnp.sum(
                jnp.where(diagonal, dbeta[s], 0.0), axis=0, keepdims=True
            )

    def share(half, target):
        rows = gcat[128 * half : 128 * half + 128, :]
        if half == 0:
            return mm(wcat[pl.ds(pl.multiple_of(576 * target, 16), 576), :], rows, 1, 1)
        return cat([
            mm(wcat[pl.ds(pl.multiple_of(576 * n + 144 * target, 16), 144), :], rows, 1, 1)
            for n in range(4)
        ])

    sums = [[], []]
    for o in (1, 0, 2):
        for half, place, axis in ((0, y, ys), (1, x, xs)):
            part[half, o] = share(half, (place + o + 1) % 4).astype(BF)
            copy = remote(
                part.at[half, o], r1.at[half, o], rsend.at[half, 0, o], rrecv.at[half, 0, o],
                axis[o],
            )
            copy.start()
            sums[half].append(copy)
    ends = [[], []]
    totals = [share(0, y), share(1, x)]
    for half, place, axis in ((0, x, xs), (1, y, ys)):
        total = totals[half]
        for copy in sums[half]:
            copy.wait_recv()
        for o in range(3):
            total = total + r1[half, o].astype(F32)
        t2f[half] = total.reshape(4, 144, 128)
        t2[half] = total.astype(BF).reshape(4, 144, 128)
        for o in (1, 0, 2):
            copy = remote(
                t2.at[half, (place + o + 1) % 4], r2.at[half, o],
                rsend.at[half, 1, o], rrecv.at[half, 1, o], axis[o],
            )
            copy.start()
            ends[half].append(copy)
    done = []
    for half, place in ((0, x), (1, y)):
        total = t2f[half, place]
        for copy in ends[half]:
            copy.wait_recv()
        for o in range(3):
            total = total + r2[half, o].astype(F32)
        done.append(total)
    total = cat(done, 1)
    ig_ref[:, :128] = total[:128].T.astype(BF)
    tail = cat([total[128:], jnp.zeros((112, 256), F32)]).T
    ig_ref[:, 128:] = tail[:, :16].astype(BF)

    for group in near + far:
        for copies in group:
            for copy in copies:
                copy.wait_send()
    for copy in [swap, give] + spread + sums[0] + sums[1] + ends[0] + ends[1]:
        copy.wait_send()


def per_device(*arrays):
    vmem = pl.BlockSpec(memory_space=pltpu.VMEM)
    anywhere = pl.BlockSpec(memory_space=pl.ANY)
    scratch = lambda *shape, dtype=F32: pltpu.VMEM(shape, dtype)
    dma = lambda *shape: pltpu.SemaphoreType.DMA(shape)
    return pl.pallas_call(
        kernel,
        out_shape=(
            jax.ShapeDtypeStruct((256, 144), BF),
            jax.ShapeDtypeStruct((256, 256), F32),
            jax.ShapeDtypeStruct((2, 256), F32),
            jax.ShapeDtypeStruct((2, 128, 128), F32),
        ),
        in_specs=[vmem, vmem] + [anywhere] * 4 + [vmem] * 3
        + [pl.BlockSpec(memory_space=pltpu.SMEM)],
        out_specs=(vmem,) * 4,
        scratch_shapes=[
            scratch(2304, 768, dtype=BF),
            scratch(256, 2304, dtype=BF),
            scratch(2304, 256, dtype=BF),
            scratch(2, 2, 4, 4, 144, 128, dtype=BF),
            scratch(256, 1024),
            scratch(256, 768, dtype=BF),
            scratch(CHUNKS, 11, 128, 128),
            scratch(CHUNKS, 9, 128, 128, dtype=BF),
            scratch(CHUNKS, 2, 3, 128, 128),
            scratch(CHUNKS, 8, 128),
            scratch(2, 3, 128, 256),
            scratch(2, 3, 128, 256),
            scratch(2, 3, 128, 128, dtype=BF),
            scratch(3, 128, 128, dtype=BF),
            scratch(4, 3, 128, 128, dtype=BF),
            scratch(4, 3, 128, 128, dtype=BF),
            scratch(2, 3, 576, 128, dtype=BF),
            scratch(2, 3, 576, 128, dtype=BF),
            scratch(2, 4, 144, 128, dtype=BF),
            scratch(2, 4, 144, 128),
            scratch(2, 3, 144, 128, dtype=BF),
            dma(4), dma(2, 2, 2, 3), dma(2, 2, 2, 3), dma(5), dma(5), dma(2, 2, 3), dma(2, 2, 3),
        ],
        compiler_params=pltpu.CompilerParams(
            collective_id=0, has_side_effects=True, vmem_limit_bytes=48 * 1024 * 1024
        ),
        cost_estimate=pl.CostEstimate(
            flops=3 * 10**9, bytes_accessed=6 * 10**6, transcendentals=3 * 10**5
        ),
    )(*arrays)


def solution(mesh):
    return jax.shard_map(
        per_device,
        mesh=mesh,
        in_specs=(
            P("seq", "head"),
            P("seq", "head"),
            P(None, "head"),
            P(None, "head"),
            P(None, "head"),
            P("head", None),
            P("seq", "head"),
            P("head", "seq"),
            P("head", None, None),
            P(),
        ),
        out_specs=(P("seq", "head"), P("seq", "head"), P("head", "seq"), P("head", None, None)),
        check_vma=False,
    )
```

```python
import jax
import jax.numpy as jnp
from jax import lax
from jax.experimental import pallas as pl
from jax.experimental.pallas import tpu as pltpu
from jax.sharding import PartitionSpec as P

F32, BF = jnp.float32, jnp.bfloat16
MESH = pl.DeviceIdType.MESH
CHUNK = 64
CHUNKS = 4
EPSILON = 1e-06


def mm(a, b, ca=1, cb=0):
    return lax.dot_general(
        a.astype(BF), b.astype(BF), (((ca,), (cb,)), ((), ())), preferred_element_type=F32
    )


def cat(parts, axis=0):
    return jnp.concatenate(parts, axis=axis)


def split(x):
    hi = x.astype(BF)
    return hi, (x - hi.astype(F32)).astype(BF)


def rowsum(x):
    return jnp.sum(x, axis=1, keepdims=True)


def per_head(rows):
    return cat([jnp.broadcast_to(r, (CHUNK, 128)) for r in rows])


def iotas():
    i = lax.broadcasted_iota(jnp.int32, (128, 128), 0)
    j = lax.broadcasted_iota(jnp.int32, (128, 128), 1)
    return i, j


HEADS = (slice(0, CHUNK), slice(CHUNK, 2 * CHUNK))


def invert(n, i, j):
    eye = (i == j).astype(F32)
    d = jnp.where((i >> 4) == (j >> 4), n, 0.0)
    d2 = mm(d, d)
    p = mm(eye - d, eye + d2)
    d4 = mm(d2, d2)
    p = mm(p, eye + d4)
    d8 = mm(d4, d4)
    t = mm(p, eye + d8)
    for s in (4, 5):
        off = jnp.where(((i >> (s + 1)) == (j >> (s + 1))) & ((i >> s) != (j >> s)), n, 0.0)
        t = t - mm(t, mm(off, t))
    return t


(QN, KN, RQ, RK, EO, EG, ES, EX, U_, BETA) = range(10)
(QG, KG, KS, W_, TK, KO, PT, CAUSAL, STRICT) = range(9)


def segments(ds_ref, t0):
    row = t0 + (lax.broadcasted_iota(jnp.int32, (128, 1), 0) & (CHUNK - 1))
    col = t0 + (lax.broadcasted_iota(jnp.int32, (1, 128), 1) & (CHUNK - 1))
    segr, segc = jnp.zeros_like(row), jnp.zeros_like(col)
    for k in range(4):
        start = ds_ref[k]
        here = (start >= t0).astype(jnp.int32)
        segr = segr + (row >= start).astype(jnp.int32) * here
        segc = segc + (col >= start).astype(jnp.int32) * here
    return segr, segc


def first_pass(c, t0, q, k, v, g, beta, ds_ref, sf, sb, chain, passed):
    i, j = iotas()
    segr, segc = segments(ds_ref, t0)
    same = ((i >> 6) == (j >> 6)) & (segr == segc)
    strict, causal = same & (i > j), same & (i >= j)
    tri = (((i >> 6) == (j >> 6)) & (i >= j)).astype(BF)
    rq = lax.rsqrt(rowsum(q * q) + EPSILON)
    rk = lax.rsqrt(rowsum(k * k) + EPSILON)
    qn, kn = q * rq, k * rk
    hi, lo = split(g)
    G = mm(cat([tri, tri], 1), cat([hi, lo]))
    mid = per_head([G[31:32], G[95:96]])
    last = per_head([G[63:64], G[127:128]])
    opening = (segr == 0).astype(F32)
    final = [segr[63:64], segr[127:128]]
    closing = (segr == cat([jnp.broadcast_to(f, (CHUNK, 1)) for f in final])).astype(F32)
    eg, es = jnp.exp(G - mid), jnp.exp(mid - G)
    eo = jnp.exp(G) * opening
    ex = jnp.exp(last - G) * closing
    kg, qg, ks = (kn * eg).astype(BF), (qn * eg).astype(BF), (kn * es).astype(BF)
    kout = (kn * ex).astype(BF)
    ap = mm(cat([kg, qg]), ks, 1, 1)
    a = jnp.where(strict, ap[:128], 0.0)
    p = jnp.where(causal, ap[128:], 0.0).astype(BF)
    t = invert(beta * a, i, j).astype(BF)
    uw = mm(t, cat([beta * v, beta * (kn * eo)], 1))
    u, w = uw[:, :128], uw[:, 128:]
    qt = qn * eo - mm(p, w)
    tk = mm(t, kout, 0, 0)
    pt = mm(p, t)
    for h, s in enumerate(HEADS):
        end = CHUNK * h + CHUNK - 1
        keep = jnp.exp(G[end : end + 1]) * (final[h] == 0).astype(F32)
        passed[c, h : h + 1, :] = keep
        kw = mm(kout[s], uw[s], 0, 0)
        chain[c, h, 0] = jnp.where(i == j, keep, 0.0) - kw[:, 128:]
        chain[c, h, 1] = kw[:, :128]
    wide = lambda z: jnp.broadcast_to(z, (128, 128))
    for slot, value in (
        (QN, qn), (KN, kn), (RQ, wide(rq)), (RK, wide(rk)), (EO, eo), (EG, eg), (ES, es),
        (EX, ex), (U_, u), (BETA, wide(beta)),
    ):
        sf[c, slot] = value
    for slot, value in (
        (QG, qg), (KG, kg), (KS, ks), (W_, w), (TK, tk), (KO, kout), (PT, pt),
        (CAUSAL, causal.astype(F32)), (STRICT, strict.astype(F32)),
    ):
        sb[c, slot] = value.astype(BF)
    return qt


def second_pass(c, S, dO, sf, sb):
    S = [s.astype(BF) for s in S]
    dO = dO.astype(BF)
    w = sb[c, W_]
    x = sf[c, U_] - cat([mm(w[s], S[h]) for h, s in enumerate(HEADS)])
    xb = x.astype(BF)
    dp = jnp.where(sb[c, CAUSAL].astype(F32) > 0, mm(dO, xb, 1, 1), 0.0).astype(BF)
    qs = cat([mm(dO[s], S[h], 1, 1) for h, s in enumerate(HEADS)]) * sf[c, EO]
    dqg = mm(dp, sb[c, KS])
    dks = mm(dp, sb[c, QG], 0, 0)
    y0 = mm(sb[c, PT], dO, 0, 0)
    return S, x, xb, qs, dqg, dks, y0


def third_pass(c, kept, D, sf, sb, passed):
    f = lambda slot: sf[c, slot]
    b = lambda slot: sb[c, slot]
    i, j = iotas()
    S, x, xb, qs, dqg, dks, y0 = kept
    D = [d.astype(BF) for d in D]
    tk, beta, eo = b(TK), f(BETA), f(EO)
    y = y0 + cat([mm(tk[s], D[h]) for h, s in enumerate(HEADS)])
    dbeta = rowsum(y * x) / beta[:, :1]
    dv = beta * y
    yb = y.astype(BF)
    da = jnp.where(b(STRICT).astype(F32) > 0, -beta * mm(yb, xb, 1, 1), 0.0).astype(BF)
    ke = cat([mm(yb[s], S[h], 1, 1) for h, s in enumerate(HEADS)]) * (-beta * eo)
    dko = cat([mm(xb[s], D[h], 1, 1) for h, s in enumerate(HEADS)])
    qg, kg, ks = b(QG), b(KG), b(KS)
    dkg = mm(da, ks)
    dks = dks + mm(da, kg, 0, 0)
    qn, kn, eg = f(QN), f(KN), f(EG)
    dq = qs + dqg * eg
    dk = ke + dkg * eg + dks * f(ES) + dko * f(EX)
    kd = b(KO).astype(F32) * dko
    dG = (
        qn * qs + qg.astype(F32) * dqg + kg.astype(F32) * dkg
        - ks.astype(F32) * dks + kn * ke - kd
    )
    ends = []
    for h, s in enumerate(HEADS):
        hi, lo = split(S[h].astype(F32) * D[h].astype(F32))
        through = mm(jnp.ones((8, 256), BF), cat([hi, lo], 1), 1, 1)[0:1]
        ends.append(jnp.sum(kd[s], axis=0, keepdims=True) + passed[c, h : h + 1, :] * through)
    hi, lo = split(dG)
    upper = (((i >> 6) == (j >> 6)) & (i <= j)).astype(BF)
    dg = mm(cat([upper, upper], 1), cat([hi, lo])) + per_head(ends)
    dqr = f(RQ) * (dq - qn * rowsum(qn * dq))
    dkr = f(RK) * (dk - kn * rowsum(kn * dk))
    return dqr, dkr, dv, dg, dbeta


def kernel(
    x_ref, og_ref, wq_ref, wk_ref, wv_ref, wo_ref, gate_ref, beta_ref, init_ref, ds_ref,
    ig_ref, gg_ref, bg_ref, sg_ref,
    gate, beta_in, start, ds, wcat, wo, wot, xg, raw, gcat, sf, sb, chain, passed, prefix, qe,
    own, heard, comm, states, grads, part, r1, t2, t2f, r2,
    wsem, gsend, grecv, esend, erecv, rsend, rrecv,
):
    seq, head = lax.axis_index("seq"), lax.axis_index("head")
    y, x = head // 4, head % 4
    z, core = seq // 2, seq % 2
    xs = [{"head": y * 4 + (x + o) % 4} for o in (1, 2, 3)]
    ys = [{"head": ((y + o) % 4) * 4 + x} for o in (1, 2, 3)]
    zs = [{"seq": ((z + o) % 4) * 2 + core} for o in (1, 2, 3)]
    sibling = {"seq": z * 2 + (1 - core)}

    loads = [
        pltpu.make_async_copy(
            ref.at[:, 128 * half : 128 * half + 128], xg.at[item, half, y, x], wsem.at[item, half]
        )
        for item, ref in enumerate((x_ref, og_ref))
        for half in (0, 1)
    ]
    loads += [
        pltpu.make_async_copy(ref, wcat.at[:, 256 * n : 256 * n + 256], wsem.at[2, n])
        for n, ref in enumerate((wq_ref, wk_ref, wv_ref))
    ]
    loads += [
        pltpu.make_async_copy(src, dst, wsem.at[3, n])
        for n, (src, dst) in enumerate((
            (wo_ref, wo), (gate_ref, gate), (beta_ref, beta_in), (init_ref, start), (ds_ref, ds)
        ))
    ]
    for load in loads:
        load.start()

    barrier = pltpu.get_barrier_semaphore()
    partners = xs + ys + zs + [sibling]
    for device in partners:
        pl.semaphore_signal(barrier, inc=1, device_id=device, device_id_type=MESH)

    pl.semaphore_wait(barrier, len(partners))

    sent = []
    for load in loads[:4]:
        load.wait()

    def remote(src, dst, ssem, rsem, device):
        copy = pltpu.make_async_remote_copy(
            src_ref=src, dst_ref=dst, send_sem=ssem, recv_sem=rsem,
            device_id=device, device_id_type=MESH,
        )
        sent.append(copy)
        return copy

    def gather(item, half, phase):
        axis = xs if (half + phase) % 2 == 0 else ys
        if phase == 0:
            block = xg.at[item, half, y, x]
        else:
            block = xg.at[item, 0, y] if half == 0 else xg.at[item, 1, :, x]
        return [
            remote(block, block, gsend.at[item, half, phase, o], grecv.at[item, half, phase, o],
                   axis[o])
            for o in (1, 0, 2)
        ]

    near = [[gather(item, half, 0) for half in (0, 1)] for item in (0, 1)]
    far = [[gather(item, half, 1) for half in (0, 1)] for item in (0, 1)]
    for item in (0, 1):
        for o in range(3):
            for half in (0, 1):
                near[item][half][o].start()
    for item in (0, 1):
        for half in (0, 1):
            for copy in near[item][half]:
                copy.wait_recv()
            for copy in far[item][half]:
                copy.start()

    for load in loads[4:]:
        load.wait()
    for n in range(18):
        wot[128 * n : 128 * n + 128, :] = wo[:, 128 * n : 128 * n + 128].T

    def project(item, weight, columns):
        for half in (0, 1):
            for copy in far[item][half]:
                copy.wait_recv()
            rows = xg[item, half].reshape(2304, 128)
            raw[128 * half : 128 * half + 128, columns] = mm(rows, weight[...], 0, 0)

    project(0, wcat, slice(0, 768))

    def stacked(ref, c, first):
        t = slice(CHUNK * c, CHUNK * c + CHUNK)
        return cat([ref[t, first : first + 128], ref[t, first + 128 : first + 256]])

    diagonal = (
        lax.broadcasted_iota(jnp.int32, (CHUNK, CHUNK), 0)
        == lax.broadcasted_iota(jnp.int32, (CHUNK, CHUNK), 1)
    )
    reads = []
    for c in range(CHUNKS):
        t = slice(CHUNK * c, CHUNK * c + CHUNK)
        beta = cat([rowsum(jnp.where(diagonal, beta_in[h : h + 1, t], 0.0)) for h in (0, 1)])
        reads.append(first_pass(
            c, seq * 256 + CHUNK * c,
            stacked(raw, c, 0), stacked(raw, c, 256), stacked(raw, c, 512),
            stacked(gate, c, 0), beta, ds, sf, sb, chain, passed,
        ))

    for h, rows in enumerate(HEADS):
        m, v = chain[0, h, 0], chain[0, h, 1]
        prefix[h, 0, :, :128], prefix[h, 0, :, 128:] = m, v
        for n in (1, 2, 3):
            step = mm(chain[n, h, 0], cat([m, v], 1))
            m, v = step[:, :128], step[:, 128:] + chain[n, h, 1]
            if n < 3:
                prefix[h, n, :, :128], prefix[h, n, :, 128:] = m, v
        own[h, 0], own[h, 1] = m.astype(BF), v.astype(BF)
    swap = remote(
        own.at[1 - core, pl.ds(0, 2)], heard.at[pl.ds(0, 2)], esend.at[0], erecv.at[0], sibling
    )
    swap.start()
    for h, rows in enumerate(HEADS):
        qe[h, 0:CHUNK] = reads[0][rows].astype(BF)
        for n in (1, 2, 3):
            qe[h, CHUNK * n : CHUNK * n + CHUNK] = mm(
                reads[n][rows], prefix[h, n - 1, :, :128]
            ).astype(BF)
    swap.wait_recv()
    first = core == 0
    m0, b0 = [jnp.where(first, own[core, n], heard[n]) for n in (0, 1)]
    m1, b1 = [jnp.where(first, heard[n], own[core, n]) for n in (0, 1)]
    both = mm(m1, cat([m0, b0], 1))
    comm[z, 0] = both[:, :128].astype(BF)
    comm[z, 1] = (both[:, 128:] + b1.astype(F32)).astype(BF)
    spread = [
        remote(comm.at[z, pl.ds(0, 2)], comm.at[z, pl.ds(0, 2)], esend.at[1 + o],
               erecv.at[1 + o], zs[o])
        for o in (1, 0, 2)
    ]
    for copy in spread:
        copy.start()

    project(1, wot, slice(768, 1024))

    for h in (0, 1):
        dO = raw[:, 768 + 128 * h : 896 + 128 * h]
        own[h, 2] = mm(qe[h], dO, 0, 0).astype(BF)
    swap_l = remote(own.at[1 - core, 2], heard.at[2], esend.at[4], erecv.at[4], sibling)
    swap_l.start()

    for copy in spread:
        copy.wait_recv()
    state, entering = start[core], start[core]
    for n in range(3):
        state = mm(comm[n, 0], state) + comm[n, 1].astype(F32)
        entering = jnp.where(z == n + 1, state, entering)
    after = mm(m0, entering) + b0.astype(F32)
    states[2] = jnp.where(first, after, entering).astype(BF)
    give_s = remote(states.at[2], states.at[core], esend.at[5], erecv.at[5], sibling)
    give_s.start()
    states[core] = jnp.where(first, entering, after).astype(BF)

    swap_l.wait_recv()
    l0 = jnp.where(first, own[core, 2], heard[2])
    l1 = jnp.where(first, heard[2], own[core, 2])
    comm[z, 2] = (l0.astype(F32) + mm(m0, l1, 0, 0)).astype(BF)
    spread_l = [
        remote(comm.at[z, 2], comm.at[z, 2], esend.at[6 + o], erecv.at[6 + o], zs[o])
        for o in (1, 0, 2)
    ]
    for copy in spread_l:
        copy.start()

    give_s.wait_recv()
    S = []
    for h in (0, 1):
        s = states[h]
        S.append([s] + [mm(prefix[h, n, :, :128], s) + prefix[h, n, :, 128:] for n in range(3)])
    kept = [
        second_pass(c, [S[0][c], S[1][c]], stacked(raw, c, 768), sf, sb) for c in range(CHUNKS)
    ]
    local = [[None] * CHUNKS, [None] * CHUNKS]
    turn = [[None] * CHUNKS, [None] * CHUNKS]
    for h, rows in enumerate(HEADS):
        for n in (3, 2, 1):
            step = mm(reads[n][rows], stacked(raw, n, 768)[rows], 0, 0)
            m = chain[n, h, 0]
            if n == 3:
                local[h][2], turn[h][2] = step, m.T
            else:
                local[h][n - 1] = mm(m, local[h][n], 0, 0) + step
                turn[h][n - 1] = mm(m, turn[h][n], 0, 0)

    for copy in spread_l:
        copy.wait_recv()
    grad = comm[3, 2].astype(F32)
    leaving = jnp.where(z == 2, grad, 0.0)
    for n in (2, 1, 0):
        grad = mm(comm[n, 0], grad, 0, 0) + comm[n, 2].astype(F32)
        leaving = jnp.where(z == n - 1, grad, leaving)
    before = mm(m1, leaving, 0, 0) + l1.astype(F32)
    grads[2, 0] = jnp.where(first, leaving, before).astype(BF)
    grads[2, 1] = grad.astype(BF)
    give_d = remote(grads.at[2], grads.at[core], esend.at[9], erecv.at[9], sibling)
    give_d.start()
    grads[core, 0] = jnp.where(first, before, leaving).astype(BF)
    grads[core, 1] = grad.astype(BF)
    give_d.wait_recv()

    D = []
    for h in (0, 1):
        sg_ref[h] = grads[h, 1].astype(F32)
        d = grads[h, 0]
        D.append([mm(turn[h][n], d) + local[h][n] for n in range(3)] + [d])

    def share(half, target):
        rows = gcat[128 * half : 128 * half + 128, :]
        if half == 0:
            return mm(wcat[pl.ds(pl.multiple_of(576 * target, 16), 576), :], rows, 1, 1)
        return cat([
            mm(wcat[pl.ds(pl.multiple_of(576 * n + 144 * target, 16), 144), :], rows, 1, 1)
            for n in range(4)
        ])

    sums = [[], []]
    for half, place, axis in ((0, y, ys), (1, x, xs)):
        for c in (2 * half, 2 * half + 1):
            t = slice(CHUNK * c, CHUNK * c + CHUNK)
            dq, dk, dv, dg, dbeta = third_pass(c, kept[c], [D[0][c], D[1][c]], sf, sb, passed)
            for h, s in enumerate(HEADS):
                for n, value in enumerate((dq, dk, dv)):
                    gcat[t, 256 * n + 128 * h : 256 * n + 128 * h + 128] = value[s].astype(BF)
                gg_ref[t, 128 * h : 128 * h + 128] = dg[s]
                bg_ref[h : h + 1, t] = jnp.sum(
                    jnp.where(diagonal, dbeta[s], 0.0), axis=0, keepdims=True
                )
        for o in (1, 0, 2):
            part[half, o] = share(half, (place + o + 1) % 4).astype(BF)
            copy = remote(
                part.at[half, o], r1.at[half, o], rsend.at[half, 0, o], rrecv.at[half, 0, o],
                axis[o],
            )
            copy.start()
            sums[half].append(copy)
    ends = [[], []]
    totals = [share(0, y), share(1, x)]
    for half, place, axis in ((0, x, xs), (1, y, ys)):
        total = totals[half]
        for copy in sums[half]:
            copy.wait_recv()
        for o in range(3):
            total = total + r1[half, o].astype(F32)
        t2f[half] = total.reshape(4, 144, 128)
        t2[half] = total.astype(BF).reshape(4, 144, 128)
        for o in (1, 0, 2):
            copy = remote(
                t2.at[half, (place + o + 1) % 4], r2.at[half, o],
                rsend.at[half, 1, o], rrecv.at[half, 1, o], axis[o],
            )
            copy.start()
            ends[half].append(copy)
    done = []
    for half, place in ((0, x), (1, y)):
        total = t2f[half, place]
        for copy in ends[half]:
            copy.wait_recv()
        for o in range(3):
            total = total + r2[half, o].astype(F32)
        done.append(total)
    ig_ref[...] = cat(done, 1).astype(BF)

    for copy in sent:
        copy.wait_send()


def finish(*refs):
    for n in range(4):
        refs[4 + n][...] = refs[n][...]


def per_device(inputs, output_grad, *others):
    vmem = pl.BlockSpec(memory_space=pltpu.VMEM)
    anywhere = pl.BlockSpec(memory_space=pl.ANY)
    scratch = lambda *shape, dtype=F32: pltpu.VMEM(shape, dtype)
    dma = lambda *shape: pltpu.SemaphoreType.DMA(shape)
    shapes = (
        jax.ShapeDtypeStruct((144, 256), BF),
        jax.ShapeDtypeStruct((256, 256), F32),
        jax.ShapeDtypeStruct((2, 256), F32),
        jax.ShapeDtypeStruct((2, 128, 128), F32),
    )
    results = pl.pallas_call(
        kernel,
        out_shape=shapes,
        in_specs=[anywhere] * 10,
        out_specs=(vmem,) * 4,
        scratch_shapes=[
            scratch(256, 256),
            scratch(2, 256),
            scratch(2, 128, 128),
            pltpu.SMEM((4,), jnp.int32),
            scratch(2304, 768, dtype=BF),
            scratch(256, 2304, dtype=BF),
            scratch(2304, 256, dtype=BF),
            scratch(2, 2, 4, 4, 144, 128, dtype=BF),
            scratch(256, 1024),
            scratch(256, 768, dtype=BF),
            scratch(CHUNKS, 10, 128, 128),
            scratch(CHUNKS, 9, 128, 128, dtype=BF),
            scratch(CHUNKS, 2, 2, 128, 128),
            scratch(CHUNKS, 8, 128),
            scratch(2, 3, 128, 256),
            scratch(2, 256, 128, dtype=BF),
            scratch(2, 3, 128, 128, dtype=BF),
            scratch(3, 128, 128, dtype=BF),
            scratch(4, 3, 128, 128, dtype=BF),
            scratch(3, 128, 128, dtype=BF),
            scratch(3, 2, 128, 128, dtype=BF),
            scratch(2, 3, 576, 128, dtype=BF),
            scratch(2, 3, 576, 128, dtype=BF),
            scratch(2, 4, 144, 128, dtype=BF),
            scratch(2, 4, 144, 128),
            scratch(2, 3, 144, 128, dtype=BF),
            dma(4, 5), dma(2, 2, 2, 3), dma(2, 2, 2, 3), dma(10), dma(10), dma(2, 2, 3), dma(2, 2, 3),
        ],
        compiler_params=pltpu.CompilerParams(
            collective_id=0, has_side_effects=True, vmem_limit_bytes=60 * 1024 * 1024
        ),
        cost_estimate=pl.CostEstimate(
            flops=3 * 10**9, bytes_accessed=6 * 10**6, transcendentals=3 * 10**5
        ),
    )(inputs.T, output_grad.T, *others)
    results = pl.pallas_call(
        finish,
        out_shape=shapes,
        in_specs=[vmem] * 4,
        out_specs=(vmem,) * 4,
    )(*results)
    return (results[0].T, *results[1:])


def solution(mesh):
    return jax.shard_map(
        per_device,
        mesh=mesh,
        in_specs=(
            P("seq", "head"),
            P("seq", "head"),
            P(None, "head"),
            P(None, "head"),
            P(None, "head"),
            P("head", None),
            P("seq", "head"),
            P("head", "seq"),
            P("head", None, None),
            P(),
        ),
        out_specs=(P("seq", "head"), P("seq", "head"), P("head", "seq"), P("head", None, None)),
        check_vma=False,
    )
```

```python
import jax
import jax.numpy as jnp
from jax import lax
from jax.experimental import pallas as pl
from jax.experimental.pallas import tpu as pltpu
from jax.sharding import PartitionSpec as P

F32, BF = jnp.float32, jnp.bfloat16
MESH = pl.DeviceIdType.MESH
CHUNK = 64
CHUNKS = 4
EPSILON = 1e-06


def mm(a, b, ca=1, cb=0):
    return lax.dot_general(
        a.astype(BF), b.astype(BF), (((ca,), (cb,)), ((), ())), preferred_element_type=F32
    )


def mm3(a, b, ca=1, cb=0):
    (ah, al), (bh, bl) = split(a), split(b)
    return mm(ah, bh, ca, cb) + (mm(ah, bl, ca, cb) + mm(al, bh, ca, cb))


def cat(parts, axis=0):
    return jnp.concatenate(parts, axis=axis)


def split(x):
    hi = x.astype(BF)
    return hi, (x - hi.astype(F32)).astype(BF)


def rowsum(x):
    return jnp.sum(x, axis=1, keepdims=True)


def per_head(rows):
    return cat([jnp.broadcast_to(r, (CHUNK, 128)) for r in rows])


def iotas():
    i = lax.broadcasted_iota(jnp.int32, (128, 128), 0)
    j = lax.broadcasted_iota(jnp.int32, (128, 128), 1)
    return i, j


HEADS = (slice(0, CHUNK), slice(CHUNK, 2 * CHUNK))


def together(steps):
    results = [None] * len(steps)
    live = list(range(len(steps)))
    while live:
        for n in list(live):
            try:
                next(steps[n])
            except StopIteration as stop:
                results[n] = stop.value
                live.remove(n)
    return results


def invert(n, i, j):
    eye = (i == j).astype(F32)
    d = jnp.where((i >> 4) == (j >> 4), n, 0.0)
    d2 = mm(d, d)
    yield
    p = mm(eye - d, eye + d2)
    d4 = mm(d2, d2)
    yield
    p = mm(p, eye + d4)
    d8 = mm(d4, d4)
    yield
    t = mm(p, eye + d8)
    yield
    for s in (4, 5):
        off = jnp.where(((i >> (s + 1)) == (j >> (s + 1))) & ((i >> s) != (j >> s)), n, 0.0)
        step = mm(off, t)
        yield
        t = t - mm(t, step)
        yield
    return t


(QN, KN, RQ, RK, EO, EG, ES, EX, U_, BETA) = range(10)
(QG, KG, KS, W_, TK, KO, PT, CAUSAL, STRICT) = range(9)


def segments(ds_ref, t0):
    row = t0 + (lax.broadcasted_iota(jnp.int32, (128, 1), 0) & (CHUNK - 1))
    col = t0 + (lax.broadcasted_iota(jnp.int32, (1, 128), 1) & (CHUNK - 1))
    segr, segc = jnp.zeros_like(row), jnp.zeros_like(col)
    for k in range(4):
        start = ds_ref[k]
        here = (start >= t0).astype(jnp.int32)
        segr = segr + (row >= start).astype(jnp.int32) * here
        segc = segc + (col >= start).astype(jnp.int32) * here
    return segr, segc


def first_pass(c, t0, q, k, v, g, beta, ds_ref, sf, sb, chain, passed):
    i, j = iotas()
    segr, segc = segments(ds_ref, t0)
    same = ((i >> 6) == (j >> 6)) & (segr == segc)
    strict, causal = same & (i > j), same & (i >= j)
    tri = (((i >> 6) == (j >> 6)) & (i >= j)).astype(BF)
    rq = lax.rsqrt(rowsum(q * q) + EPSILON)
    rk = lax.rsqrt(rowsum(k * k) + EPSILON)
    qn, kn = q * rq, k * rk
    hi, lo = split(g)
    G = mm(cat([tri, tri], 1), cat([hi, lo]))
    yield
    mid = per_head([G[31:32], G[95:96]])
    last = per_head([G[63:64], G[127:128]])
    opening = (segr == 0).astype(F32)
    final = [segr[63:64], segr[127:128]]
    closing = (segr == cat([jnp.broadcast_to(f, (CHUNK, 1)) for f in final])).astype(F32)
    eg, es = jnp.exp(G - mid), jnp.exp(mid - G)
    eo = jnp.exp(G) * opening
    ex = jnp.exp(last - G) * closing
    kg, qg, ks = (kn * eg).astype(BF), (qn * eg).astype(BF), (kn * es).astype(BF)
    kof = kn * ex
    kout = kof.astype(BF)
    yield
    ap = mm(cat([kg, qg]), ks, 1, 1)
    yield
    a = jnp.where(strict, ap[:128], 0.0)
    p = jnp.where(causal, ap[128:], 0.0).astype(BF)
    t = (yield from invert(beta * a, i, j)).astype(BF)
    uw = mm(t, cat([beta * v, beta * (kn * eo)], 1))
    yield
    u, w = uw[:, :128], uw[:, 128:]
    qt = qn * eo - mm(p, w)
    tk = mm(t, kout, 0, 0)
    pt = mm(p, t)
    yield
    for h, s in enumerate(HEADS):
        end = CHUNK * h + CHUNK - 1
        keep = jnp.exp(G[end : end + 1]) * (final[h] == 0).astype(F32)
        passed[c, h : h + 1, :] = keep
        kw = mm3(kof[s], uw[s], 0, 0)
        chain[c, h, 0] = jnp.where(i == j, keep, 0.0) - kw[:, 128:]
        chain[c, h, 1] = kw[:, :128]
    wide = lambda z: jnp.broadcast_to(z, (128, 128))
    for slot, value in (
        (QN, qn), (KN, kn), (RQ, wide(rq)), (RK, wide(rk)), (EO, eo), (EG, eg), (ES, es),
        (EX, ex), (U_, u), (BETA, wide(beta)),
    ):
        sf[c, slot] = value
    for slot, value in (
        (QG, qg), (KG, kg), (KS, ks), (W_, w), (TK, tk), (KO, kout), (PT, pt),
        (CAUSAL, causal.astype(F32)), (STRICT, strict.astype(F32)),
    ):
        sb[c, slot] = value.astype(BF)
    return qt


def second_pass(c, S, dO, sf, sb):
    S = [s.astype(BF) for s in S]
    dO = dO.astype(BF)
    w = sb[c, W_]
    x = sf[c, U_] - cat([mm(w[s], S[h]) for h, s in enumerate(HEADS)])
    xb = x.astype(BF)
    yield
    dp = jnp.where(sb[c, CAUSAL].astype(F32) > 0, mm(dO, xb, 1, 1), 0.0).astype(BF)
    qs = cat([mm(dO[s], S[h], 1, 1) for h, s in enumerate(HEADS)]) * sf[c, EO]
    yield
    dqg = mm(dp, sb[c, KS])
    dks = mm(dp, sb[c, QG], 0, 0)
    y0 = mm(sb[c, PT], dO, 0, 0)
    yield
    qn = sf[c, QN]
    dq = qs + dqg * sf[c, EG]
    dqr = sf[c, RQ] * (dq - qn * rowsum(qn * dq))
    gate = qn * qs + sb[c, QG].astype(F32) * dqg
    return dqr, (S, x, xb, gate, dks, y0)


def third_pass(c, kept, D, sf, sb):
    f = lambda slot: sf[c, slot]
    b = lambda slot: sb[c, slot]
    S, x, xb, gate, dks, y0 = kept
    D = [d.astype(BF) for d in D]
    tk, beta, eo = b(TK), f(BETA), f(EO)
    y = y0 + cat([mm(tk[s], D[h]) for h, s in enumerate(HEADS)])
    yb = y.astype(BF)
    yield
    da = jnp.where(b(STRICT).astype(F32) > 0, -beta * mm(yb, xb, 1, 1), 0.0).astype(BF)
    ke = cat([mm(yb[s], S[h], 1, 1) for h, s in enumerate(HEADS)]) * (-beta * eo)
    dko = cat([mm(xb[s], D[h], 1, 1) for h, s in enumerate(HEADS)])
    yield
    dkg = mm(da, b(KS))
    dks = dks + mm(da, b(KG), 0, 0)
    yield
    kn = f(KN)
    dk = ke + dkg * f(EG) + dks * f(ES) + dko * f(EX)
    dkr = f(RK) * (dk - kn * rowsum(kn * dk))
    return dkr, beta * y, (S, D, x, y, gate, ke, dko, dkg, dks)


def last_pass(c, kept, sf, sb, passed):
    i, j = iotas()
    S, D, x, y, gate, ke, dko, dkg, dks = kept
    dbeta = rowsum(y * x) / sf[c, BETA][:, :1]
    kd = sb[c, KO].astype(F32) * dko
    dG = (
        gate + sb[c, KG].astype(F32) * dkg - sb[c, KS].astype(F32) * dks + sf[c, KN] * ke - kd
    )
    ends = []
    for h, s in enumerate(HEADS):
        hi, lo = split(S[h].astype(F32) * D[h].astype(F32))
        through = mm(jnp.ones((8, 256), BF), cat([hi, lo], 1), 1, 1)[0:1]
        ends.append(jnp.sum(kd[s], axis=0, keepdims=True) + passed[c, h : h + 1, :] * through)
    hi, lo = split(dG)
    upper = (((i >> 6) == (j >> 6)) & (i <= j)).astype(BF)
    yield
    dg = mm(cat([upper, upper], 1), cat([hi, lo])) + per_head(ends)
    yield
    return dg, dbeta


def kernel(
    x_ref, og_ref, wq_ref, wk_ref, wv_ref, wo_ref, gate_ref, beta_ref, init_ref, ds_ref,
    ig_ref, gg_ref, bg_ref, sg_ref,
    gate, beta_in, start, ds, wcat, wo, wot, xg, raw, gcat, sf, sb, chain, passed, prefix, qe,
    own, heard, comm, states, grads, part, r1, t2, t2f, r2,
    wsem, gsend, grecv, esend, erecv, rsend, rrecv,
):
    seq, head = lax.axis_index("seq"), lax.axis_index("head")
    y, x = head // 4, head % 4
    z, core = seq // 2, seq % 2
    xs = [{"head": y * 4 + (x + o) % 4} for o in (1, 2, 3)]
    ys = [{"head": ((y + o) % 4) * 4 + x} for o in (1, 2, 3)]
    zs = [{"seq": ((z + o) % 4) * 2 + core} for o in (1, 2, 3)]
    sibling = {"seq": z * 2 + (1 - core)}

    loads = [
        pltpu.make_async_copy(
            ref.at[:, 128 * half : 128 * half + 128], xg.at[item, half, y, x], wsem.at[item, half]
        )
        for item, ref in enumerate((x_ref, og_ref))
        for half in (0, 1)
    ]
    loads += [
        pltpu.make_async_copy(ref, wcat.at[:, 256 * n : 256 * n + 256], wsem.at[2, n])
        for n, ref in enumerate((wq_ref, wk_ref, wv_ref))
    ]
    loads += [
        pltpu.make_async_copy(src, dst, wsem.at[3, n])
        for n, (src, dst) in enumerate((
            (wo_ref, wo), (gate_ref, gate), (beta_ref, beta_in), (init_ref, start), (ds_ref, ds)
        ))
    ]
    for load in loads:
        load.start()

    barrier = pltpu.get_barrier_semaphore()
    partners = xs + ys + zs + [sibling]
    for device in partners:
        pl.semaphore_signal(barrier, inc=1, device_id=device, device_id_type=MESH)

    pl.semaphore_wait(barrier, len(partners))

    sent = []
    for load in loads[:4]:
        load.wait()

    def remote(src, dst, ssem, rsem, device):
        copy = pltpu.make_async_remote_copy(
            src_ref=src, dst_ref=dst, send_sem=ssem, recv_sem=rsem,
            device_id=device, device_id_type=MESH,
        )
        sent.append(copy)
        return copy

    def gather(item, half, phase):
        axis = xs if (half + phase) % 2 == 0 else ys
        if phase == 0:
            block = xg.at[item, half, y, x]
        else:
            block = xg.at[item, 0, y] if half == 0 else xg.at[item, 1, :, x]
        return [
            remote(block, block, gsend.at[item, half, phase, o], grecv.at[item, half, phase, o],
                   axis[o])
            for o in (1, 0, 2)
        ]

    near = [[gather(item, half, 0) for half in (0, 1)] for item in (0, 1)]
    far = [[gather(item, half, 1) for half in (0, 1)] for item in (0, 1)]
    for item in (0, 1):
        for o in range(3):
            for half in (0, 1):
                near[item][half][o].start()
    for item in (0, 1):
        for half in (0, 1):
            for copy in near[item][half]:
                copy.wait_recv()
            for copy in far[item][half]:
                copy.start()

    for load in loads[4:]:
        load.wait()
    for n in range(18):
        wot[128 * n : 128 * n + 128, :] = wo[:, 128 * n : 128 * n + 128].T

    def project(item, weight, columns):
        for half in (0, 1):
            for copy in far[item][half]:
                copy.wait_recv()
            rows = xg[item, half].reshape(2304, 128)
            raw[128 * half : 128 * half + 128, columns] = mm(rows, weight[...], 0, 0)

    project(0, wcat, slice(0, 768))

    def stacked(ref, c, first):
        t = slice(CHUNK * c, CHUNK * c + CHUNK)
        return cat([ref[t, first : first + 128], ref[t, first + 128 : first + 256]])

    diagonal = (
        lax.broadcasted_iota(jnp.int32, (CHUNK, CHUNK), 0)
        == lax.broadcasted_iota(jnp.int32, (CHUNK, CHUNK), 1)
    )
    betas = [
        cat([
            rowsum(jnp.where(diagonal, beta_in[h : h + 1, CHUNK * c : CHUNK * c + CHUNK], 0.0))
            for h in (0, 1)
        ])
        for c in range(CHUNKS)
    ]
    reads = together([
        first_pass(
            c, seq * 256 + CHUNK * c,
            stacked(raw, c, 0), stacked(raw, c, 256), stacked(raw, c, 512),
            stacked(gate, c, 0), betas[c], ds, sf, sb, chain, passed,
        )
        for c in range(CHUNKS)
    ])

    pairs = [(chain[0, h, 0], chain[0, h, 1]) for h in (0, 1)]
    for n in range(CHUNKS):
        for h in (0, 1):
            m, v = pairs[h]
            if n > 0:
                step = mm3(chain[n, h, 0], cat([m, v], 1))
                m, v = step[:, :128], step[:, 128:] + chain[n, h, 1]
            if n < 3:
                prefix[h, n, :, :128], prefix[h, n, :, 128:] = m, v
            else:
                own[h, 0], own[h, 1] = m.astype(BF), v.astype(BF)
            pairs[h] = m, v
    swap = remote(
        own.at[1 - core, pl.ds(0, 2)], heard.at[pl.ds(0, 2)], esend.at[0], erecv.at[0], sibling
    )
    swap.start()
    for h, rows in enumerate(HEADS):
        qe[h, 0:CHUNK] = reads[0][rows].astype(BF)
        for n in (1, 2, 3):
            qe[h, CHUNK * n : CHUNK * n + CHUNK] = mm(
                reads[n][rows], prefix[h, n - 1, :, :128]
            ).astype(BF)
    swap.wait_recv()
    first = core == 0
    m0, b0 = [jnp.where(first, own[core, n], heard[n]) for n in (0, 1)]
    m1, b1 = [jnp.where(first, heard[n], own[core, n]) for n in (0, 1)]
    both = mm(m1, cat([m0, b0], 1))
    comm[z, 0] = both[:, :128].astype(BF)
    comm[z, 1] = (both[:, 128:] + b1.astype(F32)).astype(BF)
    spread = [
        remote(comm.at[z, pl.ds(0, 2)], comm.at[z, pl.ds(0, 2)], esend.at[1 + o],
               erecv.at[1 + o], zs[o])
        for o in (1, 0, 2)
    ]
    for copy in spread:
        copy.start()

    project(1, wot, slice(768, 1024))

    for h in (0, 1):
        dO = raw[:, 768 + 128 * h : 896 + 128 * h]
        own[h, 2] = mm(qe[h], dO, 0, 0).astype(BF)
    swap_l = remote(own.at[1 - core, 2], heard.at[2], esend.at[4], erecv.at[4], sibling)
    swap_l.start()

    swap_l.wait_recv()
    l0 = jnp.where(first, own[core, 2], heard[2])
    l1 = jnp.where(first, heard[2], own[core, 2])
    comm[z, 2] = (l0.astype(F32) + mm(m0, l1, 0, 0)).astype(BF)
    spread_l = [
        remote(comm.at[z, 2], comm.at[z, 2], esend.at[6 + o], erecv.at[6 + o], zs[o])
        for o in (1, 0, 2)
    ]
    for copy in spread_l:
        copy.start()

    for copy in spread:
        copy.wait_recv()
    state, entering = start[core], start[core]
    for n in range(3):
        state = mm(comm[n, 0], state) + comm[n, 1].astype(F32)
        entering = jnp.where(z == n + 1, state, entering)
    after = mm(m0, entering) + b0.astype(F32)
    states[2] = jnp.where(first, after, entering).astype(BF)
    give_s = remote(states.at[2], states.at[core], esend.at[5], erecv.at[5], sibling)
    give_s.start()
    states[core] = jnp.where(first, entering, after).astype(BF)

    local = [[None] * CHUNKS, [None] * CHUNKS]
    turn = [[None] * CHUNKS, [None] * CHUNKS]
    for n in (3, 2, 1):
        for h, rows in enumerate(HEADS):
            step = mm(reads[n][rows], stacked(raw, n, 768)[rows], 0, 0)
            m = chain[n, h, 0]
            if n == 3:
                local[h][2], turn[h][2] = step, m.T
            else:
                local[h][n - 1] = mm3(m, local[h][n], 0, 0) + step
                turn[h][n - 1] = mm3(m, turn[h][n], 0, 0)

    for copy in spread_l:
        copy.wait_recv()
    grad = comm[3, 2].astype(F32)
    leaving = jnp.where(z == 2, grad, 0.0)
    for n in (2, 1, 0):
        grad = mm(comm[n, 0], grad, 0, 0) + comm[n, 2].astype(F32)
        leaving = jnp.where(z == n - 1, grad, leaving)
    before = mm(m1, leaving, 0, 0) + l1.astype(F32)
    grads[2, 0] = jnp.where(first, leaving, before).astype(BF)
    grads[2, 1] = grad.astype(BF)
    give_d = remote(grads.at[2], grads.at[core], esend.at[9], erecv.at[9], sibling)
    give_d.start()
    grads[core, 0] = jnp.where(first, before, leaving).astype(BF)
    grads[core, 1] = grad.astype(BF)
    give_s.wait_recv()
    S = []
    for h in (0, 1):
        s = states[h]
        S.append([s] + [mm(prefix[h, n, :, :128], s) + prefix[h, n, :, 128:] for n in range(3)])
    outs = together([
        second_pass(c, [S[0][c], S[1][c]], stacked(raw, c, 768), sf, sb) for c in range(CHUNKS)
    ])
    kept = [rest for _, rest in outs]

    def keep_rows(c, first, value):
        for h, s in enumerate(HEADS):
            gcat[CHUNK * c : CHUNK * c + CHUNK, first + 128 * h : first + 128 * h + 128] = value[
                s
            ].astype(BF)

    for c, (dqr, _) in enumerate(outs):
        keep_rows(c, 0, dqr)
    give_d.wait_recv()

    D = []
    for h in (0, 1):
        sg_ref[h] = grads[h, 1].astype(F32)
        d = grads[h, 0]
        D.append([mm(turn[h][n], d) + local[h][n] for n in range(3)] + [d])

    def share(half, target):
        rows = gcat[128 * half : 128 * half + 128, :]
        if half == 0:
            return mm(wcat[pl.ds(pl.multiple_of(576 * target, 16), 576), :], rows, 1, 1)
        return cat([
            mm(wcat[pl.ds(pl.multiple_of(576 * n + 144 * target, 16), 144), :], rows, 1, 1)
            for n in range(4)
        ])

    outs = together([
        third_pass(c, kept[c], [D[0][c], D[1][c]], sf, sb) for c in range(CHUNKS)
    ])
    for c, (dkr, dv, _) in enumerate(outs):
        keep_rows(c, 256, dkr)
        keep_rows(c, 512, dv)
    sums = [[], []]
    for o in (1, 0, 2):
        for half, place, axis in ((0, y, ys), (1, x, xs)):
            part[half, o] = share(half, (place + o + 1) % 4).astype(BF)
            copy = remote(
                part.at[half, o], r1.at[half, o], rsend.at[half, 0, o], rrecv.at[half, 0, o],
                axis[o],
            )
            copy.start()
            sums[half].append(copy)
    for c, (dg, dbeta) in enumerate(together([
        last_pass(c, outs[c][2], sf, sb, passed) for c in range(CHUNKS)
    ])):
        t = slice(CHUNK * c, CHUNK * c + CHUNK)
        for h, s in enumerate(HEADS):
            gg_ref[t, 128 * h : 128 * h + 128] = dg[s]
            bg_ref[h : h + 1, t] = jnp.sum(
                jnp.where(diagonal, dbeta[s], 0.0), axis=0, keepdims=True
            )
    ends = [[], []]
    totals = [share(0, y), share(1, x)]
    for half, place, axis in ((0, x, xs), (1, y, ys)):
        total = totals[half]
        for copy in sums[half]:
            copy.wait_recv()
        for o in range(3):
            total = total + r1[half, o].astype(F32)
        t2f[half] = total.reshape(4, 144, 128)
        t2[half] = total.astype(BF).reshape(4, 144, 128)
        for o in (1, 0, 2):
            copy = remote(
                t2.at[half, (place + o + 1) % 4], r2.at[half, o],
                rsend.at[half, 1, o], rrecv.at[half, 1, o], axis[o],
            )
            copy.start()
            ends[half].append(copy)
    done = []
    for half, place in ((0, x), (1, y)):
        total = t2f[half, place]
        for copy in ends[half]:
            copy.wait_recv()
        for o in range(3):
            total = total + r2[half, o].astype(F32)
        done.append(total)
    ig_ref[...] = cat(done, 1).astype(BF)

    for copy in sent:
        copy.wait_send()


def finish(*refs):
    for n in range(4):
        refs[4 + n][...] = refs[n][...]


def per_device(inputs, output_grad, *others):
    vmem = pl.BlockSpec(memory_space=pltpu.VMEM)
    anywhere = pl.BlockSpec(memory_space=pl.ANY)
    scratch = lambda *shape, dtype=F32: pltpu.VMEM(shape, dtype)
    dma = lambda *shape: pltpu.SemaphoreType.DMA(shape)
    shapes = (
        jax.ShapeDtypeStruct((144, 256), BF),
        jax.ShapeDtypeStruct((256, 256), F32),
        jax.ShapeDtypeStruct((2, 256), F32),
        jax.ShapeDtypeStruct((2, 128, 128), F32),
    )
    results = pl.pallas_call(
        kernel,
        out_shape=shapes,
        in_specs=[anywhere] * 10,
        out_specs=(vmem,) * 4,
        scratch_shapes=[
            scratch(256, 256),
            scratch(2, 256),
            scratch(2, 128, 128),
            pltpu.SMEM((4,), jnp.int32),
            scratch(2304, 768, dtype=BF),
            scratch(256, 2304, dtype=BF),
            scratch(2304, 256, dtype=BF),
            scratch(2, 2, 4, 4, 144, 128, dtype=BF),
            scratch(256, 1024),
            scratch(256, 768, dtype=BF),
            scratch(CHUNKS, 10, 128, 128),
            scratch(CHUNKS, 9, 128, 128, dtype=BF),
            scratch(CHUNKS, 2, 2, 128, 128),
            scratch(CHUNKS, 8, 128),
            scratch(2, 3, 128, 256),
            scratch(2, 256, 128, dtype=BF),
            scratch(2, 3, 128, 128, dtype=BF),
            scratch(3, 128, 128, dtype=BF),
            scratch(4, 3, 128, 128, dtype=BF),
            scratch(3, 128, 128, dtype=BF),
            scratch(3, 2, 128, 128, dtype=BF),
            scratch(2, 3, 576, 128, dtype=BF),
            scratch(2, 3, 576, 128, dtype=BF),
            scratch(2, 4, 144, 128, dtype=BF),
            scratch(2, 4, 144, 128),
            scratch(2, 3, 144, 128, dtype=BF),
            dma(4, 5), dma(2, 2, 2, 3), dma(2, 2, 2, 3), dma(10), dma(10), dma(2, 2, 3), dma(2, 2, 3),
        ],
        compiler_params=pltpu.CompilerParams(
            collective_id=0, has_side_effects=True, vmem_limit_bytes=60 * 1024 * 1024
        ),
        cost_estimate=pl.CostEstimate(
            flops=3 * 10**9, bytes_accessed=6 * 10**6, transcendentals=3 * 10**5
        ),
    )(inputs.T, output_grad.T, *others)
    results = pl.pallas_call(
        finish,
        out_shape=shapes,
        in_specs=[vmem] * 4,
        out_specs=(vmem,) * 4,
    )(*results)
    return (results[0].T, *results[1:])


def solution(mesh):
    return jax.shard_map(
        per_device,
        mesh=mesh,
        in_specs=(
            P("seq", "head"),
            P("seq", "head"),
            P(None, "head"),
            P(None, "head"),
            P(None, "head"),
            P("head", None),
            P("seq", "head"),
            P("head", "seq"),
            P("head", None, None),
            P(),
        ),
        out_specs=(P("seq", "head"), P("seq", "head"), P("head", "seq"), P("head", None, None)),
        check_vma=False,
    )
```

```python
import jax
import jax.numpy as jnp
from jax import lax
from jax.experimental import pallas as pl
from jax.experimental.pallas import tpu as pltpu
from jax.sharding import PartitionSpec as P

F32, BF = jnp.float32, jnp.bfloat16
MESH = pl.DeviceIdType.MESH
CHUNK = 64
CHUNKS = 4
EPSILON = 1e-06


def mm(a, b, ca=1, cb=0):
    return lax.dot_general(
        a.astype(BF), b.astype(BF), (((ca,), (cb,)), ((), ())), preferred_element_type=F32
    )


def mm3(a, b, ca=1, cb=0):
    (ah, al), (bh, bl) = split(a), split(b)
    return mm(ah, bh, ca, cb) + (mm(ah, bl, ca, cb) + mm(al, bh, ca, cb))


def cat(parts, axis=0):
    return jnp.concatenate(parts, axis=axis)


def split(x):
    hi = x.astype(BF)
    return hi, (x - hi.astype(F32)).astype(BF)


def rowsum(x):
    return jnp.sum(x, axis=1, keepdims=True)


def per_head(rows):
    return cat([jnp.broadcast_to(r, (CHUNK, 128)) for r in rows])


def iotas():
    i = lax.broadcasted_iota(jnp.int32, (128, 128), 0)
    j = lax.broadcasted_iota(jnp.int32, (128, 128), 1)
    return i, j


HEADS = (slice(0, CHUNK), slice(CHUNK, 2 * CHUNK))


def together(steps, hooks=None):
    rounds, hooks = 0, hooks or {}
    results = [None] * len(steps)
    live = list(range(len(steps)))
    while live:
        if rounds in hooks:
            hooks[rounds]()
        rounds += 1
        for n in list(live):
            try:
                next(steps[n])
            except StopIteration as stop:
                results[n] = stop.value
                live.remove(n)
    return results


def invert(n, i, j):
    eye = (i == j).astype(F32)
    d = jnp.where((i >> 4) == (j >> 4), n, 0.0)
    d2 = mm(d, d)
    yield
    p = mm(eye - d, eye + d2)
    d4 = mm(d2, d2)
    yield
    p = mm(p, eye + d4)
    d8 = mm(d4, d4)
    yield
    t = mm(p, eye + d8)
    yield
    for s in (4, 5):
        off = jnp.where(((i >> (s + 1)) == (j >> (s + 1))) & ((i >> s) != (j >> s)), n, 0.0)
        step = mm(off, t)
        yield
        t = t - mm(t, step)
        yield
    return t


(QN, KN, RQ, RK, EO, EG, ES, EX, U_, BETA) = range(10)
(QG, KG, KS, W_, TK, KO, PT, CAUSAL, STRICT, TT) = range(10)


def segments(ds_ref, t0):
    row = t0 + (lax.broadcasted_iota(jnp.int32, (128, 1), 0) & (CHUNK - 1))
    col = t0 + (lax.broadcasted_iota(jnp.int32, (1, 128), 1) & (CHUNK - 1))
    segr, segc = jnp.zeros_like(row), jnp.zeros_like(col)
    for k in range(4):
        start = ds_ref[k]
        here = (start >= t0).astype(jnp.int32)
        segr = segr + (row >= start).astype(jnp.int32) * here
        segc = segc + (col >= start).astype(jnp.int32) * here
    return segr, segc


def key_pass(c, t0, k, v, g, beta, ds_ref, sf, sb, chain, passed):
    i, j = iotas()
    segr, segc = segments(ds_ref, t0)
    same = ((i >> 6) == (j >> 6)) & (segr == segc)
    strict, causal = same & (i > j), same & (i >= j)
    tri = (((i >> 6) == (j >> 6)) & (i >= j)).astype(BF)
    hi, lo = split(g)
    G = mm(cat([tri, tri], 1), cat([hi, lo]))
    rk = lax.rsqrt(rowsum(k * k) + EPSILON)
    kn = k * rk
    yield
    mid = per_head([G[31:32], G[95:96]])
    last = per_head([G[63:64], G[127:128]])
    opening = (segr == 0).astype(F32)
    final = [segr[63:64], segr[127:128]]
    closing = (segr == cat([jnp.broadcast_to(f, (CHUNK, 1)) for f in final])).astype(F32)
    eg, es = jnp.exp(G - mid), jnp.exp(mid - G)
    kg, ks = (kn * eg).astype(BF), (kn * es).astype(BF)
    a = mm(kg, ks, 1, 1)
    yield
    eo = jnp.exp(G) * opening
    ex = jnp.exp(last - G) * closing
    kof = kn * ex
    t = (yield from invert(beta * jnp.where(strict, a, 0.0), i, j)).astype(BF)
    uw = mm(t, cat([beta * v, beta * (kn * eo)], 1))
    yield
    u, w = uw[:, :128], uw[:, 128:]
    for h, s in enumerate(HEADS):
        end = CHUNK * h + CHUNK - 1
        keep = jnp.exp(G[end : end + 1]) * (final[h] == 0).astype(F32)
        passed[c, h : h + 1, :] = keep
        kw = mm3(kof[s], uw[s], 0, 0)
        chain[c, h, 0] = jnp.where(i == j, keep, 0.0) - kw[:, 128:]
        chain[c, h, 1] = kw[:, :128]
    wide = lambda z: jnp.broadcast_to(z, (128, 128))
    for slot, value in (
        (KN, kn), (RK, wide(rk)), (EO, eo), (EG, eg), (ES, es), (EX, ex), (U_, u),
        (BETA, wide(beta)),
    ):
        sf[c, slot] = value
    for slot, value in (
        (KG, kg), (KS, ks), (W_, w), (KO, kof), (TT, t),
        (CAUSAL, causal.astype(F32)), (STRICT, strict.astype(F32)),
    ):
        sb[c, slot] = value.astype(BF)


def query_pass(c, q, sf, sb):
    rq = lax.rsqrt(rowsum(q * q) + EPSILON)
    qn = q * rq
    qg = (qn * sf[c, EG]).astype(BF)
    p = mm(qg, sb[c, KS], 1, 1)
    t = sb[c, TT]
    tk = mm(t, sb[c, KO], 0, 0)
    yield
    p = jnp.where(sb[c, CAUSAL].astype(F32) > 0, p, 0.0).astype(BF)
    qt = qn * sf[c, EO] - mm(p, sb[c, W_])
    pt = mm(p, t)
    yield
    sf[c, QN], sf[c, RQ] = qn, jnp.broadcast_to(rq, (128, 128))
    sb[c, QG], sb[c, PT], sb[c, TK] = qg, pt.astype(BF), tk.astype(BF)
    return qt


def second_pass(c, S, dO, sf, sb):
    S = [s.astype(BF) for s in S]
    dO = dO.astype(BF)
    w = sb[c, W_]
    x = sf[c, U_] - cat([mm(w[s], S[h]) for h, s in enumerate(HEADS)])
    xb = x.astype(BF)
    yield
    dp = jnp.where(sb[c, CAUSAL].astype(F32) > 0, mm(dO, xb, 1, 1), 0.0).astype(BF)
    qs = cat([mm(dO[s], S[h], 1, 1) for h, s in enumerate(HEADS)]) * sf[c, EO]
    yield
    dqg = mm(dp, sb[c, KS])
    dks = mm(dp, sb[c, QG], 0, 0)
    yield
    qn = sf[c, QN]
    dq = qs + dqg * sf[c, EG]
    dqr = sf[c, RQ] * (dq - qn * rowsum(qn * dq))
    gate = qn * qs + sb[c, QG].astype(F32) * dqg
    return dqr, (S, x, xb, gate, dks)


def third_pass(c, kept, y0, tk, d, D, sf, sb):
    f = lambda slot: sf[c, slot]
    b = lambda slot: sb[c, slot]
    S, x, xb, gate, dks = kept
    beta, eo = f(BETA), f(EO)
    y = y0 + cat([mm(tk[s], d[h]) for h, s in enumerate(HEADS)])
    D = [z.astype(BF) for z in D]
    yb = y.astype(BF)
    yield
    da = jnp.where(b(STRICT).astype(F32) > 0, -beta * mm(yb, xb, 1, 1), 0.0).astype(BF)
    ke = cat([mm(yb[s], S[h], 1, 1) for h, s in enumerate(HEADS)]) * (-beta * eo)
    dko = cat([mm(xb[s], D[h], 1, 1) for h, s in enumerate(HEADS)])
    yield
    dkg = mm(da, b(KS))
    dks = dks + mm(da, b(KG), 0, 0)
    yield
    kn = f(KN)
    dk = ke + dkg * f(EG) + dks * f(ES) + dko * f(EX)
    dkr = f(RK) * (dk - kn * rowsum(kn * dk))
    return dkr, beta * y, (S, D, x, y, gate, ke, dko, dkg, dks)


def last_pass(c, kept, sf, sb, passed):
    i, j = iotas()
    S, D, x, y, gate, ke, dko, dkg, dks = kept
    dbeta = rowsum(y * x) / sf[c, BETA][:, :1]
    kd = sb[c, KO].astype(F32) * dko
    dG = (
        gate + sb[c, KG].astype(F32) * dkg - sb[c, KS].astype(F32) * dks + sf[c, KN] * ke - kd
    )
    ends = []
    for h, s in enumerate(HEADS):
        hi, lo = split(S[h].astype(F32) * D[h].astype(F32))
        through = mm(jnp.ones((8, 256), BF), cat([hi, lo], 1), 1, 1)[0:1]
        ends.append(jnp.sum(kd[s], axis=0, keepdims=True) + passed[c, h : h + 1, :] * through)
    hi, lo = split(dG)
    upper = (((i >> 6) == (j >> 6)) & (i <= j)).astype(BF)
    yield
    dg = mm(cat([upper, upper], 1), cat([hi, lo])) + per_head(ends)
    yield
    return dg, dbeta


def kernel(
    x_ref, og_ref, wq_ref, wk_ref, wv_ref, wo_ref, gate_ref, beta_ref, init_ref, ds_ref,
    ig_ref, gg_ref, bg_ref, sg_ref,
    gate, beta_in, start, ds, wcat, wo, wot, xg, raw, gcat, sf, sb, chain, passed, prefix, qe,
    own, heard, comm, states, grads, origin, part, r1, t2, t2f, r2,
    wsem, gsend, grecv, esend, erecv, rsend, rrecv,
):
    seq, head = lax.axis_index("seq"), lax.axis_index("head")
    y, x = head // 4, head % 4
    z, core = seq // 2, seq % 2
    xs = [{"head": y * 4 + (x + o) % 4} for o in (1, 2, 3)]
    ys = [{"head": ((y + o) % 4) * 4 + x} for o in (1, 2, 3)]
    zs = [{"seq": ((z + o) % 4) * 2 + core} for o in (1, 2, 3)]
    sibling = {"seq": z * 2 + (1 - core)}

    loads = [
        pltpu.make_async_copy(
            ref.at[:, 128 * half : 128 * half + 128], xg.at[item, half, y, x], wsem.at[item, half]
        )
        for item, ref in enumerate((x_ref, og_ref))
        for half in (0, 1)
    ]
    loads += [
        pltpu.make_async_copy(ref, wcat.at[:, 256 * n : 256 * n + 256], wsem.at[2, n])
        for n, ref in enumerate((wq_ref, wk_ref, wv_ref))
    ]
    loads += [
        pltpu.make_async_copy(src, dst, wsem.at[3, n])
        for n, (src, dst) in enumerate((
            (wo_ref, wo), (gate_ref, gate), (beta_ref, beta_in), (init_ref, start), (ds_ref, ds)
        ))
    ]
    for load in loads:
        load.start()

    barrier = pltpu.get_barrier_semaphore()
    partners = xs + ys + zs + [sibling]
    for device in partners:
        pl.semaphore_signal(barrier, inc=1, device_id=device, device_id_type=MESH)

    pl.semaphore_wait(barrier, len(partners))

    sent = []
    for load in loads[:4]:
        load.wait()

    def remote(src, dst, ssem, rsem, device):
        copy = pltpu.make_async_remote_copy(
            src_ref=src, dst_ref=dst, send_sem=ssem, recv_sem=rsem,
            device_id=device, device_id_type=MESH,
        )
        sent.append(copy)
        return copy

    def near(item, half):
        block = xg.at[item, half, y, x]
        axis = xs if half == 0 else ys
        return [
            remote(block, block, gsend.at[item, half, o], grecv.at[item, half, o], axis[o])
            for o in (1, 0, 2)
        ]

    def piece(item, half, group, n):
        pair = pl.ds(2 * n, 2)
        return xg.at[item, 0, group, pair] if half == 0 else xg.at[item, 1, pair, group]

    def far(item, half):
        place, axis = (y, ys) if half == 0 else (x, xs)
        copies = []
        for n, (forward, number) in enumerate(((0, 0), (2, 1), (0, 1), (2, 0))):
            block = piece(item, half, place, number)
            copies.append(remote(
                block, block, gsend.at[item, half, 3 + n], grecv.at[item, half, 3 + n],
                axis[forward],
            ))
        return copies

    def hand_on(item, half):
        place, axis = (y, ys) if half == 0 else (x, xs)
        copies = []
        for n, (forward, group) in enumerate(((0, (place + 3) % 4), (2, (place + 1) % 4))):
            block = piece(item, half, group, n)
            copies.append(remote(
                block, block, gsend.at[item, half, 7 + n], grecv.at[item, half, 7 + n],
                axis[forward],
            ))
        return copies

    parts = [(item, half) for item in (0, 1) for half in (0, 1)]
    nears = {part: near(*part) for part in parts}
    fars = {part: far(*part) for part in parts}
    relays = {part: hand_on(*part) for part in parts}

    def begin(item):
        for o in range(3):
            for half in (0, 1):
                nears[item, half][o].start()

    def widen(item):
        for half in (0, 1):
            for copy in nears[item, half]:
                copy.wait_recv()
        for n in range(4):
            for half in (0, 1):
                fars[item, half][n].start()

    def pass_on(item):
        for n in (0, 1):
            for half in (0, 1):
                fars[item, half][n].wait_recv()
                relays[item, half][n].start()

    def project(item, weight, taken, columns, groups):
        for half, place in ((0, y), (1, x)):
            rows = slice(128 * half, 128 * half + 128)
            for o in groups:
                group = (place + o) % 4
                if half == 0:
                    block = xg[item, 0, group].reshape(576, 128)
                    matrix = weight[pl.ds(pl.multiple_of(576 * group, 16), 576), taken]
                else:
                    block = cat([xg[item, 1, k, group] for k in range(4)])
                    matrix = cat([
                        weight[pl.ds(pl.multiple_of(576 * k + 144 * group, 16), 144), taken]
                        for k in range(4)
                    ])
                value = mm(block, matrix, 0, 0)
                if o == 0:
                    raw[rows, columns] = value
                else:
                    raw[rows, columns] += value

    begin(0)
    begin(1)
    widen(0)
    for load in loads[4:]:
        load.wait()
    first_rows = (0, wcat, slice(0, 768), slice(0, 768))
    second_rows = (1, wot, slice(0, 256), slice(768, 1024))
    project(*first_rows, (0,))
    pass_on(0)
    widen(1)
    for n in range(18):
        wot[128 * n : 128 * n + 128, :] = wo[:, 128 * n : 128 * n + 128].T
    for half in (0, 1):
        for copy in fars[0, half][2:]:
            copy.wait_recv()
    project(*first_rows, (1, 3))
    project(*second_rows, (0,))
    for half in (0, 1):
        for copy in relays[0, half]:
            copy.wait_recv()
    project(0, wcat, slice(256, 768), slice(256, 768), (2,))

    def stacked(ref, c, first):
        t = slice(CHUNK * c, CHUNK * c + CHUNK)
        return cat([ref[t, first : first + 128], ref[t, first + 128 : first + 256]])

    diagonal = (
        lax.broadcasted_iota(jnp.int32, (CHUNK, CHUNK), 0)
        == lax.broadcasted_iota(jnp.int32, (CHUNK, CHUNK), 1)
    )
    betas = [
        cat([
            rowsum(jnp.where(diagonal, beta_in[h : h + 1, CHUNK * c : CHUNK * c + CHUNK], 0.0))
            for h in (0, 1)
        ])
        for c in range(CHUNKS)
    ]
    together([
        key_pass(
            c, seq * 256 + CHUNK * c, stacked(raw, c, 256), stacked(raw, c, 512),
            stacked(gate, c, 0), betas[c], ds, sf, sb, chain, passed,
        )
        for c in range(CHUNKS)
    ], {5: lambda: pass_on(1)})

    def compose(n, m, v, h):
        step = mm3(chain[n, h, 0], cat([m, v], 1))
        return step[:, :128], step[:, 128:] + chain[n, h, 1]

    low = [compose(1, chain[0, h, 0], chain[0, h, 1], h) for h in (0, 1)]
    high = [compose(3, chain[2, h, 0], chain[2, h, 1], h) for h in (0, 1)]
    for h in (0, 1):
        step = mm3(high[h][0], cat(low[h], 1))
        own[h, 0] = step[:, :128].astype(BF)
        own[h, 1] = (step[:, 128:] + high[h][1]).astype(BF)
    swap = remote(
        own.at[1 - core, pl.ds(0, 2)], heard.at[pl.ds(0, 2)], esend.at[0], erecv.at[0], sibling
    )
    swap.start()
    project(0, wcat, slice(0, 256), slice(0, 256), (2,))
    for half in (0, 1):
        for copy in fars[1, half][2:]:
            copy.wait_recv()
    project(*second_rows, (1, 3))
    swap.wait_recv()
    first = core == 0
    m0, b0 = [jnp.where(first, own[core, n], heard[n]) for n in (0, 1)]
    m1, b1 = [jnp.where(first, heard[n], own[core, n]) for n in (0, 1)]
    m0t, m1t = [m.astype(F32).T.astype(BF) for m in (m0, m1)]
    both = mm(m1, cat([m0, b0], 1))
    comm[z, 0] = both[:, :128].astype(BF)
    comm[z, 1] = (both[:, 128:] + b1.astype(F32)).astype(BF)
    spread = [
        remote(comm.at[z, pl.ds(0, 2)], comm.at[z, pl.ds(0, 2)], esend.at[1 + o],
               erecv.at[1 + o], zs[o])
        for o in (1, 0, 2)
    ]
    for copy in spread:
        copy.start()

    reads = together([query_pass(c, stacked(raw, c, 0), sf, sb) for c in range(CHUNKS)])
    for h, rows in enumerate(HEADS):
        for n, pair in ((0, (chain[0, h, 0], chain[0, h, 1])), (1, low[h]),
                        (2, compose(2, *low[h], h))):
            prefix[h, n, :, :128], prefix[h, n, :, 128:] = pair
        qe[h, 0:CHUNK] = reads[0][rows].astype(BF)
        for n in (1, 2, 3):
            qe[h, CHUNK * n : CHUNK * n + CHUNK] = mm(
                reads[n][rows], prefix[h, n - 1, :, :128]
            ).astype(BF)
    for half in (0, 1):
        for copy in relays[1, half]:
            copy.wait_recv()
    project(*second_rows, (2,))

    for h in (0, 1):
        dO = raw[:, 768 + 128 * h : 896 + 128 * h]
        own[h, 2] = mm(qe[h], dO, 0, 0).astype(BF)
    swap_l = remote(own.at[1 - core, 2], heard.at[2], esend.at[4], erecv.at[4], sibling)
    swap_l.start()

    swap_l.wait_recv()
    l0 = jnp.where(first, own[core, 2], heard[2])
    l1 = jnp.where(first, heard[2], own[core, 2])
    comm[z, 2] = (l0.astype(F32) + mm(m0t, l1)).astype(BF)
    spread_l = [
        remote(comm.at[z, 2], comm.at[z, 2], esend.at[6 + o], erecv.at[6 + o], zs[o])
        for o in (1, 0, 2)
    ]
    for copy in spread_l:
        copy.start()

    for copy in spread:
        copy.wait_recv()
    state, entering = start[core], start[core]
    for n in range(3):
        state = mm(comm[n, 0], state) + comm[n, 1].astype(F32)
        entering = jnp.where(z == n + 1, state, entering)
    after = mm(m0, entering) + b0.astype(F32)
    states[2] = jnp.where(first, after, entering).astype(BF)
    give_s = remote(states.at[2], states.at[core], esend.at[5], erecv.at[5], sibling)
    give_s.start()
    states[core] = jnp.where(first, entering, after).astype(BF)

    turned = [comm[n, 0].astype(F32).T.astype(BF) for n in range(3)]
    across = mm(turned[1], turned[2])
    eye = (iotas()[0] == iotas()[1]).astype(F32)
    none = jnp.zeros_like(eye)
    pull = cat([
        jnp.where(z == 0, eye, none),
        jnp.where(z == 1, eye, jnp.where(z == 0, turned[1].astype(F32), none)),
        jnp.where(
            z == 2, eye,
            jnp.where(z == 1, turned[2].astype(F32), jnp.where(z == 0, across, none)),
        ),
    ], 1).astype(BF)
    pull = cat([pull, mm(m1t, pull).astype(BF)])

    local = [[None] * CHUNKS, [None] * CHUNKS]
    turn = [[None] * CHUNKS, [None] * CHUNKS]
    for n in (3, 2, 1):
        for h, rows in enumerate(HEADS):
            step = mm(reads[n][rows], stacked(raw, n, 768)[rows], 0, 0)
            m = chain[n, h, 0]
            if n == 3:
                local[h][2], turn[h][2] = step, m.T
            else:
                local[h][n - 1] = mm3(m, local[h][n], 0, 0) + step
                turn[h][n - 1] = mm3(m, turn[h][n], 0, 0)

    y0, pulls = [], []
    for c in range(CHUNKS):
        base = mm(sb[c, PT], stacked(raw, c, 768), 0, 0)
        tk = sb[c, TK]
        if c < 3:
            base = base + cat([mm(tk[s], local[h][c]) for h, s in enumerate(HEADS)])
            tk = cat([mm(tk[s], turn[h][c]) for h, s in enumerate(HEADS)]).astype(BF)
        y0.append(base)
        pulls.append(tk)

    for copy in spread_l:
        copy.wait_recv()
    last = comm[1:, 2].reshape(384, 128)
    pulled = mm(pull, last)
    leaving, before = pulled[:128], pulled[128:] + l1.astype(F32)
    grads[2] = jnp.where(first, leaving, before).astype(BF)
    give_d = remote(grads.at[2], grads.at[core], esend.at[9], erecv.at[9], sibling)
    give_d.start()
    grads[core] = jnp.where(first, before, leaving).astype(BF)
    give_s.wait_recv()
    S = []
    for h in (0, 1):
        s = states[h]
        S.append([s] + [mm(prefix[h, n, :, :128], s) + prefix[h, n, :, 128:] for n in range(3)])
    outs = together([
        second_pass(c, [S[0][c], S[1][c]], stacked(raw, c, 768), sf, sb) for c in range(CHUNKS)
    ])
    kept = [rest for _, rest in outs]

    def keep_rows(c, first, value):
        for h, s in enumerate(HEADS):
            gcat[CHUNK * c : CHUNK * c + CHUNK, first + 128 * h : first + 128 * h + 128] = value[
                s
            ].astype(BF)

    for c, (dqr, _) in enumerate(outs):
        keep_rows(c, 0, dqr)
    give_d.wait_recv()

    D, ends = [], [grads[0], grads[1]]
    for h in (0, 1):
        d = ends[h]
        D.append([mm(turn[h][n], d) + local[h][n] for n in range(3)] + [d])

    def share(half, target, n):
        rows = gcat[128 * half : 128 * half + 128, :]
        if half == 0:
            first_row = 576 * target + 288 * n
            return mm(wcat[pl.ds(pl.multiple_of(first_row, 16), 288), :], rows, 1, 1)
        return cat([
            mm(wcat[pl.ds(pl.multiple_of(576 * k + 144 * target, 16), 144), :], rows, 1, 1)
            for k in (2 * n, 2 * n + 1)
        ])

    outs = together([
        third_pass(c, kept[c], y0[c], pulls[c], ends, [D[0][c], D[1][c]], sf, sb) for c in range(CHUNKS)
    ])
    for c, (dkr, dv, _) in enumerate(outs):
        keep_rows(c, 256, dkr)
        keep_rows(c, 512, dv)
    inner = (
        last[:128].astype(F32) + mm(turned[1], last[128:256]) + mm(across, last[256:])
    )
    back = comm[0, 2].astype(F32) + mm(turned[0], inner)
    origin[2] = back.astype(BF)
    give_o = remote(origin.at[2], origin.at[core], esend.at[10], erecv.at[10], sibling)
    give_o.start()
    origin[core] = back.astype(BF)

    lines = ((0, y, ys), (1, x, xs))

    def send(half, slot, value, axis, forward):
        part[half, slot] = value.astype(BF)
        copy = remote(
            part.at[half, slot], r1.at[half, slot], rsend.at[half, slot], rrecv.at[half, slot],
            axis[forward],
        )
        copy.start()
        return copy

    sums = [[], []]
    for n, forward in ((0, 0), (1, 2)):
        for half, place, axis in lines:
            sums[half].append(
                send(half, n, share(half, (place + 2) % 4, n), axis, forward)
            )
    for n, forward in ((1, 0), (0, 2)):
        for half, place, axis in lines:
            target = (place + forward + 1) % 4
            sums[half].append(send(half, 3 - n, share(half, target, n), axis, forward))
    for n, forward in ((0, 0), (1, 2)):
        for half, place, axis in lines:
            value = share(half, (place + forward + 1) % 4, n)
            sums[half][n].wait_recv()
            value = value + r1[half, n].astype(F32)
            sums[half].append(send(half, 4 + n, value, axis, forward))
    for c, (dg, dbeta) in enumerate(together([
        last_pass(c, outs[c][2], sf, sb, passed) for c in range(CHUNKS)
    ])):
        t = slice(CHUNK * c, CHUNK * c + CHUNK)
        for h, s in enumerate(HEADS):
            gg_ref[t, 128 * h : 128 * h + 128] = dg[s]
            bg_ref[h : h + 1, t] = jnp.sum(
                jnp.where(diagonal, dbeta[s], 0.0), axis=0, keepdims=True
            )
    finals = [[], []]
    totals = [cat([share(half, place, n) for n in (0, 1)]) for half, place, _ in lines]
    for half, place, axis in ((0, x, xs), (1, y, ys)):
        for copy in sums[half][2:]:
            copy.wait_recv()
        got = [r1[half, n].astype(F32) for n in range(2, 6)]
        total = totals[half] + cat([got[1] + got[2], got[0] + got[3]])
        t2f[half] = total.reshape(4, 144, 128)
        t2[half] = total.astype(BF).reshape(4, 144, 128)
        for o in (1, 0, 2):
            copy = remote(
                t2.at[half, (place + o + 1) % 4], r2.at[half, o],
                rsend.at[half, 6 + o], rrecv.at[half, 6 + o], axis[o],
            )
            copy.start()
            finals[half].append(copy)
    done = []
    for half, place in ((0, x), (1, y)):
        total = t2f[half, place]
        for copy in finals[half]:
            copy.wait_recv()
        for o in range(3):
            total = total + r2[half, o].astype(F32)
        done.append(total)
    give_o.wait_recv()
    for h in (0, 1):
        sg_ref[h] = origin[h].astype(F32)
    ig_ref[...] = cat(done, 1).astype(BF)

    for copy in sent:
        copy.wait_send()


def finish(*refs):
    for n in range(4):
        refs[4 + n][...] = refs[n][...]


def per_device(inputs, output_grad, *others):
    vmem = pl.BlockSpec(memory_space=pltpu.VMEM)
    anywhere = pl.BlockSpec(memory_space=pl.ANY)
    scratch = lambda *shape, dtype=F32: pltpu.VMEM(shape, dtype)
    dma = lambda *shape: pltpu.SemaphoreType.DMA(shape)
    shapes = (
        jax.ShapeDtypeStruct((144, 256), BF),
        jax.ShapeDtypeStruct((256, 256), F32),
        jax.ShapeDtypeStruct((2, 256), F32),
        jax.ShapeDtypeStruct((2, 128, 128), F32),
    )
    results = pl.pallas_call(
        kernel,
        out_shape=shapes,
        in_specs=[anywhere] * 10,
        out_specs=(vmem,) * 4,
        scratch_shapes=[
            scratch(256, 256),
            scratch(2, 256),
            scratch(2, 128, 128),
            pltpu.SMEM((4,), jnp.int32),
            scratch(2304, 768, dtype=BF),
            scratch(256, 2304, dtype=BF),
            scratch(2304, 256, dtype=BF),
            scratch(2, 2, 4, 4, 144, 128, dtype=BF),
            scratch(256, 1024),
            scratch(256, 768, dtype=BF),
            scratch(CHUNKS, 10, 128, 128),
            scratch(CHUNKS, 10, 128, 128, dtype=BF),
            scratch(CHUNKS, 2, 2, 128, 128),
            scratch(CHUNKS, 8, 128),
            scratch(2, 3, 128, 256),
            scratch(2, 256, 128, dtype=BF),
            scratch(2, 3, 128, 128, dtype=BF),
            scratch(3, 128, 128, dtype=BF),
            scratch(4, 3, 128, 128, dtype=BF),
            scratch(3, 128, 128, dtype=BF),
            scratch(3, 128, 128, dtype=BF),
            scratch(3, 128, 128, dtype=BF),
            scratch(2, 6, 288, 128, dtype=BF),
            scratch(2, 6, 288, 128, dtype=BF),
            scratch(2, 4, 144, 128, dtype=BF),
            scratch(2, 4, 144, 128),
            scratch(2, 3, 144, 128, dtype=BF),
            dma(4, 5), dma(2, 2, 9), dma(2, 2, 9), dma(11), dma(11), dma(2, 9), dma(2, 9),
        ],
        compiler_params=pltpu.CompilerParams(
            collective_id=0, has_side_effects=True, vmem_limit_bytes=60 * 1024 * 1024
        ),
        cost_estimate=pl.CostEstimate(
            flops=3 * 10**9, bytes_accessed=6 * 10**6, transcendentals=3 * 10**5
        ),
    )(inputs.T, output_grad.T, *others)
    results = pl.pallas_call(
        finish,
        out_shape=shapes,
        in_specs=[vmem] * 4,
        out_specs=(vmem,) * 4,
    )(*results)
    return (results[0].T, *results[1:])


def solution(mesh):
    return jax.shard_map(
        per_device,
        mesh=mesh,
        in_specs=(
            P("seq", "head"),
            P("seq", "head"),
            P(None, "head"),
            P(None, "head"),
            P(None, "head"),
            P("head", None),
            P("seq", "head"),
            P("head", "seq"),
            P("head", None, None),
            P(),
        ),
        out_specs=(P("seq", "head"), P("seq", "head"), P("head", "seq"), P("head", None, None)),
        check_vma=False,
    )
```

```python
import jax
import jax.numpy as jnp
from jax import lax
from jax.experimental import pallas as pl
from jax.experimental.pallas import tpu as pltpu
from jax.sharding import PartitionSpec as P

F32, BF = jnp.float32, jnp.bfloat16
MESH = pl.DeviceIdType.MESH
CHUNK = 64
CHUNKS = 4
EPSILON = 1e-06


def mm(a, b, ca=1, cb=0):
    return lax.dot_general(
        a.astype(BF), b.astype(BF), (((ca,), (cb,)), ((), ())), preferred_element_type=F32
    )


def mm3(a, b, ca=1, cb=0):
    (ah, al), (bh, bl) = split(a), split(b)
    return mm(ah, bh, ca, cb) + (mm(ah, bl, ca, cb) + mm(al, bh, ca, cb))


def cat(parts, axis=0):
    return jnp.concatenate(parts, axis=axis)


def split(x):
    hi = x.astype(BF)
    return hi, (x - hi.astype(F32)).astype(BF)


def rowsum(x):
    return jnp.sum(x, axis=1, keepdims=True)


def per_head(rows):
    return cat([jnp.broadcast_to(r, (CHUNK, 128)) for r in rows])


def iotas():
    i = lax.broadcasted_iota(jnp.int32, (128, 128), 0)
    j = lax.broadcasted_iota(jnp.int32, (128, 128), 1)
    return i, j


HEADS = (slice(0, CHUNK), slice(CHUNK, 2 * CHUNK))


def together(steps, hooks=None):
    rounds, hooks = 0, hooks or {}
    results = [None] * len(steps)
    live = list(range(len(steps)))
    while live:
        if rounds in hooks:
            hooks[rounds]()
        rounds += 1
        for n in list(live):
            try:
                next(steps[n])
            except StopIteration as stop:
                results[n] = stop.value
                live.remove(n)
    return results


def invert(n, i, j):
    eye = (i == j).astype(F32)
    d = jnp.where((i >> 4) == (j >> 4), n, 0.0)
    d2 = mm(d, d)
    yield
    p = mm(eye - d, eye + d2)
    d4 = mm(d2, d2)
    yield
    p = mm(p, eye + d4)
    d8 = mm(d4, d4)
    yield
    t = mm(p, eye + d8)
    yield
    for s in (4, 5):
        off = jnp.where(((i >> (s + 1)) == (j >> (s + 1))) & ((i >> s) != (j >> s)), n, 0.0)
        step = mm(off, t)
        yield
        t = t - mm(t, step)
        yield
    return t


(QN, KN, RQ, RK, EO, EG, ES, EX, U_, BETA) = range(10)
(QG, KG, KS, W_, TK, KO, PT, CAUSAL, STRICT, TT) = range(10)


def segments(ds_ref, t0):
    row = t0 + (lax.broadcasted_iota(jnp.int32, (128, 1), 0) & (CHUNK - 1))
    col = t0 + (lax.broadcasted_iota(jnp.int32, (1, 128), 1) & (CHUNK - 1))
    segr, segc = jnp.zeros_like(row), jnp.zeros_like(col)
    for k in range(4):
        start = ds_ref[k]
        here = (start >= t0).astype(jnp.int32)
        segr = segr + (row >= start).astype(jnp.int32) * here
        segc = segc + (col >= start).astype(jnp.int32) * here
    return segr, segc


def key_pass(c, t0, k, v, g, beta, ds_ref, sf, sb, chain, passed):
    i, j = iotas()
    segr, segc = segments(ds_ref, t0)
    same = ((i >> 6) == (j >> 6)) & (segr == segc)
    strict, causal = same & (i > j), same & (i >= j)
    tri = (((i >> 6) == (j >> 6)) & (i >= j)).astype(BF)
    hi, lo = split(g)
    G = mm(cat([tri, tri], 1), cat([hi, lo]))
    rk = lax.rsqrt(rowsum(k * k) + EPSILON)
    kn = k * rk
    yield
    mid = per_head([G[31:32], G[95:96]])
    last = per_head([G[63:64], G[127:128]])
    opening = (segr == 0).astype(F32)
    final = [segr[63:64], segr[127:128]]
    closing = (segr == cat([jnp.broadcast_to(f, (CHUNK, 1)) for f in final])).astype(F32)
    eg, es = jnp.exp(G - mid), jnp.exp(mid - G)
    kg, ks = (kn * eg).astype(BF), (kn * es).astype(BF)
    a = mm(kg, ks, 1, 1)
    yield
    eo = jnp.exp(G) * opening
    ex = jnp.exp(last - G) * closing
    kof = kn * ex
    t = (yield from invert(beta * jnp.where(strict, a, 0.0), i, j)).astype(BF)
    uw = mm(t, cat([beta * v, beta * (kn * eo)], 1))
    yield
    u, w = uw[:, :128], uw[:, 128:]
    for h, s in enumerate(HEADS):
        end = CHUNK * h + CHUNK - 1
        keep = jnp.exp(G[end : end + 1]) * (final[h] == 0).astype(F32)
        passed[c, h : h + 1, :] = keep
        kw = mm3(kof[s], uw[s], 0, 0)
        chain[c, h, 0] = jnp.where(i == j, keep, 0.0) - kw[:, 128:]
        chain[c, h, 1] = kw[:, :128]
    wide = lambda z: jnp.broadcast_to(z, (128, 128))
    for slot, value in (
        (KN, kn), (RK, wide(rk)), (EO, eo), (EG, eg), (ES, es), (EX, ex), (U_, u),
        (BETA, wide(beta)),
    ):
        sf[c, slot] = value
    for slot, value in (
        (KG, kg), (KS, ks), (W_, w), (KO, kof), (TT, t),
        (CAUSAL, causal.astype(F32)), (STRICT, strict.astype(F32)),
    ):
        sb[c, slot] = value.astype(BF)


def query_pass(c, q, sf, sb):
    rq = lax.rsqrt(rowsum(q * q) + EPSILON)
    qn = q * rq
    qg = (qn * sf[c, EG]).astype(BF)
    p = mm(qg, sb[c, KS], 1, 1)
    t = sb[c, TT]
    tk = mm(t, sb[c, KO], 0, 0)
    yield
    p = jnp.where(sb[c, CAUSAL].astype(F32) > 0, p, 0.0).astype(BF)
    qt = qn * sf[c, EO] - mm(p, sb[c, W_])
    pt = mm(p, t)
    yield
    sf[c, QN], sf[c, RQ] = qn, jnp.broadcast_to(rq, (128, 128))
    sb[c, QG], sb[c, PT], sb[c, TK] = qg, pt.astype(BF), tk.astype(BF)
    return qt


def second_pass(c, S, dO, sf, sb):
    S = [s.astype(BF) for s in S]
    dO = dO.astype(BF)
    w = sb[c, W_]
    x = sf[c, U_] - cat([mm(w[s], S[h]) for h, s in enumerate(HEADS)])
    xb = x.astype(BF)
    yield
    dp = jnp.where(sb[c, CAUSAL].astype(F32) > 0, mm(dO, xb, 1, 1), 0.0).astype(BF)
    qs = cat([mm(dO[s], S[h], 1, 1) for h, s in enumerate(HEADS)]) * sf[c, EO]
    yield
    dqg = mm(dp, sb[c, KS])
    dks = mm(dp, sb[c, QG], 0, 0)
    yield
    qn = sf[c, QN]
    dq = qs + dqg * sf[c, EG]
    dqr = sf[c, RQ] * (dq - qn * rowsum(qn * dq))
    gate = qn * qs + sb[c, QG].astype(F32) * dqg
    return dqr, (S, x, xb, gate, dks)


def third_pass(c, kept, y0, tk, d, D, sf, sb):
    f = lambda slot: sf[c, slot]
    b = lambda slot: sb[c, slot]
    S, x, xb, gate, dks = kept
    beta, eo = f(BETA), f(EO)
    y = y0 + cat([mm(tk[s], d[h]) for h, s in enumerate(HEADS)])
    D = [z.astype(BF) for z in D]
    yb = y.astype(BF)
    yield
    da = jnp.where(b(STRICT).astype(F32) > 0, -beta * mm(yb, xb, 1, 1), 0.0).astype(BF)
    ke = cat([mm(yb[s], S[h], 1, 1) for h, s in enumerate(HEADS)]) * (-beta * eo)
    dko = cat([mm(xb[s], D[h], 1, 1) for h, s in enumerate(HEADS)])
    yield
    dkg = mm(da, b(KS))
    dks = dks + mm(da, b(KG), 0, 0)
    yield
    kn = f(KN)
    dk = ke + dkg * f(EG) + dks * f(ES) + dko * f(EX)
    dkr = f(RK) * (dk - kn * rowsum(kn * dk))
    return dkr, beta * y, (S, D, x, y, gate, ke, dko, dkg, dks)


def last_pass(c, kept, sf, sb, passed):
    i, j = iotas()
    S, D, x, y, gate, ke, dko, dkg, dks = kept
    dbeta = rowsum(y * x) / sf[c, BETA][:, :1]
    kd = sb[c, KO].astype(F32) * dko
    dG = (
        gate + sb[c, KG].astype(F32) * dkg - sb[c, KS].astype(F32) * dks + sf[c, KN] * ke - kd
    )
    ends = []
    for h, s in enumerate(HEADS):
        hi, lo = split(S[h].astype(F32) * D[h].astype(F32))
        through = mm(jnp.ones((8, 256), BF), cat([hi, lo], 1), 1, 1)[0:1]
        ends.append(jnp.sum(kd[s], axis=0, keepdims=True) + passed[c, h : h + 1, :] * through)
    hi, lo = split(dG)
    upper = (((i >> 6) == (j >> 6)) & (i <= j)).astype(BF)
    yield
    dg = mm(cat([upper, upper], 1), cat([hi, lo])) + per_head(ends)
    yield
    return dg, dbeta


def kernel(
    x_ref, og_ref, wq_ref, wk_ref, wv_ref, wo_ref, gate_ref, beta_ref, init_ref, ds_ref,
    ig_ref, gg_ref, bg_ref, sg_ref,
    gg, bg, gate, beta_in, start, ds, wcat, wo, wot, xg, raw, gcat, sf, sb, chain, passed, prefix, qe,
    own, heard, comm, states, grads, origin, part, r1, t2, t2f, r2,
    wsem, gsend, grecv, esend, erecv, rsend, rrecv,
):
    seq, head = lax.axis_index("seq"), lax.axis_index("head")
    y, x = head // 4, head % 4
    z, core = seq // 2, seq % 2
    xs = [{"head": y * 4 + (x + o) % 4} for o in (1, 2, 3)]
    ys = [{"head": ((y + o) % 4) * 4 + x} for o in (1, 2, 3)]
    zs = [{"seq": ((z + o) % 4) * 2 + core} for o in (1, 2, 3)]
    sibling = {"seq": z * 2 + (1 - core)}

    loads = [
        pltpu.make_async_copy(
            ref.at[:, 128 * half : 128 * half + 128], xg.at[item, half, y, x], wsem.at[item, half]
        )
        for item, ref in enumerate((x_ref, og_ref))
        for half in (0, 1)
    ]
    loads += [
        pltpu.make_async_copy(ref, wcat.at[:, 256 * n : 256 * n + 256], wsem.at[2, n])
        for n, ref in enumerate((wq_ref, wk_ref, wv_ref))
    ]
    loads += [
        pltpu.make_async_copy(src, dst, wsem.at[3, n])
        for n, (src, dst) in enumerate((
            (wo_ref, wo), (gate_ref, gate), (beta_ref, beta_in), (init_ref, start), (ds_ref, ds)
        ))
    ]
    comm[...] = jnp.zeros_like(comm)
    barrier = pltpu.get_barrier_semaphore()
    partners = xs + ys + zs + [sibling]
    for device in partners:
        pl.semaphore_signal(barrier, inc=1, device_id=device, device_id_type=MESH)

    for load in loads:
        load.start()
    pl.semaphore_wait(barrier, len(partners))

    sent = []

    def remote(src, dst, ssem, rsem, device):
        copy = pltpu.make_async_remote_copy(
            src_ref=src, dst_ref=dst, send_sem=ssem, recv_sem=rsem,
            device_id=device, device_id_type=MESH,
        )
        sent.append(copy)
        return copy

    def near(item, half):
        block = xg.at[item, half, y, x]
        source = (x_ref, og_ref)[item].at[:, 128 * half : 128 * half + 128]
        axis = xs if half == 0 else ys
        return [
            remote(source, block, gsend.at[item, half, o], grecv.at[item, half, o], axis[o])
            for o in (1, 0, 2)
        ]

    def piece(item, half, group, first, count):
        taken = pl.ds(first, count)
        return xg.at[item, 0, group, taken] if half == 0 else xg.at[item, 1, taken, group]

    def far(item, half):
        place, axis = (y, ys) if half == 0 else (x, xs)
        single = ((0, 0, 1), (2, 2, 1), (0, 1, 1), (2, 3, 1))
        double = ((0, 0, 2), (2, 2, 2))
        copies = []
        for n, (forward, first, count) in enumerate(
            (single if item == 0 else double) + ((0, 2, 2), (2, 0, 2))
        ):
            block = piece(item, half, place, first, count)
            copies.append(remote(
                block, block, gsend.at[item, half, 3 + n], grecv.at[item, half, 3 + n],
                axis[forward],
            ))
        return copies

    def hand_on(item, half):
        place, axis = (y, ys) if half == 0 else (x, xs)
        single = ((0, 0, 1), (2, 2, 1), (0, 1, 1), (2, 3, 1))
        double = ((0, 0, 2), (2, 2, 2))
        copies = []
        for n, (forward, first, count) in enumerate(single if item == 0 else double):
            group = (place + 3) % 4 if forward == 0 else (place + 1) % 4
            block = piece(item, half, group, first, count)
            copies.append(remote(
                block, block, gsend.at[item, half, 9 + n], grecv.at[item, half, 9 + n],
                axis[forward],
            ))
        return copies

    parts = [(item, half) for item in (0, 1) for half in (0, 1)]
    nears = {part: near(*part) for part in parts}
    fars = {part: far(*part) for part in parts}
    relays = {part: hand_on(*part) for part in parts}

    def begin(item):
        for o in range(3):
            for half in (0, 1):
                nears[item, half][o].start()

    def widen(item):
        for half in (0, 1):
            for copy in nears[item, half]:
                copy.wait_recv()
        for n in range(len(fars[item, 0])):
            for half in (0, 1):
                fars[item, half][n].start()

    def pass_on(item):
        for n in range(len(relays[item, 0])):
            for half in (0, 1):
                fars[item, half][n].wait_recv()
                relays[item, half][n].start()

    def project(item, weight, taken, columns, groups):
        for half, place in ((0, y), (1, x)):
            rows = slice(128 * half, 128 * half + 128)
            for o in groups:
                group = (place + o) % 4
                if half == 0:
                    block = xg[item, 0, group].reshape(576, 128)
                    matrix = weight[pl.ds(pl.multiple_of(576 * group, 16), 576), taken]
                else:
                    block = cat([xg[item, 1, k, group] for k in range(4)])
                    matrix = cat([
                        weight[pl.ds(pl.multiple_of(576 * k + 144 * group, 16), 144), taken]
                        for k in range(4)
                    ])
                value = mm(block, matrix, 0, 0)
                if o == 0:
                    raw[rows, columns] = value
                else:
                    raw[rows, columns] += value

    begin(0)
    begin(1)
    for load in loads[:4]:
        load.wait()
    widen(0)
    for load in loads[4:]:
        load.wait()
    first_rows = (0, wcat, slice(0, 768), slice(0, 768))
    second_rows = (1, wot, slice(0, 256), slice(768, 1024))
    project(*first_rows, (0,))
    pass_on(0)
    widen(1)
    for n in range(18):
        wot[128 * n : 128 * n + 128, :] = wo[:, 128 * n : 128 * n + 128].T
    for half in (0, 1):
        for copy in fars[0, half][4:]:
            copy.wait_recv()
    project(*first_rows, (1, 3))
    project(*second_rows, (0,))
    for half in (0, 1):
        for copy in relays[0, half]:
            copy.wait_recv()
    project(0, wcat, slice(256, 768), slice(256, 768), (2,))

    def stacked(ref, c, first):
        t = slice(CHUNK * c, CHUNK * c + CHUNK)
        return cat([ref[t, first : first + 128], ref[t, first + 128 : first + 256]])

    diagonal = (
        lax.broadcasted_iota(jnp.int32, (CHUNK, CHUNK), 0)
        == lax.broadcasted_iota(jnp.int32, (CHUNK, CHUNK), 1)
    )
    betas = [
        cat([
            rowsum(jnp.where(diagonal, beta_in[h : h + 1, CHUNK * c : CHUNK * c + CHUNK], 0.0))
            for h in (0, 1)
        ])
        for c in range(CHUNKS)
    ]
    together([
        key_pass(
            c, seq * 256 + CHUNK * c, stacked(raw, c, 256), stacked(raw, c, 512),
            stacked(gate, c, 0), betas[c], ds, sf, sb, chain, passed,
        )
        for c in range(CHUNKS)
    ], {2: lambda: pass_on(1)})

    def compose(n, m, v, h):
        step = mm3(chain[n, h, 0], cat([m, v], 1))
        return step[:, :128], step[:, 128:] + chain[n, h, 1]

    low = [compose(1, chain[0, h, 0], chain[0, h, 1], h) for h in (0, 1)]
    high = [compose(3, chain[2, h, 0], chain[2, h, 1], h) for h in (0, 1)]
    for h in (0, 1):
        step = mm3(high[h][0], cat(low[h], 1))
        own[h, 0] = step[:, :128].astype(BF)
        own[h, 1] = (step[:, 128:] + high[h][1]).astype(BF)
    swap = remote(
        own.at[1 - core, pl.ds(0, 2)], heard.at[pl.ds(0, 2)], esend.at[0], erecv.at[0], sibling
    )
    swap.start()
    project(0, wcat, slice(0, 256), slice(0, 256), (2,))
    reads = together([query_pass(c, stacked(raw, c, 0), sf, sb) for c in range(CHUNKS)])
    swap.wait_recv()
    first = core == 0
    m0, b0 = [jnp.where(first, own[core, n], heard[n]) for n in (0, 1)]
    m1, b1 = [jnp.where(first, heard[n], own[core, n]) for n in (0, 1)]
    m0t, m1t = [m.astype(F32).T.astype(BF) for m in (m0, m1)]
    both = mm(m1, cat([m0, b0], 1))
    comm[z, 0] = both[:, :128].astype(BF)
    comm[z, 1] = (both[:, 128:] + b1.astype(F32)).astype(BF)
    def line(first, count, number, o):
        block = comm.at[z, pl.ds(first, count)]
        return pltpu.make_async_remote_copy(
            src_ref=block, dst_ref=block, send_sem=esend.at[number], recv_sem=erecv.at[number],
            device_id=zs[o - 1], device_id_type=MESH,
        )

    both_maps = {o: line(0, 2, o, o) for o in (1, 2, 3)}
    one_map = {o: line(0, 1, o, o) for o in (1, 2, 3)}
    back = {o: line(2, 1, 5 + o, o) for o in (1, 2, 3)}
    for o in (2, 1, 3):
        pl.when(z < 4 - o)(both_maps[o].start)
        pl.when(z >= 4 - o)(one_map[o].start)

    for half in (0, 1):
        for copy in fars[1, half][2:]:
            copy.wait_recv()
    project(*second_rows, (1, 3))
    for h, rows in enumerate(HEADS):
        for n, pair in ((0, (chain[0, h, 0], chain[0, h, 1])), (1, low[h]),
                        (2, compose(2, *low[h], h))):
            prefix[h, n, :, :128], prefix[h, n, :, 128:] = pair
        qe[h, 0:CHUNK] = reads[0][rows].astype(BF)
        for n in (1, 2, 3):
            qe[h, CHUNK * n : CHUNK * n + CHUNK] = mm(
                reads[n][rows], prefix[h, n - 1, :, :128]
            ).astype(BF)
    for half in (0, 1):
        for copy in relays[1, half]:
            copy.wait_recv()
    project(*second_rows, (2,))

    for h in (0, 1):
        dO = raw[:, 768 + 128 * h : 896 + 128 * h]
        own[h, 2] = mm(qe[h], dO, 0, 0).astype(BF)
    swap_l = remote(own.at[1 - core, 2], heard.at[2], esend.at[4], erecv.at[4], sibling)
    swap_l.start()

    bases = [mm(sb[c, PT], stacked(raw, c, 768), 0, 0) for c in range(CHUNKS)]
    swap_l.wait_recv()
    l0 = jnp.where(first, own[core, 2], heard[2])
    l1 = jnp.where(first, heard[2], own[core, 2])
    comm[z, 2] = (l0.astype(F32) + mm(m0t, l1)).astype(BF)
    for o in (2, 1, 3):
        pl.when(z >= 4 - o)(back[o].start)

    for o in (1, 2, 3):
        pl.when(z >= o)(both_maps[o].wait_recv)
        pl.when(z < o)(one_map[o].wait_recv)
    state, entering = start[core], start[core]
    for n in range(3):
        state = mm(comm[n, 0], state) + comm[n, 1].astype(F32)
        entering = jnp.where(z == n + 1, state, entering)
    after = mm(m0, entering) + b0.astype(F32)
    states[2] = jnp.where(first, after, entering).astype(BF)
    give_s = remote(states.at[2], states.at[core], esend.at[5], erecv.at[5], sibling)
    give_s.start()
    states[core] = jnp.where(first, entering, after).astype(BF)

    turned = [comm[n, 0].astype(F32).T.astype(BF) for n in range(3)]
    across = mm(turned[1], turned[2])
    eye = (iotas()[0] == iotas()[1]).astype(F32)
    none = jnp.zeros_like(eye)
    pull = cat([
        jnp.where(z == 0, eye, none),
        jnp.where(z == 1, eye, jnp.where(z == 0, turned[1].astype(F32), none)),
        jnp.where(
            z == 2, eye,
            jnp.where(z == 1, turned[2].astype(F32), jnp.where(z == 0, across, none)),
        ),
    ], 1).astype(BF)
    pull = cat([pull, mm(m1t, pull).astype(BF)])

    local = [[None] * CHUNKS, [None] * CHUNKS]
    turn = [[None] * CHUNKS, [None] * CHUNKS]
    for n in (3, 2, 1):
        for h, rows in enumerate(HEADS):
            step = mm(reads[n][rows], stacked(raw, n, 768)[rows], 0, 0)
            m = chain[n, h, 0]
            if n == 3:
                local[h][2], turn[h][2] = step, m.T
            else:
                local[h][n - 1] = mm3(m, local[h][n], 0, 0) + step
                turn[h][n - 1] = mm3(m, turn[h][n], 0, 0)

    y0, pulls = [], []
    for c in range(CHUNKS):
        base = bases[c]
        tk = sb[c, TK]
        if c < 3:
            base = base + cat([mm(tk[s], local[h][c]) for h, s in enumerate(HEADS)])
            tk = cat([mm(tk[s], turn[h][c]) for h, s in enumerate(HEADS)]).astype(BF)
        y0.append(base)
        pulls.append(tk)

    for o in (1, 2, 3):
        pl.when(z < o)(back[o].wait_recv)
    last = comm[1:, 2].reshape(384, 128)
    pulled = mm(pull, last)
    leaving, before = pulled[:128], pulled[128:] + l1.astype(F32)
    grads[2] = jnp.where(first, leaving, before).astype(BF)
    give_d = remote(grads.at[2], grads.at[core], esend.at[9], erecv.at[9], sibling)
    give_d.start()
    grads[core] = jnp.where(first, before, leaving).astype(BF)
    give_s.wait_recv()
    S = []
    for h in (0, 1):
        s = states[h]
        S.append([s] + [mm(prefix[h, n, :, :128], s) + prefix[h, n, :, 128:] for n in range(3)])
    outs = together([
        second_pass(c, [S[0][c], S[1][c]], stacked(raw, c, 768), sf, sb) for c in range(CHUNKS)
    ])
    kept = [rest for _, rest in outs]

    def keep_rows(c, first, value):
        for h, s in enumerate(HEADS):
            gcat[CHUNK * c : CHUNK * c + CHUNK, first + 128 * h : first + 128 * h + 128] = value[
                s
            ].astype(BF)

    for c, (dqr, _) in enumerate(outs):
        keep_rows(c, 0, dqr)
    give_d.wait_recv()

    D, ends = [], [grads[0], grads[1]]
    for h in (0, 1):
        d = ends[h]
        D.append([mm(turn[h][n], d) + local[h][n] for n in range(3)] + [d])

    def share(half, target, n):
        rows = gcat[128 * half : 128 * half + 128, :]
        if half == 0:
            first_row = 576 * target + 288 * n
            return mm(wcat[pl.ds(pl.multiple_of(first_row, 16), 288), :], rows, 1, 1)
        return cat([
            mm(wcat[pl.ds(pl.multiple_of(576 * k + 144 * target, 16), 144), :], rows, 1, 1)
            for k in (2 * n, 2 * n + 1)
        ])

    outs = together([
        third_pass(c, kept[c], y0[c], pulls[c], ends, [D[0][c], D[1][c]], sf, sb) for c in range(CHUNKS)
    ])
    for c, (dkr, dv, _) in enumerate(outs):
        keep_rows(c, 256, dkr)
        keep_rows(c, 512, dv)
    inner = (
        last[:128].astype(F32) + mm(turned[1], last[128:256]) + mm(across, last[256:])
    )
    origin[2] = (comm[0, 2].astype(F32) + mm(turned[0], inner)).astype(BF)
    tell = {
        o: pltpu.make_async_remote_copy(
            src_ref=origin.at[2], dst_ref=origin.at[3], send_sem=esend.at[10 + o],
            recv_sem=erecv.at[10 + o], device_id=zs[o - 1], device_id_type=MESH,
        )
        for o in (1, 2, 3)
    }
    for o in (1, 2, 3):
        pl.when(z == 0)(tell[o].start)

    lines = ((0, y, ys), (1, x, xs))

    def send(half, slot, count, axis, forward):
        block = part.at[half, pl.ds(slot, count)]
        copy = remote(
            block, r1.at[half, pl.ds(slot, count)], rsend.at[half, slot], rrecv.at[half, slot],
            axis[forward],
        )
        copy.start()
        return copy

    def keep(half, slot, value):
        count = value.shape[0] // 144
        part[half, slot : slot + count] = value.astype(BF).reshape(count, 144, 128)

    sums = [[None] * 10, [None] * 10]
    for n, forward in ((0, 0), (1, 2)):
        for half, place, axis in lines:
            keep(half, 2 * n, share(half, (place + 2) % 4, n))
            for slot in (2 * n, 2 * n + 1):
                sums[half][slot] = send(half, slot, 1, axis, forward)
    for n, forward in ((1, 0), (0, 2)):
        for half, place, axis in lines:
            keep(half, 4 + 2 * n, share(half, (place + forward + 1) % 4, n))
            sums[half][4 + n] = send(half, 4 + 2 * n, 2, axis, forward)
    added = {
        (half, n): share(half, (place + forward + 1) % 4, n)
        for n, forward in ((0, 0), (1, 2)) for half, place, _ in lines
    }
    for k in (0, 1):
        for n, forward in ((0, 0), (1, 2)):
            for half, place, axis in lines:
                slot = 2 * n + k
                sums[half][slot].wait_recv()
                value = added[half, n][144 * k : 144 * k + 144] + r1[half, slot].astype(F32)
                keep(half, 8 + slot, value)
                sums[half][6 + slot] = send(half, 8 + slot, 1, axis, forward)
    for c, (dg, dbeta) in enumerate(together([
        last_pass(c, outs[c][2], sf, sb, passed) for c in range(CHUNKS)
    ])):
        t = slice(CHUNK * c, CHUNK * c + CHUNK)
        for h, s in enumerate(HEADS):
            gg[t, 128 * h : 128 * h + 128] = dg[s]
            bg[h : h + 1, t] = jnp.sum(
                jnp.where(diagonal, dbeta[s], 0.0), axis=0, keepdims=True
            )
    stores = [
        pltpu.make_async_copy(gg, gg_ref, wsem.at[0, 2]),
        pltpu.make_async_copy(bg, bg_ref, wsem.at[0, 3]),
    ]
    for store in stores:
        store.start()
    for o in (1, 2, 3):
        pl.when(z == o)(tell[o].wait_recv)
    origin[core] = jnp.where(z == 0, origin[2], origin[3])
    give_o = remote(origin.at[core], origin.at[core], esend.at[10], erecv.at[10], sibling)
    give_o.start()
    finals = [[], []]
    totals = [cat([share(half, place, n) for n in (0, 1)]) for half, place, _ in lines]
    for half, place, axis in ((0, x, xs), (1, y, ys)):
        for copy in sums[half][4:]:
            copy.wait_recv()
        got = [r1[half, 4 * n : 4 * n + 4].astype(F32) for n in (1, 2)]
        total = totals[half].reshape(4, 144, 128) + got[0] + got[1]
        t2f[half] = total
        t2[half] = total.astype(BF)
        for o in (1, 0, 2):
            copy = remote(
                t2.at[half, (place + o + 1) % 4], r2.at[half, o],
                rsend.at[half, 12 + o], rrecv.at[half, 12 + o], axis[o],
            )
            copy.start()
            finals[half].append(copy)
    done = []
    for half, place in ((0, x), (1, y)):
        total = t2f[half, place]
        for copy in finals[half]:
            copy.wait_recv()
        for o in range(3):
            total = total + r2[half, o].astype(F32)
        done.append(total)
    give_o.wait_recv()
    for h in (0, 1):
        sg_ref[h] = origin[h].astype(F32)
    ig_ref[...] = cat(done, 1).astype(BF)
    for store in stores:
        store.wait()

    for o in (1, 2, 3):
        pl.when(z < 4 - o)(both_maps[o].wait_send)
        pl.when(z >= 4 - o)(one_map[o].wait_send)
        pl.when(z >= 4 - o)(back[o].wait_send)
        pl.when(z == 0)(tell[o].wait_send)
    for copy in sent:
        copy.wait_send()


def finish(*refs):
    for n in range(4):
        refs[4 + n][...] = refs[n][...]


def per_device(inputs, output_grad, *others):
    vmem = pl.BlockSpec(memory_space=pltpu.VMEM)
    anywhere = pl.BlockSpec(memory_space=pl.ANY)
    scratch = lambda *shape, dtype=F32: pltpu.VMEM(shape, dtype)
    dma = lambda *shape: pltpu.SemaphoreType.DMA(shape)
    shapes = (
        jax.ShapeDtypeStruct((144, 256), BF),
        jax.ShapeDtypeStruct((256, 256), F32),
        jax.ShapeDtypeStruct((2, 256), F32),
        jax.ShapeDtypeStruct((2, 128, 128), F32),
    )
    results = pl.pallas_call(
        kernel,
        out_shape=shapes,
        in_specs=[anywhere] * 10,
        out_specs=(vmem, anywhere, anywhere, vmem),
        scratch_shapes=[
            scratch(256, 256),
            scratch(2, 256),
            scratch(256, 256),
            scratch(2, 256),
            scratch(2, 128, 128),
            pltpu.SMEM((4,), jnp.int32),
            scratch(2304, 768, dtype=BF),
            scratch(256, 2304, dtype=BF),
            scratch(2304, 256, dtype=BF),
            scratch(2, 2, 4, 4, 144, 128, dtype=BF),
            scratch(256, 1024),
            scratch(256, 768, dtype=BF),
            scratch(CHUNKS, 10, 128, 128),
            scratch(CHUNKS, 10, 128, 128, dtype=BF),
            scratch(CHUNKS, 2, 2, 128, 128),
            scratch(CHUNKS, 8, 128),
            scratch(2, 3, 128, 256),
            scratch(2, 256, 128, dtype=BF),
            scratch(2, 3, 128, 128, dtype=BF),
            scratch(3, 128, 128, dtype=BF),
            scratch(4, 3, 128, 128, dtype=BF),
            scratch(3, 128, 128, dtype=BF),
            scratch(3, 128, 128, dtype=BF),
            scratch(4, 128, 128, dtype=BF),
            scratch(2, 12, 144, 128, dtype=BF),
            scratch(2, 12, 144, 128, dtype=BF),
            scratch(2, 4, 144, 128, dtype=BF),
            scratch(2, 4, 144, 128),
            scratch(2, 3, 144, 128, dtype=BF),
            dma(4, 5), dma(2, 2, 13), dma(2, 2, 13), dma(14), dma(14), dma(2, 15), dma(2, 15),
        ],
        compiler_params=pltpu.CompilerParams(
            collective_id=0, has_side_effects=True, vmem_limit_bytes=60 * 1024 * 1024
        ),
        cost_estimate=pl.CostEstimate(
            flops=3 * 10**9, bytes_accessed=6 * 10**6, transcendentals=3 * 10**5
        ),
    )(inputs.T, output_grad.T, *others)
    results = pl.pallas_call(
        finish,
        out_shape=shapes,
        in_specs=[vmem] * 4,
        out_specs=(vmem,) * 4,
    )(*results)
    return (results[0].T, *results[1:])


def solution(mesh):
    return jax.shard_map(
        per_device,
        mesh=mesh,
        in_specs=(
            P("seq", "head"),
            P("seq", "head"),
            P(None, "head"),
            P(None, "head"),
            P(None, "head"),
            P("head", None),
            P("seq", "head"),
            P("head", "seq"),
            P("head", None, None),
            P(),
        ),
        out_specs=(P("seq", "head"), P("seq", "head"), P("head", "seq"), P("head", None, None)),
        check_vma=False,
    )
```

```python
import jax
import jax.numpy as jnp
from jax import lax
from jax.experimental import pallas as pl
from jax.experimental.pallas import tpu as pltpu
from jax.sharding import PartitionSpec as P

F32, BF = jnp.float32, jnp.bfloat16
MESH = pl.DeviceIdType.MESH
CHUNK = 64
CHUNKS = 4
EPSILON = 1e-06


def mm(a, b, ca=1, cb=0):
    return lax.dot_general(
        a.astype(BF), b.astype(BF), (((ca,), (cb,)), ((), ())), preferred_element_type=F32
    )


def mm3(a, b, ca=1, cb=0):
    (ah, al), (bh, bl) = split(a), split(b)
    return mm(ah, bh, ca, cb) + (mm(ah, bl, ca, cb) + mm(al, bh, ca, cb))


def cat(parts, axis=0):
    return jnp.concatenate(parts, axis=axis)


def split(x):
    hi = x.astype(BF)
    return hi, (x - hi.astype(F32)).astype(BF)


def rowsum(x):
    return jnp.sum(x, axis=1, keepdims=True)


def per_head(rows):
    return cat([jnp.broadcast_to(r, (CHUNK, 128)) for r in rows])


def iotas():
    i = lax.broadcasted_iota(jnp.int32, (128, 128), 0)
    j = lax.broadcasted_iota(jnp.int32, (128, 128), 1)
    return i, j


HEADS = (slice(0, CHUNK), slice(CHUNK, 2 * CHUNK))


def together(steps, hooks=None):
    rounds, hooks = 0, hooks or {}
    results = [None] * len(steps)
    live = list(range(len(steps)))
    while live:
        if rounds in hooks:
            hooks[rounds]()
        rounds += 1
        for n in list(live):
            try:
                next(steps[n])
            except StopIteration as stop:
                results[n] = stop.value
                live.remove(n)
    return results


def invert(n, i, j):
    eye = (i == j).astype(F32)
    d = jnp.where((i >> 4) == (j >> 4), n, 0.0)
    d2 = mm(d, d)
    yield
    p = mm(eye - d, eye + d2)
    d4 = mm(d2, d2)
    yield
    p = mm(p, eye + d4)
    d8 = mm(d4, d4)
    yield
    t = mm(p, eye + d8)
    yield
    off = jnp.where(((i >> 6) == (j >> 6)) & ((i >> 4) != (j >> 4)), n, 0.0)
    e = mm(t, off)
    yield
    e2 = mm(e, e)
    r = t - mm(e, t)
    yield
    t = r + mm(e2, r)
    yield
    return t


(QN, KN, RQ, RK, EO, EG, ES, EX, U_, BETA) = range(10)
(QG, KG, KS, W_, TK, KO, PT, CAUSAL, STRICT, TT) = range(10)


def segments(ds_ref, t0):
    row = t0 + (lax.broadcasted_iota(jnp.int32, (128, 1), 0) & (CHUNK - 1))
    col = t0 + (lax.broadcasted_iota(jnp.int32, (1, 128), 1) & (CHUNK - 1))
    segr, segc = jnp.zeros_like(row), jnp.zeros_like(col)
    for k in range(4):
        start = ds_ref[k]
        here = (start >= t0).astype(jnp.int32)
        segr = segr + (row >= start).astype(jnp.int32) * here
        segc = segc + (col >= start).astype(jnp.int32) * here
    return segr, segc


def key_pass(c, t0, k, v, g, beta, ds_ref, sf, sb, chain, passed):
    i, j = iotas()
    segr, segc = segments(ds_ref, t0)
    same = ((i >> 6) == (j >> 6)) & (segr == segc)
    strict, causal = same & (i > j), same & (i >= j)
    tri = (((i >> 6) == (j >> 6)) & (i >= j)).astype(BF)
    hi, lo = split(g)
    G = mm(cat([tri, tri], 1), cat([hi, lo]))
    rk = lax.rsqrt(rowsum(k * k) + EPSILON)
    kn = k * rk
    yield
    mid = per_head([G[31:32], G[95:96]])
    last = per_head([G[63:64], G[127:128]])
    opening = (segr == 0).astype(F32)
    final = [segr[63:64], segr[127:128]]
    closing = (segr == cat([jnp.broadcast_to(f, (CHUNK, 1)) for f in final])).astype(F32)
    eg, es = jnp.exp(G - mid), jnp.exp(mid - G)
    kg, ks = (kn * eg).astype(BF), (kn * es).astype(BF)
    a = mm(kg, ks, 1, 1)
    yield
    eo = jnp.exp(G) * opening
    ex = jnp.exp(last - G) * closing
    kof = kn * ex
    t = (yield from invert(beta * jnp.where(strict, a, 0.0), i, j)).astype(BF)
    uw = mm(t, cat([beta * v, beta * (kn * eo)], 1))
    yield
    u, w = uw[:, :128], uw[:, 128:]
    for h, s in enumerate(HEADS):
        end = CHUNK * h + CHUNK - 1
        keep = jnp.exp(G[end : end + 1]) * (final[h] == 0).astype(F32)
        passed[c, h : h + 1, :] = keep
        kw = mm3(kof[s], uw[s], 0, 0)
        chain[c, h, 0] = jnp.where(i == j, keep, 0.0) - kw[:, 128:]
        chain[c, h, 1] = kw[:, :128]
    wide = lambda z: jnp.broadcast_to(z, (128, 128))
    for slot, value in (
        (KN, kn), (RK, wide(rk)), (EO, eo), (EG, eg), (ES, es), (EX, ex), (U_, u),
        (BETA, wide(beta)),
    ):
        sf[c, slot] = value
    for slot, value in (
        (KG, kg), (KS, ks), (W_, w), (KO, kof), (TT, t),
        (CAUSAL, causal.astype(F32)), (STRICT, strict.astype(F32)),
    ):
        sb[c, slot] = value.astype(BF)


def query_pass(c, q, sf, sb):
    rq = lax.rsqrt(rowsum(q * q) + EPSILON)
    qn = q * rq
    qg = (qn * sf[c, EG]).astype(BF)
    p = mm(qg, sb[c, KS], 1, 1)
    t = sb[c, TT]
    tk = mm(t, sb[c, KO], 0, 0)
    yield
    p = jnp.where(sb[c, CAUSAL].astype(F32) > 0, p, 0.0).astype(BF)
    qt = qn * sf[c, EO] - mm(p, sb[c, W_])
    pt = mm(p, t)
    yield
    sf[c, QN], sf[c, RQ] = qn, jnp.broadcast_to(rq, (128, 128))
    sb[c, QG], sb[c, PT], sb[c, TK] = qg, pt.astype(BF), tk.astype(BF)
    return qt


def second_pass(c, S, dO, sf, sb):
    S = [s.astype(BF) for s in S]
    dO = dO.astype(BF)
    w = sb[c, W_]
    x = sf[c, U_] - cat([mm(w[s], S[h]) for h, s in enumerate(HEADS)])
    xb = x.astype(BF)
    yield
    dp = jnp.where(sb[c, CAUSAL].astype(F32) > 0, mm(dO, xb, 1, 1), 0.0).astype(BF)
    qs = cat([mm(dO[s], S[h], 1, 1) for h, s in enumerate(HEADS)]) * sf[c, EO]
    yield
    dqg = mm(dp, sb[c, KS])
    dks = mm(dp, sb[c, QG], 0, 0)
    yield
    qn = sf[c, QN]
    dq = qs + dqg * sf[c, EG]
    dqr = sf[c, RQ] * (dq - qn * rowsum(qn * dq))
    gate = qn * qs + sb[c, QG].astype(F32) * dqg
    return dqr, (S, x, xb, gate, dks)


def third_pass(c, kept, y0, tk, d, D, sf, sb):
    f = lambda slot: sf[c, slot]
    b = lambda slot: sb[c, slot]
    S, x, xb, gate, dks = kept
    beta, eo = f(BETA), f(EO)
    y = y0 + cat([mm(tk[s], d[h]) for h, s in enumerate(HEADS)])
    D = [z.astype(BF) for z in D]
    yb = y.astype(BF)
    yield
    da = jnp.where(b(STRICT).astype(F32) > 0, -beta * mm(yb, xb, 1, 1), 0.0).astype(BF)
    ke = cat([mm(yb[s], S[h], 1, 1) for h, s in enumerate(HEADS)]) * (-beta * eo)
    dko = cat([mm(xb[s], D[h], 1, 1) for h, s in enumerate(HEADS)])
    yield
    dkg = mm(da, b(KS))
    dks = dks + mm(da, b(KG), 0, 0)
    yield
    kn = f(KN)
    dk = ke + dkg * f(EG) + dks * f(ES) + dko * f(EX)
    dkr = f(RK) * (dk - kn * rowsum(kn * dk))
    return dkr, beta * y, (S, D, x, y, gate, ke, dko, dkg, dks)


def last_pass(c, kept, sf, sb, passed):
    i, j = iotas()
    S, D, x, y, gate, ke, dko, dkg, dks = kept
    dbeta = rowsum(y * x) / sf[c, BETA][:, :1]
    kd = sb[c, KO].astype(F32) * dko
    dG = (
        gate + sb[c, KG].astype(F32) * dkg - sb[c, KS].astype(F32) * dks + sf[c, KN] * ke - kd
    )
    ends = []
    for h, s in enumerate(HEADS):
        hi, lo = split(S[h].astype(F32) * D[h].astype(F32))
        through = mm(jnp.ones((8, 256), BF), cat([hi, lo], 1), 1, 1)[0:1]
        ends.append(jnp.sum(kd[s], axis=0, keepdims=True) + passed[c, h : h + 1, :] * through)
    hi, lo = split(dG)
    upper = (((i >> 6) == (j >> 6)) & (i <= j)).astype(BF)
    yield
    dg = mm(cat([upper, upper], 1), cat([hi, lo])) + per_head(ends)
    yield
    return dg, dbeta


def kernel(
    x_ref, og_ref, wq_ref, wk_ref, wv_ref, wo_ref, gate_ref, beta_ref, init_ref, ds_ref,
    ig_ref, gg_ref, bg_ref, sg_ref,
    gg, bg, gate, beta_in, start, ds, wcat, wo, wot, xg, raw, gcat, sf, sb, chain, passed, prefix, qe,
    own, heard, comm, states, grads, origin, part, r1, t2, t2f, r2,
    wsem, gsend, grecv, esend, erecv, rsend, rrecv,
):
    seq, head = lax.axis_index("seq"), lax.axis_index("head")
    y, x = head // 4, head % 4
    z, core = seq // 2, seq % 2
    xs = [{"head": y * 4 + (x + o) % 4} for o in (1, 2, 3)]
    ys = [{"head": ((y + o) % 4) * 4 + x} for o in (1, 2, 3)]
    zs = [{"seq": ((z + o) % 4) * 2 + core} for o in (1, 2, 3)]
    sibling = {"seq": z * 2 + (1 - core)}

    loads = [
        pltpu.make_async_copy(
            ref.at[:, 128 * half : 128 * half + 128], xg.at[item, half, y, x], wsem.at[item, half]
        )
        for item, ref in enumerate((x_ref, og_ref))
        for half in (0, 1)
    ]
    loads += [
        pltpu.make_async_copy(ref, wcat.at[:, 256 * n : 256 * n + 256], wsem.at[2, n])
        for n, ref in enumerate((wq_ref, wk_ref, wv_ref))
    ]
    loads += [
        pltpu.make_async_copy(src, dst, wsem.at[3, n])
        for n, (src, dst) in enumerate((
            (wo_ref, wo), (gate_ref, gate), (beta_ref, beta_in), (init_ref, start), (ds_ref, ds)
        ))
    ]
    comm[...] = jnp.zeros_like(comm)
    barrier = pltpu.get_barrier_semaphore()
    partners = xs + ys + zs + [sibling]
    for device in partners:
        pl.semaphore_signal(barrier, inc=1, device_id=device, device_id_type=MESH)

    for load in loads:
        load.start()
    pl.semaphore_wait(barrier, len(partners))

    sent = []

    def remote(src, dst, ssem, rsem, device):
        copy = pltpu.make_async_remote_copy(
            src_ref=src, dst_ref=dst, send_sem=ssem, recv_sem=rsem,
            device_id=device, device_id_type=MESH,
        )
        sent.append(copy)
        return copy

    def near(item, half):
        block = xg.at[item, half, y, x]
        source = (x_ref, og_ref)[item].at[:, 128 * half : 128 * half + 128]
        axis = xs if half == 0 else ys
        return [
            remote(source, block, gsend.at[item, half, o], grecv.at[item, half, o], axis[o])
            for o in (1, 0, 2)
        ]

    def piece(item, half, group, first, count):
        taken = pl.ds(first, count)
        return xg.at[item, 0, group, taken] if half == 0 else xg.at[item, 1, taken, group]

    def far(item, half):
        place, axis = (y, ys) if half == 0 else (x, xs)
        pieces = ((0, 0, 1), (2, 2, 1), (0, 1, 1), (2, 3, 1), (0, 2, 2), (2, 0, 2))
        if item == 1:
            pieces = ((0, 0, 4), (2, 0, 4), (1, 0, 4))
        copies = []
        for n, (forward, first, count) in enumerate(pieces):
            block = piece(item, half, place, first, count)
            copies.append(remote(
                block, block, gsend.at[item, half, 3 + n], grecv.at[item, half, 3 + n],
                axis[forward],
            ))
        return copies

    def hand_on(item, half):
        place, axis = (y, ys) if half == 0 else (x, xs)
        pieces = ((0, 0, 1), (2, 2, 1), (0, 1, 1), (2, 3, 1))
        copies = []
        for n, (forward, first, count) in enumerate(pieces):
            group = (place + 3) % 4 if forward == 0 else (place + 1) % 4
            block = piece(item, half, group, first, count)
            copies.append(remote(
                block, block, gsend.at[item, half, 9 + n], grecv.at[item, half, 9 + n],
                axis[forward],
            ))
        return copies

    parts = [(item, half) for item in (0, 1) for half in (0, 1)]
    nears = {part: near(*part) for part in parts}
    fars = {part: far(*part) for part in parts}
    relays = {part: hand_on(*part) for part in parts[:2]}

    def begin(item):
        for o in range(3):
            for half in (0, 1):
                nears[item, half][o].start()

    def widen(item):
        for half in (0, 1):
            for copy in nears[item, half]:
                copy.wait_recv()
        for n in range(len(fars[item, 0])):
            for half in (0, 1):
                fars[item, half][n].start()

    def pass_on(item):
        for n in range(len(relays[item, 0])):
            for half in (0, 1):
                fars[item, half][n].wait_recv()
                relays[item, half][n].start()

    def project(item, weight, taken, columns, groups):
        for half, place in ((0, y), (1, x)):
            rows = slice(128 * half, 128 * half + 128)
            for o in groups:
                group = (place + o) % 4
                if half == 0:
                    block = xg[item, 0, group].reshape(576, 128)
                    matrix = weight[pl.ds(pl.multiple_of(576 * group, 16), 576), taken]
                else:
                    block = cat([xg[item, 1, k, group] for k in range(4)])
                    matrix = cat([
                        weight[pl.ds(pl.multiple_of(576 * k + 144 * group, 16), 144), taken]
                        for k in range(4)
                    ])
                value = mm(block, matrix, 0, 0)
                if o == 0:
                    raw[rows, columns] = value
                else:
                    raw[rows, columns] += value

    begin(0)
    begin(1)
    for load in loads[:4]:
        load.wait()
    widen(0)
    for load in loads[4:]:
        load.wait()
    first_rows = (0, wcat, slice(0, 768), slice(0, 768))
    second_rows = (1, wot, slice(0, 256), slice(768, 1024))
    project(*first_rows, (0,))
    pass_on(0)
    widen(1)
    for n in range(18):
        wot[128 * n : 128 * n + 128, :] = wo[:, 128 * n : 128 * n + 128].T
    for half in (0, 1):
        for copy in fars[0, half][4:]:
            copy.wait_recv()
    project(*first_rows, (1, 3))
    project(*second_rows, (0,))
    for half in (0, 1):
        for copy in relays[0, half]:
            copy.wait_recv()
    project(0, wcat, slice(256, 768), slice(256, 768), (2,))

    def stacked(ref, c, first):
        t = slice(CHUNK * c, CHUNK * c + CHUNK)
        return cat([ref[t, first : first + 128], ref[t, first + 128 : first + 256]])

    diagonal = (
        lax.broadcasted_iota(jnp.int32, (CHUNK, CHUNK), 0)
        == lax.broadcasted_iota(jnp.int32, (CHUNK, CHUNK), 1)
    )
    betas = [
        cat([
            rowsum(jnp.where(diagonal, beta_in[h : h + 1, CHUNK * c : CHUNK * c + CHUNK], 0.0))
            for h in (0, 1)
        ])
        for c in range(CHUNKS)
    ]
    together([
        key_pass(
            c, seq * 256 + CHUNK * c, stacked(raw, c, 256), stacked(raw, c, 512),
            stacked(gate, c, 0), betas[c], ds, sf, sb, chain, passed,
        )
        for c in range(CHUNKS)
    ])

    def compose(n, m, v, h):
        step = mm3(chain[n, h, 0], cat([m, v], 1))
        return step[:, :128], step[:, 128:] + chain[n, h, 1]

    low = [compose(1, chain[0, h, 0], chain[0, h, 1], h) for h in (0, 1)]
    high = [compose(3, chain[2, h, 0], chain[2, h, 1], h) for h in (0, 1)]
    third = [compose(2, *low[h], h) for h in (0, 1)]
    for h in (0, 1):
        step = mm3(high[h][0], cat(low[h], 1))
        own[h, 0] = step[:, :128].astype(BF)
        own[h, 1] = (step[:, 128:] + high[h][1]).astype(BF)
    swap = remote(
        own.at[1 - core, pl.ds(0, 2)], heard.at[pl.ds(0, 2)], esend.at[0], erecv.at[0], sibling
    )
    swap.start()
    project(0, wcat, slice(0, 256), slice(0, 256), (2,))
    reads = together([query_pass(c, stacked(raw, c, 0), sf, sb) for c in range(CHUNKS)])
    for h, rows in enumerate(HEADS):
        for n, pair in ((0, (chain[0, h, 0], chain[0, h, 1])), (1, low[h]),
                        (2, third[h])):
            prefix[h, n, :, :128], prefix[h, n, :, 128:] = pair
        qe[h, 0:CHUNK] = reads[0][rows].astype(BF)
        for n in (1, 2, 3):
            qe[h, CHUNK * n : CHUNK * n + CHUNK] = mm(
                reads[n][rows], prefix[h, n - 1, :, :128]
            ).astype(BF)
    for half in (0, 1):
        for copy in fars[1, half][:2]:
            copy.wait_recv()
    project(*second_rows, (1, 3))
    swap.wait_recv()
    first = core == 0
    m0, b0 = [jnp.where(first, own[core, n], heard[n]) for n in (0, 1)]
    m1, b1 = [jnp.where(first, heard[n], own[core, n]) for n in (0, 1)]
    m0t, m1t = [m.astype(F32).T.astype(BF) for m in (m0, m1)]
    both = mm(m1, cat([m0, b0], 1))
    comm[z, 0] = both[:, :128].astype(BF)
    comm[z, 1] = (both[:, 128:] + b1.astype(F32)).astype(BF)
    def line(first, count, number, o):
        block = comm.at[z, pl.ds(first, count)]
        return pltpu.make_async_remote_copy(
            src_ref=block, dst_ref=block, send_sem=esend.at[number], recv_sem=erecv.at[number],
            device_id=zs[o - 1], device_id_type=MESH,
        )

    both_maps = {o: line(0, 2, o, o) for o in (1, 2, 3)}
    one_map = {o: line(0, 1, o, o) for o in (1, 2, 3)}
    back = {o: line(2, 1, 5 + o, o) for o in (1, 2, 3)}
    for o in (2, 1, 3):
        pl.when(z < 4 - o)(both_maps[o].start)
        pl.when(z >= 4 - o)(one_map[o].start)

    for half in (0, 1):
        fars[1, half][2].wait_recv()
    project(*second_rows, (2,))

    for h in (0, 1):
        dO = raw[:, 768 + 128 * h : 896 + 128 * h]
        own[h, 2] = mm(qe[h], dO, 0, 0).astype(BF)
    swap_l = remote(own.at[1 - core, 2], heard.at[2], esend.at[4], erecv.at[4], sibling)
    swap_l.start()

    bases = [mm(sb[c, PT], stacked(raw, c, 768), 0, 0) for c in range(CHUNKS)]
    swap_l.wait_recv()
    l0 = jnp.where(first, own[core, 2], heard[2])
    l1 = jnp.where(first, heard[2], own[core, 2])
    comm[z, 2] = (l0.astype(F32) + mm(m0t, l1)).astype(BF)
    for o in (2, 1, 3):
        pl.when(z >= 4 - o)(back[o].start)

    for o in (1, 2, 3):
        pl.when(z >= o)(both_maps[o].wait_recv)
        pl.when(z < o)(one_map[o].wait_recv)
    state, entering = start[core], start[core]
    for n in range(3):
        state = mm(comm[n, 0], state) + comm[n, 1].astype(F32)
        entering = jnp.where(z == n + 1, state, entering)
    after = mm(m0, entering) + b0.astype(F32)
    states[2] = jnp.where(first, after, entering).astype(BF)
    give_s = remote(states.at[2], states.at[core], esend.at[5], erecv.at[5], sibling)
    give_s.start()
    states[core] = jnp.where(first, entering, after).astype(BF)

    turned = [comm[n, 0].astype(F32).T.astype(BF) for n in range(3)]
    across = mm(turned[1], turned[2])
    eye = (iotas()[0] == iotas()[1]).astype(F32)
    none = jnp.zeros_like(eye)
    pull = cat([
        jnp.where(z == 0, eye, none),
        jnp.where(z == 1, eye, jnp.where(z == 0, turned[1].astype(F32), none)),
        jnp.where(
            z == 2, eye,
            jnp.where(z == 1, turned[2].astype(F32), jnp.where(z == 0, across, none)),
        ),
    ], 1).astype(BF)
    pull = cat([pull, mm(m1t, pull).astype(BF)])

    suffix = [[None] * 3, [None] * 3]
    for n in (3, 2, 1):
        for h, rows in enumerate(HEADS):
            step = mm(reads[n][rows], stacked(raw, n, 768)[rows], 0, 0)
            m = chain[n, h, 0].T
            if n == 3:
                suffix[h][2] = cat([m, step], 1)
            else:
                value = mm(m, suffix[h][n])
                suffix[h][n - 1] = cat([value[:, :128], value[:, 128:] + step], 1)

    y0, pulls = [], []
    for c in range(CHUNKS):
        base = bases[c]
        tk = sb[c, TK]
        if c < 3:
            value = cat([mm(tk[s], suffix[h][c]) for h, s in enumerate(HEADS)])
            base = base + value[:, 128:]
            tk = value[:, :128].astype(BF)
        y0.append(base)
        pulls.append(tk)

    for o in (1, 2, 3):
        pl.when(z < o)(back[o].wait_recv)
    last = comm[1:, 2].reshape(384, 128)
    pulled = mm(pull, last)
    leaving, before = pulled[:128], pulled[128:] + l1.astype(F32)
    grads[2] = jnp.where(first, leaving, before).astype(BF)
    give_d = remote(grads.at[2], grads.at[core], esend.at[9], erecv.at[9], sibling)
    give_d.start()
    grads[core] = jnp.where(first, before, leaving).astype(BF)
    give_s.wait_recv()
    S = []
    for h in (0, 1):
        s = states[h]
        value = mm(prefix[h, :, :, :128].reshape(384, 128), s).reshape(3, 128, 128)
        S.append([s] + [value[n] + prefix[h, n, :, 128:] for n in range(3)])
    outs = together([
        second_pass(c, [S[0][c], S[1][c]], stacked(raw, c, 768), sf, sb) for c in range(CHUNKS)
    ])
    kept = [rest for _, rest in outs]

    def keep_rows(c, first, value):
        for h, s in enumerate(HEADS):
            gcat[CHUNK * c : CHUNK * c + CHUNK, first + 128 * h : first + 128 * h + 128] = value[
                s
            ].astype(BF)

    for c, (dqr, _) in enumerate(outs):
        keep_rows(c, 0, dqr)
    give_d.wait_recv()

    D, ends = [], [grads[0], grads[1]]
    for h in (0, 1):
        d = ends[h]
        value = mm(cat([suffix[h][n][:, :128] for n in range(3)]), d).reshape(3, 128, 128)
        D.append([value[n] + suffix[h][n][:, 128:] for n in range(3)] + [d])

    def share(half, target, n):
        rows = gcat[128 * half : 128 * half + 128, :]
        if half == 0:
            first_row = 576 * target + 288 * n
            return mm(wcat[pl.ds(pl.multiple_of(first_row, 16), 288), :], rows, 1, 1)
        return cat([
            mm(wcat[pl.ds(pl.multiple_of(576 * k + 144 * target, 16), 144), :], rows, 1, 1)
            for k in (2 * n, 2 * n + 1)
        ])

    outs = together([
        third_pass(c, kept[c], y0[c], pulls[c], ends, [D[0][c], D[1][c]], sf, sb) for c in range(CHUNKS)
    ])
    for c, (dkr, dv, _) in enumerate(outs):
        keep_rows(c, 256, dkr)
        keep_rows(c, 512, dv)
    inner = (
        last[:128].astype(F32) + mm(turned[1], last[128:256]) + mm(across, last[256:])
    )
    origin[2] = (comm[0, 2].astype(F32) + mm(turned[0], inner)).astype(BF)
    tell = {
        o: pltpu.make_async_remote_copy(
            src_ref=origin.at[2], dst_ref=origin.at[3], send_sem=esend.at[10 + o],
            recv_sem=erecv.at[10 + o], device_id=zs[o - 1], device_id_type=MESH,
        )
        for o in (1, 2, 3)
    }
    for o in (1, 2, 3):
        pl.when(z == 0)(tell[o].start)

    lines = ((0, y, ys), (1, x, xs))

    def send(half, slot, count, axis, forward):
        block = part.at[half, pl.ds(slot, count)]
        copy = remote(
            block, r1.at[half, pl.ds(slot, count)], rsend.at[half, slot], rrecv.at[half, slot],
            axis[forward],
        )
        copy.start()
        return copy

    def keep(half, slot, value):
        count = value.shape[0] // 144
        part[half, slot : slot + count] = value.astype(BF).reshape(count, 144, 128)

    sums = [[None] * 10, [None] * 10]
    for n, forward in ((0, 0), (1, 2)):
        for half, place, axis in lines:
            keep(half, 2 * n, share(half, (place + 2) % 4, n))
            for slot in (2 * n, 2 * n + 1):
                sums[half][slot] = send(half, slot, 1, axis, forward)
    for n, forward in ((1, 0), (0, 2)):
        for half, place, axis in lines:
            keep(half, 4 + 2 * n, share(half, (place + forward + 1) % 4, n))
            sums[half][4 + n] = send(half, 4 + 2 * n, 2, axis, forward)
    added = {
        (half, n): share(half, (place + forward + 1) % 4, n)
        for n, forward in ((0, 0), (1, 2)) for half, place, _ in lines
    }
    for k in (0, 1):
        for n, forward in ((0, 0), (1, 2)):
            for half, place, axis in lines:
                slot = 2 * n + k
                sums[half][slot].wait_recv()
                value = added[half, n][144 * k : 144 * k + 144] + r1[half, slot].astype(F32)
                keep(half, 8 + slot, value)
                sums[half][6 + slot] = send(half, 8 + slot, 1, axis, forward)
    for c, (dg, dbeta) in enumerate(together([
        last_pass(c, outs[c][2], sf, sb, passed) for c in range(CHUNKS)
    ])):
        t = slice(CHUNK * c, CHUNK * c + CHUNK)
        for h, s in enumerate(HEADS):
            gg[t, 128 * h : 128 * h + 128] = dg[s]
            bg[h : h + 1, t] = jnp.sum(
                jnp.where(diagonal, dbeta[s], 0.0), axis=0, keepdims=True
            )
    stores = [
        pltpu.make_async_copy(gg, gg_ref, wsem.at[0, 2]),
        pltpu.make_async_copy(bg, bg_ref, wsem.at[0, 3]),
    ]
    for store in stores:
        store.start()
    for o in (1, 2, 3):
        pl.when(z == o)(tell[o].wait_recv)
    origin[core] = jnp.where(z == 0, origin[2], origin[3])
    give_o = remote(origin.at[core], origin.at[core], esend.at[10], erecv.at[10], sibling)
    give_o.start()
    finals = [[], []]
    totals = [cat([share(half, place, n) for n in (0, 1)]) for half, place, _ in lines]
    for half, place, axis in ((0, x, xs), (1, y, ys)):
        for copy in sums[half][4:]:
            copy.wait_recv()
        got = [r1[half, 4 * n : 4 * n + 4].astype(F32) for n in (1, 2)]
        total = totals[half].reshape(4, 144, 128) + got[0] + got[1]
        t2f[half] = total
        t2[half] = total.astype(BF)
        for o in (1, 0, 2):
            copy = remote(
                t2.at[half, (place + o + 1) % 4], r2.at[half, o],
                rsend.at[half, 12 + o], rrecv.at[half, 12 + o], axis[o],
            )
            copy.start()
            finals[half].append(copy)
    done = []
    for half, place in ((0, x), (1, y)):
        total = t2f[half, place]
        for copy in finals[half]:
            copy.wait_recv()
        for o in range(3):
            total = total + r2[half, o].astype(F32)
        done.append(total)
    give_o.wait_recv()
    for h in (0, 1):
        sg_ref[h] = origin[h].astype(F32)
    ig_ref[...] = cat(done, 1).astype(BF)
    for store in stores:
        store.wait()

    for o in (1, 2, 3):
        pl.when(z < 4 - o)(both_maps[o].wait_send)
        pl.when(z >= 4 - o)(one_map[o].wait_send)
        pl.when(z >= 4 - o)(back[o].wait_send)
        pl.when(z == 0)(tell[o].wait_send)
    for copy in sent:
        copy.wait_send()


def finish(*refs):
    for n in range(4):
        refs[4 + n][...] = refs[n][...]


def per_device(inputs, output_grad, *others):
    vmem = pl.BlockSpec(memory_space=pltpu.VMEM)
    anywhere = pl.BlockSpec(memory_space=pl.ANY)
    scratch = lambda *shape, dtype=F32: pltpu.VMEM(shape, dtype)
    dma = lambda *shape: pltpu.SemaphoreType.DMA(shape)
    shapes = (
        jax.ShapeDtypeStruct((144, 256), BF),
        jax.ShapeDtypeStruct((256, 256), F32),
        jax.ShapeDtypeStruct((2, 256), F32),
        jax.ShapeDtypeStruct((2, 128, 128), F32),
    )
    results = pl.pallas_call(
        kernel,
        out_shape=shapes,
        in_specs=[anywhere] * 10,
        out_specs=(vmem, anywhere, anywhere, vmem),
        scratch_shapes=[
            scratch(256, 256),
            scratch(2, 256),
            scratch(256, 256),
            scratch(2, 256),
            scratch(2, 128, 128),
            pltpu.SMEM((4,), jnp.int32),
            scratch(2304, 768, dtype=BF),
            scratch(256, 2304, dtype=BF),
            scratch(2304, 256, dtype=BF),
            scratch(2, 2, 4, 4, 144, 128, dtype=BF),
            scratch(256, 1024),
            scratch(256, 768, dtype=BF),
            scratch(CHUNKS, 10, 128, 128),
            scratch(CHUNKS, 10, 128, 128, dtype=BF),
            scratch(CHUNKS, 2, 2, 128, 128),
            scratch(CHUNKS, 8, 128),
            scratch(2, 3, 128, 256),
            scratch(2, 256, 128, dtype=BF),
            scratch(2, 3, 128, 128, dtype=BF),
            scratch(3, 128, 128, dtype=BF),
            scratch(4, 3, 128, 128, dtype=BF),
            scratch(3, 128, 128, dtype=BF),
            scratch(3, 128, 128, dtype=BF),
            scratch(4, 128, 128, dtype=BF),
            scratch(2, 12, 144, 128, dtype=BF),
            scratch(2, 12, 144, 128, dtype=BF),
            scratch(2, 4, 144, 128, dtype=BF),
            scratch(2, 4, 144, 128),
            scratch(2, 3, 144, 128, dtype=BF),
            dma(4, 5), dma(2, 2, 13), dma(2, 2, 13), dma(14), dma(14), dma(2, 15), dma(2, 15),
        ],
        compiler_params=pltpu.CompilerParams(
            collective_id=0, has_side_effects=True, vmem_limit_bytes=60 * 1024 * 1024
        ),
        cost_estimate=pl.CostEstimate(
            flops=3 * 10**9, bytes_accessed=6 * 10**6, transcendentals=3 * 10**5
        ),
    )(inputs.T, output_grad.T, *others)
    results = pl.pallas_call(
        finish,
        out_shape=shapes,
        in_specs=[vmem] * 4,
        out_specs=(vmem,) * 4,
    )(*results)
    return (results[0].T, *results[1:])


def solution(mesh):
    return jax.shard_map(
        per_device,
        mesh=mesh,
        in_specs=(
            P("seq", "head"),
            P("seq", "head"),
            P(None, "head"),
            P(None, "head"),
            P(None, "head"),
            P("head", None),
            P("seq", "head"),
            P("head", "seq"),
            P("head", None, None),
            P(),
        ),
        out_specs=(P("seq", "head"), P("seq", "head"), P("head", "seq"), P("head", None, None)),
        check_vma=False,
    )
```

```python
import jax
import jax.numpy as jnp
from jax import lax
from jax.experimental import pallas as pl
from jax.experimental.pallas import tpu as pltpu
from jax.sharding import PartitionSpec as P

F32, BF = jnp.float32, jnp.bfloat16
MESH = pl.DeviceIdType.MESH
CHUNK = 64
CHUNKS = 4
EPSILON = 1e-06


def mm(a, b, ca=1, cb=0):
    return lax.dot_general(
        a.astype(BF), b.astype(BF), (((ca,), (cb,)), ((), ())), preferred_element_type=F32
    )


def mm3(a, b, ca=1, cb=0):
    (ah, al), (bh, bl) = split(a), split(b)
    return mm(ah, bh, ca, cb) + (mm(ah, bl, ca, cb) + mm(al, bh, ca, cb))


def cat(parts, axis=0):
    return jnp.concatenate(parts, axis=axis)


def split(x):
    hi = x.astype(BF)
    return hi, (x - hi.astype(F32)).astype(BF)


def rowsum(x):
    return jnp.sum(x, axis=1, keepdims=True)


def per_head(rows):
    return cat([jnp.broadcast_to(r, (CHUNK, 128)) for r in rows])


def iotas():
    i = lax.broadcasted_iota(jnp.int32, (128, 128), 0)
    j = lax.broadcasted_iota(jnp.int32, (128, 128), 1)
    return i, j


HEADS = (slice(0, CHUNK), slice(CHUNK, 2 * CHUNK))


def together(steps, hooks=None):
    rounds, hooks = 0, hooks or {}
    results = [None] * len(steps)
    live = list(range(len(steps)))
    while live:
        if rounds in hooks:
            hooks[rounds]()
        rounds += 1
        for n in list(live):
            try:
                next(steps[n])
            except StopIteration as stop:
                results[n] = stop.value
                live.remove(n)
    return results


def invert(n, i, j):
    eye = (i == j).astype(F32)
    d = jnp.where((i >> 4) == (j >> 4), n, 0.0)
    d2 = mm(d, d)
    yield
    p = mm(eye - d, eye + d2)
    d4 = mm(d2, d2)
    yield
    p = mm(p, eye + d4)
    d8 = mm(d4, d4)
    yield
    t = mm(p, eye + d8)
    yield
    off = jnp.where(((i >> 6) == (j >> 6)) & ((i >> 4) != (j >> 4)), n, 0.0)
    e = mm(t, off)
    yield
    e2 = mm(e, e)
    r = t - mm(e, t)
    yield
    t = r + mm(e2, r)
    yield
    return t


(QN, KN, RQ, RK, EO, EG, ES, EX, U_, BETA) = range(10)
(QG, KG, KS, W_, TK, KO, PT, CAUSAL, STRICT, TT) = range(10)


def segments(ds_ref, t0):
    row = t0 + (lax.broadcasted_iota(jnp.int32, (128, 1), 0) & (CHUNK - 1))
    col = t0 + (lax.broadcasted_iota(jnp.int32, (1, 128), 1) & (CHUNK - 1))
    segr, segc = jnp.zeros_like(row), jnp.zeros_like(col)
    for k in range(4):
        start = ds_ref[k]
        here = (start >= t0).astype(jnp.int32)
        segr = segr + (row >= start).astype(jnp.int32) * here
        segc = segc + (col >= start).astype(jnp.int32) * here
    return segr, segc


def key_pass(c, t0, k, v, g, beta, ds_ref, sf, sb, chain, passed):
    i, j = iotas()
    segr, segc = segments(ds_ref, t0)
    same = ((i >> 6) == (j >> 6)) & (segr == segc)
    strict, causal = same & (i > j), same & (i >= j)
    tri = (((i >> 6) == (j >> 6)) & (i >= j)).astype(BF)
    hi, lo = split(g)
    G = mm(cat([tri, tri], 1), cat([hi, lo]))
    rk = lax.rsqrt(rowsum(k * k) + EPSILON)
    kn = k * rk
    yield
    mid = per_head([G[31:32], G[95:96]])
    last = per_head([G[63:64], G[127:128]])
    opening = (segr == 0).astype(F32)
    final = [segr[63:64], segr[127:128]]
    closing = (segr == cat([jnp.broadcast_to(f, (CHUNK, 1)) for f in final])).astype(F32)
    eg, es = jnp.exp(G - mid), jnp.exp(mid - G)
    kg, ks = (kn * eg).astype(BF), (kn * es).astype(BF)
    a = mm(kg, ks, 1, 1)
    yield
    eo = jnp.exp(G) * opening
    ex = jnp.exp(last - G) * closing
    kof = kn * ex
    t = (yield from invert(beta * jnp.where(strict, a, 0.0), i, j)).astype(BF)
    uw = mm(t, cat([beta * v, beta * (kn * eo)], 1))
    yield
    u, w = uw[:, :128], uw[:, 128:]
    for h, s in enumerate(HEADS):
        end = CHUNK * h + CHUNK - 1
        keep = jnp.exp(G[end : end + 1]) * (final[h] == 0).astype(F32)
        passed[c, h : h + 1, :] = keep
        kw = mm3(kof[s], uw[s], 0, 0)
        chain[c, h, 0] = jnp.where(i == j, keep, 0.0) - kw[:, 128:]
        chain[c, h, 1] = kw[:, :128]
    wide = lambda z: jnp.broadcast_to(z, (128, 128))
    for slot, value in (
        (KN, kn), (RK, wide(rk)), (EO, eo), (EG, eg), (ES, es), (EX, ex), (U_, u),
        (BETA, wide(beta)),
    ):
        sf[c, slot] = value
    for slot, value in (
        (KG, kg), (KS, ks), (W_, w), (KO, kof), (TT, t),
        (CAUSAL, causal.astype(F32)), (STRICT, strict.astype(F32)),
    ):
        sb[c, slot] = value.astype(BF)


def query_pass(c, q, sf, sb):
    rq = lax.rsqrt(rowsum(q * q) + EPSILON)
    qn = q * rq
    qg = (qn * sf[c, EG]).astype(BF)
    p = mm(qg, sb[c, KS], 1, 1)
    t = sb[c, TT]
    tk = mm(t, sb[c, KO], 0, 0)
    yield
    p = jnp.where(sb[c, CAUSAL].astype(F32) > 0, p, 0.0).astype(BF)
    qt = qn * sf[c, EO] - mm(p, sb[c, W_])
    pt = mm(p, t)
    yield
    sf[c, QN], sf[c, RQ] = qn, jnp.broadcast_to(rq, (128, 128))
    sb[c, QG], sb[c, PT], sb[c, TK] = qg, pt.astype(BF), tk.astype(BF)
    return qt


def second_pass(c, S, dO, sf, sb):
    S = [s.astype(BF) for s in S]
    dO = dO.astype(BF)
    w = sb[c, W_]
    x = sf[c, U_] - cat([mm(w[s], S[h]) for h, s in enumerate(HEADS)])
    xb = x.astype(BF)
    yield
    dp = jnp.where(sb[c, CAUSAL].astype(F32) > 0, mm(dO, xb, 1, 1), 0.0).astype(BF)
    qs = cat([mm(dO[s], S[h], 1, 1) for h, s in enumerate(HEADS)]) * sf[c, EO]
    yield
    dqg = mm(dp, sb[c, KS])
    dks = mm(dp, sb[c, QG], 0, 0)
    yield
    qn = sf[c, QN]
    dq = qs + dqg * sf[c, EG]
    dqr = sf[c, RQ] * (dq - qn * rowsum(qn * dq))
    gate = qn * qs + sb[c, QG].astype(F32) * dqg
    return dqr, (S, x, xb, gate, dks)


def third_pass(c, kept, y0, tk, d, D, sf, sb):
    f = lambda slot: sf[c, slot]
    b = lambda slot: sb[c, slot]
    S, x, xb, gate, dks = kept
    beta, eo = f(BETA), f(EO)
    y = y0 + cat([mm(tk[s], d[h]) for h, s in enumerate(HEADS)])
    D = [z.astype(BF) for z in D]
    yb = y.astype(BF)
    yield
    da = jnp.where(b(STRICT).astype(F32) > 0, -beta * mm(yb, xb, 1, 1), 0.0).astype(BF)
    ke = cat([mm(yb[s], S[h], 1, 1) for h, s in enumerate(HEADS)]) * (-beta * eo)
    dko = cat([mm(xb[s], D[h], 1, 1) for h, s in enumerate(HEADS)])
    yield
    dkg = mm(da, b(KS))
    dks = dks + mm(da, b(KG), 0, 0)
    yield
    kn = f(KN)
    dk = ke + dkg * f(EG) + dks * f(ES) + dko * f(EX)
    dkr = f(RK) * (dk - kn * rowsum(kn * dk))
    return dkr, beta * y, (S, D, x, y, gate, ke, dko, dkg, dks)


def last_pass(c, kept, sf, sb, passed):
    i, j = iotas()
    S, D, x, y, gate, ke, dko, dkg, dks = kept
    dbeta = rowsum(y * x) / sf[c, BETA][:, :1]
    kd = sb[c, KO].astype(F32) * dko
    dG = (
        gate + sb[c, KG].astype(F32) * dkg - sb[c, KS].astype(F32) * dks + sf[c, KN] * ke - kd
    )
    ends = []
    for h, s in enumerate(HEADS):
        hi, lo = split(S[h].astype(F32) * D[h].astype(F32))
        through = mm(jnp.ones((8, 256), BF), cat([hi, lo], 1), 1, 1)[0:1]
        ends.append(jnp.sum(kd[s], axis=0, keepdims=True) + passed[c, h : h + 1, :] * through)
    hi, lo = split(dG)
    upper = (((i >> 6) == (j >> 6)) & (i <= j)).astype(BF)
    yield
    dg = mm(cat([upper, upper], 1), cat([hi, lo])) + per_head(ends)
    yield
    return dg, dbeta


def kernel(
    x_ref, og_ref, wq_ref, wk_ref, wv_ref, wo_ref, gate_ref, beta_ref, init_ref, ds_ref,
    ig_ref, gg_ref, bg_ref, sg_ref,
    gg, bg, gate, beta_in, start, ds, wcat, wo, wot, xg, raw, gcat, sf, sb, chain, passed, prefix, qe,
    own, heard, comm, states, grads, origin, part, r1, t2, t2f, r2,
    wsem, gsend, grecv, esend, erecv, rsend, rrecv,
):
    seq, head = lax.axis_index("seq"), lax.axis_index("head")
    y, x = head // 4, head % 4
    z, core = seq // 2, seq % 2
    xs = [{"head": y * 4 + (x + o) % 4} for o in (1, 2, 3)]
    ys = [{"head": ((y + o) % 4) * 4 + x} for o in (1, 2, 3)]
    zs = [{"seq": ((z + o) % 4) * 2 + core} for o in (1, 2, 3)]
    sibling = {"seq": z * 2 + (1 - core)}

    loads = [
        pltpu.make_async_copy(
            ref.at[:, 128 * half : 128 * half + 128], xg.at[item, half, y, x], wsem.at[item, half]
        )
        for item, ref in enumerate((x_ref, og_ref))
        for half in (0, 1)
    ]
    loads += [
        pltpu.make_async_copy(ref, wcat.at[:, 256 * n : 256 * n + 256], wsem.at[2, n])
        for n, ref in enumerate((wq_ref, wk_ref, wv_ref))
    ]
    loads += [
        pltpu.make_async_copy(src, dst, wsem.at[3, n])
        for n, (src, dst) in enumerate((
            (wo_ref, wo), (gate_ref, gate), (beta_ref, beta_in), (init_ref, start), (ds_ref, ds)
        ))
    ]
    comm[1:, 2] = jnp.zeros((3, 128, 128), BF)
    barrier = pltpu.get_barrier_semaphore()
    partners = xs + ys + zs + [sibling]
    for device in partners:
        pl.semaphore_signal(barrier, inc=1, device_id=device, device_id_type=MESH)

    for load in loads:
        load.start()
    pl.semaphore_wait(barrier, len(partners))

    sent = []

    def remote(src, dst, ssem, rsem, device):
        copy = pltpu.make_async_remote_copy(
            src_ref=src, dst_ref=dst, send_sem=ssem, recv_sem=rsem,
            device_id=device, device_id_type=MESH,
        )
        sent.append(copy)
        return copy

    def near(item, half):
        block = xg.at[item, half, y, x]
        source = (x_ref, og_ref)[item].at[:, 128 * half : 128 * half + 128]
        axis = xs if half == 0 else ys
        return [
            remote(source, block, gsend.at[item, half, o], grecv.at[item, half, o], axis[o])
            for o in (1, 0, 2)
        ]

    def piece(item, half, group, first, count):
        taken = pl.ds(first, count)
        return xg.at[item, 0, group, taken] if half == 0 else xg.at[item, 1, taken, group]

    def far(item, half):
        place, axis = (y, ys) if half == 0 else (x, xs)
        pieces = ((0, 0, 1), (2, 2, 1), (0, 1, 1), (2, 3, 1), (0, 2, 2), (2, 0, 2))
        if item == 1:
            pieces = ((0, 0, 4), (2, 0, 4), (1, 0, 4))
        copies = []
        for n, (forward, first, count) in enumerate(pieces):
            block = piece(item, half, place, first, count)
            copies.append(remote(
                block, block, gsend.at[item, half, 3 + n], grecv.at[item, half, 3 + n],
                axis[forward],
            ))
        return copies

    def hand_on(item, half):
        place, axis = (y, ys) if half == 0 else (x, xs)
        pieces = ((0, 0, 1), (2, 2, 1), (0, 1, 1), (2, 3, 1))
        copies = []
        for n, (forward, first, count) in enumerate(pieces):
            group = (place + 3) % 4 if forward == 0 else (place + 1) % 4
            block = piece(item, half, group, first, count)
            copies.append(remote(
                block, block, gsend.at[item, half, 9 + n], grecv.at[item, half, 9 + n],
                axis[forward],
            ))
        return copies

    parts = [(item, half) for item in (0, 1) for half in (0, 1)]
    nears = {part: near(*part) for part in parts}
    fars = {part: far(*part) for part in parts}
    relays = {part: hand_on(*part) for part in parts[:2]}

    def begin(item):
        for o in range(3):
            for half in (0, 1):
                nears[item, half][o].start()

    def widen(item):
        for half in (0, 1):
            for copy in nears[item, half]:
                copy.wait_recv()
        for n in range(len(fars[item, 0])):
            for half in (0, 1):
                fars[item, half][n].start()

    def pass_on(item):
        for n in range(len(relays[item, 0])):
            for half in (0, 1):
                fars[item, half][n].wait_recv()
                relays[item, half][n].start()

    def project(item, weight, taken, columns, groups):
        for half, place in ((0, y), (1, x)):
            rows = slice(128 * half, 128 * half + 128)
            for o in groups:
                group = (place + o) % 4
                if half == 0:
                    block = xg[item, 0, group].reshape(576, 128)
                    matrix = weight[pl.ds(pl.multiple_of(576 * group, 16), 576), taken]
                else:
                    block = cat([xg[item, 1, k, group] for k in range(4)])
                    matrix = cat([
                        weight[pl.ds(pl.multiple_of(576 * k + 144 * group, 16), 144), taken]
                        for k in range(4)
                    ])
                value = mm(block, matrix, 0, 0)
                if o == 0:
                    raw[rows, columns] = value
                else:
                    raw[rows, columns] += value

    begin(0)
    begin(1)
    for load in loads[:4]:
        load.wait()
    widen(0)
    for load in loads[4:]:
        load.wait()
    first_rows = (0, wcat, slice(0, 768), slice(0, 768))
    second_rows = (1, wot, slice(0, 256), slice(768, 1024))
    project(*first_rows, (0,))
    pass_on(0)
    widen(1)
    for n in range(18):
        wot[128 * n : 128 * n + 128, :] = wo[:, 128 * n : 128 * n + 128].T
    for half in (0, 1):
        for copy in fars[0, half][4:]:
            copy.wait_recv()
    project(*first_rows, (1, 3))
    project(*second_rows, (0,))
    for half in (0, 1):
        for copy in relays[0, half]:
            copy.wait_recv()
    project(0, wcat, slice(256, 768), slice(256, 768), (2,))

    def stacked(ref, c, first):
        t = slice(CHUNK * c, CHUNK * c + CHUNK)
        return cat([ref[t, first : first + 128], ref[t, first + 128 : first + 256]])

    diagonal = (
        lax.broadcasted_iota(jnp.int32, (CHUNK, CHUNK), 0)
        == lax.broadcasted_iota(jnp.int32, (CHUNK, CHUNK), 1)
    )
    betas = [
        cat([
            rowsum(jnp.where(diagonal, beta_in[h : h + 1, CHUNK * c : CHUNK * c + CHUNK], 0.0))
            for h in (0, 1)
        ])
        for c in range(CHUNKS)
    ]
    together([
        key_pass(
            c, seq * 256 + CHUNK * c, stacked(raw, c, 256), stacked(raw, c, 512),
            stacked(gate, c, 0), betas[c], ds, sf, sb, chain, passed,
        )
        for c in range(CHUNKS)
    ])

    def compose(n, m, v, h):
        step = mm3(chain[n, h, 0], cat([m, v], 1))
        return step[:, :128], step[:, 128:] + chain[n, h, 1]

    low = [compose(1, chain[0, h, 0], chain[0, h, 1], h) for h in (0, 1)]
    high = [compose(3, chain[2, h, 0], chain[2, h, 1], h) for h in (0, 1)]
    third = [compose(2, *low[h], h) for h in (0, 1)]
    for h in (0, 1):
        step = mm3(high[h][0], cat(low[h], 1))
        own[h, 0] = step[:, :128].astype(BF)
        own[h, 1] = (step[:, 128:] + high[h][1]).astype(BF)
    swap = remote(
        own.at[1 - core, pl.ds(0, 2)], heard.at[pl.ds(0, 2)], esend.at[0], erecv.at[0], sibling
    )
    swap.start()
    project(0, wcat, slice(0, 256), slice(0, 256), (2,))
    reads = together([query_pass(c, stacked(raw, c, 0), sf, sb) for c in range(CHUNKS)])
    for h, rows in enumerate(HEADS):
        for n, pair in ((0, (chain[0, h, 0], chain[0, h, 1])), (1, low[h]),
                        (2, third[h])):
            prefix[h, n, :, :128], prefix[h, n, :, 128:] = pair
        qe[h, 0:CHUNK] = reads[0][rows].astype(BF)
        for n in (1, 2, 3):
            qe[h, CHUNK * n : CHUNK * n + CHUNK] = mm(
                reads[n][rows], prefix[h, n - 1, :, :128]
            ).astype(BF)
    for half in (0, 1):
        for copy in fars[1, half][:2]:
            copy.wait_recv()
    project(*second_rows, (1, 3))
    swap.wait_recv()
    first = core == 0
    m0, b0 = [jnp.where(first, own[core, n], heard[n]) for n in (0, 1)]
    m1, b1 = [jnp.where(first, heard[n], own[core, n]) for n in (0, 1)]
    m0t, m1t = [m.astype(F32).T.astype(BF) for m in (m0, m1)]
    both = mm(m1, cat([m0, b0], 1))
    comm[z, 0] = both[:, :128].astype(BF)
    comm[z, 1] = (both[:, 128:] + b1.astype(F32)).astype(BF)
    def line(first, count, number, o):
        block = comm.at[z, pl.ds(first, count)]
        return pltpu.make_async_remote_copy(
            src_ref=block, dst_ref=block, send_sem=esend.at[number], recv_sem=erecv.at[number],
            device_id=zs[o - 1], device_id_type=MESH,
        )

    both_maps = {o: line(0, 2, o, o) for o in (1, 2, 3)}
    one_map = {o: line(0, 1, o, o) for o in (1, 2, 3)}
    back = {o: line(2, 1, 5 + o, o) for o in (1, 2, 3)}
    for o in (2, 1, 3):
        pl.when(z < 4 - o)(both_maps[o].start)
        pl.when(z >= 4 - o)(one_map[o].start)

    for half in (0, 1):
        fars[1, half][2].wait_recv()
    project(*second_rows, (2,))

    for h in (0, 1):
        dO = raw[:, 768 + 128 * h : 896 + 128 * h]
        own[h, 2] = mm(qe[h], dO, 0, 0).astype(BF)
    swap_l = remote(own.at[1 - core, 2], heard.at[2], esend.at[4], erecv.at[4], sibling)
    swap_l.start()

    bases = [mm(sb[c, PT], stacked(raw, c, 768), 0, 0) for c in range(CHUNKS)]
    swap_l.wait_recv()
    l0 = jnp.where(first, own[core, 2], heard[2])
    l1 = jnp.where(first, heard[2], own[core, 2])
    comm[z, 2] = (l0.astype(F32) + mm(m0t, l1)).astype(BF)
    for o in (2, 1, 3):
        pl.when(z >= 4 - o)(back[o].start)

    for o in (1, 2, 3):
        pl.when(z >= o)(both_maps[o].wait_recv)
        pl.when(z < o)(one_map[o].wait_recv)
    state, entering = start[core], start[core]
    for n in range(3):
        state = mm(comm[n, 0], state) + comm[n, 1].astype(F32)
        entering = jnp.where(z == n + 1, state, entering)
    after = mm(m0, entering) + b0.astype(F32)
    states[2] = jnp.where(first, after, entering).astype(BF)
    give_s = remote(states.at[2], states.at[core], esend.at[5], erecv.at[5], sibling)
    give_s.start()
    states[core] = jnp.where(first, entering, after).astype(BF)

    turned = [comm[n, 0].astype(F32).T.astype(BF) for n in range(3)]
    across = mm(turned[1], turned[2])
    eye = (iotas()[0] == iotas()[1]).astype(F32)
    none = jnp.zeros_like(eye)
    pull = cat([
        jnp.where(z == 0, eye, none),
        jnp.where(z == 1, eye, jnp.where(z == 0, turned[1].astype(F32), none)),
        jnp.where(
            z == 2, eye,
            jnp.where(z == 1, turned[2].astype(F32), jnp.where(z == 0, across, none)),
        ),
    ], 1).astype(BF)
    pull = cat([pull, mm(m1t, pull).astype(BF)])

    suffix = [[None] * 3, [None] * 3]
    for n in (3, 2, 1):
        for h, rows in enumerate(HEADS):
            step = mm(reads[n][rows], stacked(raw, n, 768)[rows], 0, 0)
            m = chain[n, h, 0].T
            if n == 3:
                suffix[h][2] = cat([m, step], 1)
            else:
                value = mm(m, suffix[h][n])
                suffix[h][n - 1] = cat([value[:, :128], value[:, 128:] + step], 1)

    y0, pulls = [], []
    for c in range(CHUNKS):
        base = bases[c]
        tk = sb[c, TK]
        if c < 3:
            value = cat([mm(tk[s], suffix[h][c]) for h, s in enumerate(HEADS)])
            base = base + value[:, 128:]
            tk = value[:, :128].astype(BF)
        y0.append(base)
        pulls.append(tk)

    for o in (1, 2, 3):
        pl.when(z < o)(back[o].wait_recv)
    last = comm[1:, 2].reshape(384, 128)
    pulled = mm(pull, last)
    leaving, before = pulled[:128], pulled[128:] + l1.astype(F32)
    grads[2] = jnp.where(first, leaving, before).astype(BF)
    give_d = remote(grads.at[2], grads.at[core], esend.at[9], erecv.at[9], sibling)
    give_d.start()
    grads[core] = jnp.where(first, before, leaving).astype(BF)
    give_s.wait_recv()
    S = []
    for h in (0, 1):
        s = states[h]
        value = mm(prefix[h, :, :, :128].reshape(384, 128), s).reshape(3, 128, 128)
        S.append([s] + [value[n] + prefix[h, n, :, 128:] for n in range(3)])
    outs = together([
        second_pass(c, [S[0][c], S[1][c]], stacked(raw, c, 768), sf, sb) for c in range(CHUNKS)
    ])
    kept = [rest for _, rest in outs]

    def keep_rows(c, first, value):
        for h, s in enumerate(HEADS):
            gcat[CHUNK * c : CHUNK * c + CHUNK, first + 128 * h : first + 128 * h + 128] = value[
                s
            ].astype(BF)

    for c, (dqr, _) in enumerate(outs):
        keep_rows(c, 0, dqr)
    give_d.wait_recv()

    D, ends = [], [grads[0], grads[1]]
    for h in (0, 1):
        d = ends[h]
        value = mm(cat([suffix[h][n][:, :128] for n in range(3)]), d).reshape(3, 128, 128)
        D.append([value[n] + suffix[h][n][:, 128:] for n in range(3)] + [d])

    def share(half, target, n):
        rows = gcat[128 * half : 128 * half + 128, :]
        if half == 0:
            first_row = 576 * target + 288 * n
            return mm(wcat[pl.ds(pl.multiple_of(first_row, 16), 288), :], rows, 1, 1)
        return cat([
            mm(wcat[pl.ds(pl.multiple_of(576 * k + 144 * target, 16), 144), :], rows, 1, 1)
            for k in (2 * n, 2 * n + 1)
        ])

    outs = together([
        third_pass(c, kept[c], y0[c], pulls[c], ends, [D[0][c], D[1][c]], sf, sb) for c in range(CHUNKS)
    ])
    for c, (dkr, dv, _) in enumerate(outs):
        keep_rows(c, 256, dkr)
        keep_rows(c, 512, dv)
    inner = (
        last[:128].astype(F32) + mm(turned[1], last[128:256]) + mm(across, last[256:])
    )
    origin[2] = (comm[0, 2].astype(F32) + mm(turned[0], inner)).astype(BF)
    tell = {
        o: pltpu.make_async_remote_copy(
            src_ref=origin.at[2], dst_ref=origin.at[3], send_sem=esend.at[10 + o],
            recv_sem=erecv.at[10 + o], device_id=zs[o - 1], device_id_type=MESH,
        )
        for o in (1, 2, 3)
    }
    for o in (1, 2, 3):
        pl.when(z == 0)(tell[o].start)

    lines = ((0, y, ys), (1, x, xs))

    def send(half, slot, count, axis, forward):
        block = part.at[half, pl.ds(slot, count)]
        copy = remote(
            block, r1.at[half, pl.ds(slot, count)], rsend.at[half, slot], rrecv.at[half, slot],
            axis[forward],
        )
        copy.start()
        return copy

    def keep(half, slot, value):
        count = value.shape[0] // 144
        part[half, slot : slot + count] = value.astype(BF).reshape(count, 144, 128)

    sums = [[None] * 10, [None] * 10]
    for n, forward in ((0, 0), (1, 2)):
        for half, place, axis in lines:
            keep(half, 2 * n, share(half, (place + 2) % 4, n))
            for slot in (2 * n, 2 * n + 1):
                sums[half][slot] = send(half, slot, 1, axis, forward)
    for n, forward in ((1, 0), (0, 2)):
        for half, place, axis in lines:
            keep(half, 4 + 2 * n, share(half, (place + forward + 1) % 4, n))
            sums[half][4 + n] = send(half, 4 + 2 * n, 2, axis, forward)
    added = {
        (half, n): share(half, (place + forward + 1) % 4, n)
        for n, forward in ((0, 0), (1, 2)) for half, place, _ in lines
    }
    for k in (0, 1):
        for n, forward in ((0, 0), (1, 2)):
            for half, place, axis in lines:
                slot = 2 * n + k
                sums[half][slot].wait_recv()
                value = added[half, n][144 * k : 144 * k + 144] + r1[half, slot].astype(F32)
                keep(half, 8 + slot, value)
                sums[half][6 + slot] = send(half, 8 + slot, 1, axis, forward)
    for c, (dg, dbeta) in enumerate(together([
        last_pass(c, outs[c][2], sf, sb, passed) for c in range(CHUNKS)
    ])):
        t = slice(CHUNK * c, CHUNK * c + CHUNK)
        for h, s in enumerate(HEADS):
            gg[t, 128 * h : 128 * h + 128] = dg[s]
            bg[h : h + 1, t] = jnp.sum(
                jnp.where(diagonal, dbeta[s], 0.0), axis=0, keepdims=True
            )
    stores = [
        pltpu.make_async_copy(gg, gg_ref, wsem.at[0, 2]),
        pltpu.make_async_copy(bg, bg_ref, wsem.at[0, 3]),
    ]
    for store in stores:
        store.start()
    for o in (1, 2, 3):
        pl.when(z == o)(tell[o].wait_recv)
    origin[core] = jnp.where(z == 0, origin[2], origin[3])
    give_o = remote(origin.at[core], origin.at[core], esend.at[10], erecv.at[10], sibling)
    give_o.start()
    finals = [[], []]
    totals = [cat([share(half, place, n) for n in (0, 1)]) for half, place, _ in lines]
    for half, place, axis in ((0, x, xs), (1, y, ys)):
        for copy in sums[half][4:]:
            copy.wait_recv()
        got = [r1[half, 4 * n : 4 * n + 4].astype(F32) for n in (1, 2)]
        total = totals[half].reshape(4, 144, 128) + got[0] + got[1]
        t2f[half] = total
        t2[half] = total.astype(BF)
        for o in (1, 0, 2):
            copy = remote(
                t2.at[half, (place + o + 1) % 4], r2.at[half, o],
                rsend.at[half, 12 + o], rrecv.at[half, 12 + o], axis[o],
            )
            copy.start()
            finals[half].append(copy)
    done = []
    for half, place in ((0, x), (1, y)):
        total = t2f[half, place]
        for copy in finals[half]:
            copy.wait_recv()
        for o in range(3):
            total = total + r2[half, o].astype(F32)
        done.append(total)
    give_o.wait_recv()
    for h in (0, 1):
        sg_ref[h] = origin[h].astype(F32)
    ig_ref[...] = cat(done, 1).astype(BF)
    for store in stores:
        store.wait()

    for o in (1, 2, 3):
        pl.when(z < 4 - o)(both_maps[o].wait_send)
        pl.when(z >= 4 - o)(one_map[o].wait_send)
        pl.when(z >= 4 - o)(back[o].wait_send)
        pl.when(z == 0)(tell[o].wait_send)
    for copy in sent:
        copy.wait_send()


def finish(*refs):
    for n in range(4):
        refs[4 + n][...] = refs[n][...]


def per_device(inputs, output_grad, *others):
    vmem = pl.BlockSpec(memory_space=pltpu.VMEM)
    anywhere = pl.BlockSpec(memory_space=pl.ANY)
    scratch = lambda *shape, dtype=F32: pltpu.VMEM(shape, dtype)
    dma = lambda *shape: pltpu.SemaphoreType.DMA(shape)
    shapes = (
        jax.ShapeDtypeStruct((144, 256), BF),
        jax.ShapeDtypeStruct((256, 256), F32),
        jax.ShapeDtypeStruct((2, 256), F32),
        jax.ShapeDtypeStruct((2, 128, 128), F32),
    )
    results = pl.pallas_call(
        kernel,
        out_shape=shapes,
        in_specs=[anywhere] * 10,
        out_specs=(vmem, anywhere, anywhere, vmem),
        scratch_shapes=[
            scratch(256, 256),
            scratch(2, 256),
            scratch(256, 256),
            scratch(2, 256),
            scratch(2, 128, 128),
            pltpu.SMEM((4,), jnp.int32),
            scratch(2304, 768, dtype=BF),
            scratch(256, 2304, dtype=BF),
            scratch(2304, 256, dtype=BF),
            scratch(2, 2, 4, 4, 144, 128, dtype=BF),
            scratch(256, 1024),
            scratch(256, 768, dtype=BF),
            scratch(CHUNKS, 10, 128, 128),
            scratch(CHUNKS, 10, 128, 128, dtype=BF),
            scratch(CHUNKS, 2, 2, 128, 128),
            scratch(CHUNKS, 8, 128),
            scratch(2, 3, 128, 256),
            scratch(2, 256, 128, dtype=BF),
            scratch(2, 3, 128, 128, dtype=BF),
            scratch(3, 128, 128, dtype=BF),
            scratch(4, 3, 128, 128, dtype=BF),
            scratch(3, 128, 128, dtype=BF),
            scratch(3, 128, 128, dtype=BF),
            scratch(4, 128, 128, dtype=BF),
            scratch(2, 12, 144, 128, dtype=BF),
            scratch(2, 12, 144, 128, dtype=BF),
            scratch(2, 4, 144, 128, dtype=BF),
            scratch(2, 4, 144, 128),
            scratch(2, 3, 144, 128, dtype=BF),
            dma(4, 5), dma(2, 2, 13), dma(2, 2, 13), dma(14), dma(14), dma(2, 15), dma(2, 15),
        ],
        compiler_params=pltpu.CompilerParams(
            collective_id=0, has_side_effects=True, vmem_limit_bytes=60 * 1024 * 1024
        ),
        cost_estimate=pl.CostEstimate(
            flops=3 * 10**9, bytes_accessed=6 * 10**6, transcendentals=3 * 10**5
        ),
    )(inputs.T, output_grad.T, *others)
    results = pl.pallas_call(
        finish,
        out_shape=shapes,
        in_specs=[vmem] * 4,
        out_specs=(vmem,) * 4,
    )(*results)
    return (results[0].T, *results[1:])


def solution(mesh):
    return jax.shard_map(
        per_device,
        mesh=mesh,
        in_specs=(
            P("seq", "head"),
            P("seq", "head"),
            P(None, "head"),
            P(None, "head"),
            P(None, "head"),
            P("head", None),
            P("seq", "head"),
            P("head", "seq"),
            P("head", None, None),
            P(),
        ),
        out_specs=(P("seq", "head"), P("seq", "head"), P("head", "seq"), P("head", None, None)),
        check_vma=False,
    )
```
